32 devices in a mesh: groups: 2 (over x), ab: 8 (over z, y), cd: 2 (over core).
Axes of the slice: x: 2, y: 2, z: 4, core: 2. Of those that a mesh axis runs over, the one named last changes fastest.
Arguments:
- amplitudes: float32 [4, 128, 4096], P('groups', 'ab', 'cd'), parts along dimension 0, may hold values from -6 to 6
- integrals: float32 [16384, 4096], P(('groups', 'ab'), 'cd'), parts along dimension 0, may hold values from -0.21875 to 0.21875
- ab_irrep: int32 [128], P(('groups', 'ab')), parts along dimension 0, may hold values from 0 to 7
- cd_irrep: int32 [64], P(('groups', 'cd')), parts along dimension 0, may hold values from 0 to 7
- block_pattern: int32 [128, 32], P(('groups', 'ab'), 'cd'), parts along dimension 0, may hold values 0 or 1
Outputs:
- residual: float32 [4, 128, 8192], P('groups', 'cd', 'ab'), parts along dimension 0
The draws below stay inside these ranges and needn't reach their ends.
There are 2 independent parts, one for each index of `groups`. The reference program is written for one: setup_inputs(seed, part) draws one part's arguments, and reference() takes and returns one part's arrays. A program takes and returns all parts, laid end to end along the dimension named above; each array names one. Nothing has to cross between parts.
All inputs are finite; a program needn't handle non-finite values. No bound on the sum of `block_pattern` on one device may be relied on, other than what follows from the above.
Results may differ from the reference program's by a relative error of at most 0.000071.
Values sent between devices are 32-bit elements; how exact they have to be, the bound alone decides.
No kernel may reach another device: no remote copies, remote signals or barrier semaphores. Data moves between devices by JAX's collectives and lax.ppermute only.
A program may use at most 128 MiB of HBM per device.

```python
import jax
import jax.numpy as jnp
from jax import lax

TILE = 128
SPANS = 2
PAIRS = 128
AB_TILES = 64
CD_TILES = 32
NAB = 8192
NCD = 4096


def with_ends(entries, stream_key, least, top_value):
    longest = entries.shape.index(max(entries.shape))
    spots = []
    for shift in (0, 1):
        where = [jax.random.randint(jax.random.fold_in(stream_key, axis), (), 0, length) for axis, length in enumerate(entries.shape)]
        where[longest] = (where[longest] + shift) % entries.shape[longest]
        spots.append(tuple(where))
    return entries.at[spots[0]].set(least).at[spots[1]].set(top_value)


def block_levels(stream_key, dims, cuts, low, largest):
    def one(axis_at, shards_of):
        heights = jax.random.uniform(jax.random.fold_in(jax.random.fold_in(stream_key, 6), axis_at), (shards_of,), jnp.float32, low / len(cuts), largest / len(cuts))
        return jnp.repeat(jnp.exp(heights), dims[axis_at] // shards_of).reshape((-1,) + (1,) * (len(dims) - axis_at - 1))

    loudness = one(*cuts[0])
    for cut in cuts[1:]:
        loudness = loudness * one(*cut)
    return loudness


def centred(key, extent, deviation, most, cuts=(), held_as=jnp.bfloat16):
    array = deviation * jax.random.normal(key, extent, jnp.float32)
    if cuts:
        array = array * block_levels(key, extent, cuts, -0.22, 0.18)
    return jnp.clip(array, -most, most).astype(held_as)


def setup_inputs(seed: int = 0, part: int = 0) -> dict:
    arg_keys = jax.random.split(jax.random.key(seed), 6)
    own_keys = jax.random.split(jax.random.fold_in(arg_keys[5], part), 6)
    return {
        "amplitudes": centred(own_keys[0], (SPANS, PAIRS, NCD), 1.0, 6.0, ((1, 8), (2, 2)), jnp.float32),
        "integrals": centred(own_keys[1], (NAB, NCD), (TILE * 6) ** -0.5, 0.21875, ((0, 8), (1, 2)), jnp.float32),
        "ab_irrep": with_ends(jax.random.randint(own_keys[2], (AB_TILES,), 0, 8), jax.random.fold_in(own_keys[2], 1), 0, 7).astype(jnp.int32),
        "cd_irrep": with_ends(jax.random.randint(own_keys[3], (CD_TILES,), 0, 8), jax.random.fold_in(own_keys[3], 1), 0, 7).astype(jnp.int32),
        "block_pattern": with_ends((jax.random.randint(own_keys[4], (AB_TILES, CD_TILES), 0, 4) < 3).astype(jnp.int32), jax.random.fold_in(own_keys[4], 1), 0, 1),
    }


def reference(amplitudes, integrals, ab_irrep, cd_irrep, block_pattern):
    allowed = ((block_pattern == 1) & (ab_irrep[:, None] == cd_irrep[None, :])).astype(jnp.float32)
    amplitude_rows = amplitudes.reshape(SPANS * PAIRS, NCD)
    tile_stack = integrals.reshape(AB_TILES, TILE, NCD)

    def tile_block(pieces):
        tile_rows, tile_mask = pieces
        widened = jnp.repeat(tile_mask, TILE)
        return jnp.dot(amplitude_rows, (tile_rows * widened[None, :]).T, precision=lax.Precision.HIGHEST, preferred_element_type=jnp.float32)

    stacked = lax.map(tile_block, (tile_stack, allowed))
    return jnp.transpose(stacked, (1, 0, 2)).reshape(SPANS, PAIRS, NAB)
```

```python
import functools

import jax
import jax.numpy as jnp
import numpy as np
from jax import lax
from jax.experimental import pallas as pl
from jax.experimental.pallas import tpu as pltpu
from jax.sharding import PartitionSpec as P

TILE = 128
SLOTS = 16
VMEM_LIMIT = 48 * 2**20


def ring_order(count):
    bits = count.bit_length() - 1
    if count != 1 << bits or bits < 2:
        return list(range(count))
    rows = 1 << ((bits + 1) // 2)
    columns = count // rows
    order = [row * columns for row in range(rows)]
    for at, row in enumerate(reversed(range(rows))):
        across = range(1, columns) if at % 2 == 0 else range(columns - 1, 0, -1)
        order += [row * columns + column for column in across]
    return order


def pick_kernel(ab_tiles, cd_tiles, pattern, ab_irrep, cd_irrep, integrals, listed, high, low, landed, sems):
    def row(p, count):
        label = ab_irrep[p]

        def column(q, count):
            listed[1 + count] = p * cd_tiles + q
            keep = jnp.logical_and(pattern[p, q] == 1, label == cd_irrep[q])
            return count + keep.astype(jnp.int32)

        return lax.fori_loop(0, cd_tiles, column, count, unroll=True)

    count = lax.fori_loop(0, ab_tiles, row, jnp.int32(0))
    listed[0] = count

    def fetch(k):
        tile = listed[1 + k]
        p = tile // cd_tiles
        q = tile - p * cd_tiles
        slot = k % SLOTS
        return pltpu.make_async_copy(
            integrals.at[pl.ds(pl.multiple_of(p * TILE, TILE), TILE), pl.ds(pl.multiple_of(q * TILE, TILE), TILE)],
            landed.at[slot],
            sems.at[slot],
        )

    def begin(k, carry):
        fetch(k).start()
        return carry

    lax.fori_loop(0, jnp.minimum(count, SLOTS), begin, 0)

    def split(k, carry):
        fetch(k).wait()
        tile = landed[k % SLOTS].T
        upper = tile.astype(jnp.bfloat16)
        high[k] = upper
        low[k] = (tile - upper.astype(jnp.float32)).astype(jnp.bfloat16)

        @pl.when(k + SLOTS < count)
        def _():
            fetch(k + SLOTS).start()

        return carry

    lax.fori_loop(0, count, split, 0)


def contract_kernel(spans, rows, half, cd_tiles, listed, places, high, low, *refs):
    pieces, (mine, send, total) = refs[:-3], refs[-3:]
    total[...] = jnp.zeros_like(total)

    def step(k, carry):
        tile = listed[1 + k]
        p = tile // cd_tiles
        q = tile - p * cd_tiles
        columns = pl.ds(pl.multiple_of(q * TILE, TILE), TILE)
        left = jnp.concatenate([piece[0, :, columns] for piece in pieces], axis=0)
        upper = left.astype(jnp.bfloat16)
        lower = (left - upper.astype(jnp.float32)).astype(jnp.bfloat16)
        dot = functools.partial(jnp.dot, preferred_element_type=jnp.float32)
        into = pl.ds(pl.multiple_of(p * TILE, TILE), TILE)
        total[:, into] += dot(upper, high[k]) + (dot(lower, high[k]) + dot(upper, low[k]))
        return carry

    lax.fori_loop(0, listed[0], step, 0)

    for at in range(len(pieces)):
        span = at % spans
        place = places[at // spans]
        block = total[at * rows : (at + 1) * rows, :]

        @pl.when(place < half)
        def _():
            mine[span, pl.ds(pl.multiple_of(place, rows), rows), :] = block

        @pl.when(place >= half)
        def _():
            send[span, pl.ds(pl.multiple_of(place - half, rows), rows), :] = block


def solution(mesh):
    count = mesh.shape["ab"]
    order = ring_order(count)
    ahead = [(order[at], order[(at + 1) % count]) for at in range(count)]
    back = [(to, start) for start, to in ahead]
    offsets = list(range(-(count // 2), (count + 1) // 2))
    place_of = {device: at for at, device in enumerate(order)}
    owners = np.array([[order[(place_of[d] + o) % count] for o in offsets] for d in range(count)], np.int32)

    def shards(amplitudes, integrals, ab_irrep, cd_irrep, block_pattern):
        spans, rows, depth = amplitudes.shape
        slab = integrals.shape[0]
        ab_tiles, cd_tiles = block_pattern.shape
        tiles = ab_tiles * cd_tiles
        half = rows * count // 2

        listed, high, low = pl.pallas_call(
            functools.partial(pick_kernel, ab_tiles, cd_tiles),
            out_shape=(
                jax.ShapeDtypeStruct((tiles + 2,), jnp.int32),
                jax.ShapeDtypeStruct((tiles, TILE, TILE), jnp.bfloat16),
                jax.ShapeDtypeStruct((tiles, TILE, TILE), jnp.bfloat16),
            ),
            in_specs=[pl.BlockSpec(memory_space=pltpu.SMEM)] * 3 + [pl.BlockSpec(memory_space=pl.ANY)],
            out_specs=(
                pl.BlockSpec(memory_space=pltpu.SMEM),
                pl.BlockSpec(memory_space=pltpu.VMEM),
                pl.BlockSpec(memory_space=pltpu.VMEM),
            ),
            scratch_shapes=[pltpu.VMEM((SLOTS, TILE, TILE), jnp.float32), pltpu.SemaphoreType.DMA((SLOTS,))],
            compiler_params=pltpu.CompilerParams(vmem_limit_bytes=VMEM_LIMIT),
            cost_estimate=pl.CostEstimate(flops=0, bytes_accessed=8 << 20, transcendentals=0),
            name="pick",
        )(block_pattern, ab_irrep, cd_irrep, integrals)

        held = {}
        for span in range(spans):
            own = amplitudes[span : span + 1]
            held[span, 0] = own
            long_way = ahead if span % 2 == 0 else back
            for pairs, sign in ((ahead, -1), (back, 1)):
                hops = count // 2 if pairs is long_way else (count - 1) // 2
                piece = own
                for hop in range(1, hops + 1):
                    piece = lax.ppermute(piece, "ab", pairs)
                    at = sign * hop
                    held[span, -(count // 2) if abs(at) == count // 2 and count % 2 == 0 else at] = piece
        pieces = [held[span, offset] for offset in offsets for span in range(spans)]

        owner = jnp.asarray(owners)[lax.axis_index("ab")]
        core = lax.axis_index("cd")
        start = owner * rows
        places = jnp.where(core == 0, start, (start + half) % (2 * half))

        block = jax.ShapeDtypeStruct((spans, half, slab), jnp.float32)
        mine, send = pl.pallas_call(
            functools.partial(contract_kernel, spans, rows, half, cd_tiles),
            out_shape=(block, block),
            in_specs=[pl.BlockSpec(memory_space=pltpu.SMEM)] * 2
            + [pl.BlockSpec(memory_space=pltpu.VMEM)] * (2 + len(pieces)),
            out_specs=(pl.BlockSpec(memory_space=pltpu.VMEM),) * 2,
            scratch_shapes=[pltpu.VMEM((len(pieces) * rows, slab), jnp.float32)],
            compiler_params=pltpu.CompilerParams(vmem_limit_bytes=VMEM_LIMIT),
            name="contract",
        )(listed, places, high, low, *pieces)
        return mine + lax.ppermute(send, "cd", [(0, 1), (1, 0)])

    in_specs = (
        P("groups", "ab", "cd"),
        P(("groups", "ab"), "cd"),
        P(("groups", "ab")),
        P(("groups", "cd")),
        P(("groups", "ab"), "cd"),
    )
    out_specs = P("groups", "cd", "ab")
    return jax.shard_map(shards, mesh=mesh, in_specs=in_specs, out_specs=out_specs, check_vma=False)
```

```python
import functools

import jax
import jax.numpy as jnp
from jax import lax
from jax.experimental import pallas as pl
from jax.experimental.pallas import tpu as pltpu
from jax.sharding import PartitionSpec as P

TILE = 128
UNROLL = 4
FLIGHT = 32
VMEM_LIMIT = 12 * 2**20


def grid_of(count):
    bits = count.bit_length() - 1
    if count != 1 << bits or bits < 2:
        return count, 1
    rows = 1 << ((bits + 1) // 2)
    return rows, count // rows


def at_ring(place, rows, columns):
    if columns == 1:
        return place
    wide = columns - 1
    beyond = place - rows
    line = beyond // wide
    step = beyond - line * wide
    even = (line % 2) == 0
    if isinstance(place, int):
        back = (rows - 1 - line) * columns + (1 + step if even else columns - 1 - step)
        return place * columns if place < rows else back
    back = (rows - 1 - line) * columns + jnp.where(even, 1 + step, columns - 1 - step)
    return jnp.where(place < rows, place * columns, back)


def ring_of(index, rows, columns):
    if columns == 1:
        return index
    wide = columns - 1
    row = index // columns
    column = index - row * columns
    line = rows - 1 - row
    step = jnp.where((line % 2) == 0, column - 1, columns - 1 - column)
    return jnp.where(column == 0, row, rows + line * wide + step)


def pick_kernel(count, offsets, rows, ab_tiles, cd_tiles, pattern, ab_irrep, cd_irrep, integrals, listed, split, landed, sems):
    def row(p, found):
        label = ab_irrep[p]
        for q in range(cd_tiles):
            listed[1 + found] = p * cd_tiles + q
            keep = jnp.logical_and(pattern[p, q] == 1, label == cd_irrep[q])
            found = found + keep.astype(jnp.int32)
        return found

    found = lax.fori_loop(0, ab_tiles, row, jnp.int32(0))
    listed[0] = found

    def fetch(k):
        tile = listed[1 + k]
        p = tile // cd_tiles
        q = tile - p * cd_tiles
        slot = k % FLIGHT
        return pltpu.make_async_copy(
            integrals.at[pl.ds(pl.multiple_of(p * TILE, TILE), TILE), pl.ds(pl.multiple_of(q * TILE, TILE), TILE)],
            landed.at[slot],
            sems.at[slot],
        )

    def begin(k, carry):
        fetch(k).start()
        return carry

    lax.fori_loop(0, jnp.minimum(found, FLIGHT), begin, 0)

    for extra in range(UNROLL):
        listed[1 + found + extra] = 0
        split[found + extra] = jnp.zeros((TILE, 2 * TILE), jnp.bfloat16)
    grid = grid_of(count)
    here = ring_of(lax.axis_index("ab"), *grid)
    first = 1 + ab_tiles * cd_tiles + UNROLL
    half = rows * count // 2
    turn = lax.axis_index("cd") * half
    for at, offset in enumerate(offsets):
        start = at_ring((here + offset + count) % count, *grid) * rows + turn
        listed[first + at] = jnp.where(start >= 2 * half, start - 2 * half, start)

    def part(k, carry):
        fetch(k).wait()
        tile = landed[k % FLIGHT].T
        upper = tile.astype(jnp.bfloat16)
        split[k, :, :TILE] = upper
        split[k, :, TILE:] = (tile - upper.astype(jnp.float32)).astype(jnp.bfloat16)

        @pl.when(k + FLIGHT < found)
        def _():
            fetch(k + FLIGHT).start()

        return carry

    lax.fori_loop(0, found, part, 0)


def products(cd_tiles, listed, split, pieces, total):
    total[...] = jnp.zeros_like(total)

    def step(round_at, carry):
        for unrolled in range(UNROLL):
            k = round_at * UNROLL + unrolled
            tile = listed[1 + k]
            p = tile // cd_tiles
            q = tile - p * cd_tiles
            columns = pl.ds(pl.multiple_of(q * TILE, TILE), TILE)
            left = jnp.concatenate([piece[0, :, columns] for piece in pieces], axis=0)
            upper = left.astype(jnp.bfloat16)
            lower = (left - upper.astype(jnp.float32)).astype(jnp.bfloat16)
            both = jnp.dot(jnp.concatenate([upper, lower], axis=0), split[k], preferred_element_type=jnp.float32)
            high, low = both[: left.shape[0]], both[left.shape[0] :]
            into = pl.ds(pl.multiple_of(p * TILE, TILE), TILE)
            total[:, into] += high[:, :TILE] + (high[:, TILE:] + (low[:, :TILE] + low[:, TILE:]))
        return carry

    lax.fori_loop(0, (listed[0] + UNROLL - 1) // UNROLL, step, 0)


def step_kernel(spans, rows, half, cd_tiles, chunks, listed, split, *refs):
    pieces = refs[: len(chunks) * spans]
    mine, send, total = refs[-3:]
    products(cd_tiles, listed, split, pieces, total)
    for at, chunk in enumerate(chunks):
        place = listed[chunk]
        for span in range(spans):
            from_row = (at * spans + span) * rows
            block = total[from_row : from_row + rows, :]

            @pl.when(place < half)
            def _():
                mine[span, pl.ds(pl.multiple_of(place, rows), rows), :] = block

            @pl.when(place >= half)
            def _():
                send[span, pl.ds(pl.multiple_of(place - half, rows), rows), :] = block


def last_kernel(cd_tiles, listed, split, *refs):
    products(cd_tiles, listed, split, refs[:-1], refs[-1])


def solution(mesh):
    count = mesh.shape["ab"]
    grid = grid_of(count)
    ahead = [(at_ring(at, *grid), at_ring((at + 1) % count, *grid)) for at in range(count)]
    back = [(to, start) for start, to in ahead]
    far = count // 2
    steps = [[0]] + [[-hop, hop] for hop in range(1, far)] + [[-far]]
    offsets = [offset for step in steps for offset in step]

    def shards(amplitudes, integrals, ab_irrep, cd_irrep, block_pattern):
        spans, rows, depth = amplitudes.shape
        slab = integrals.shape[0]
        ab_tiles, cd_tiles = block_pattern.shape
        tiles = ab_tiles * cd_tiles
        half = rows * far
        first = 1 + tiles + UNROLL

        in_hbm = functools.partial(pltpu.with_memory_space_constraint, memory_space=pltpu.HBM)
        smem = pl.BlockSpec(memory_space=pltpu.SMEM)
        vmem = pl.BlockSpec(memory_space=pltpu.VMEM)
        params = pltpu.CompilerParams(vmem_limit_bytes=VMEM_LIMIT)

        listed, split = pl.pallas_call(
            functools.partial(pick_kernel, count, offsets, rows, ab_tiles, cd_tiles),
            out_shape=(
                jax.ShapeDtypeStruct((first + len(offsets),), jnp.int32),
                pltpu.VMEM((tiles + UNROLL, TILE, 2 * TILE), jnp.bfloat16),
            ),
            in_specs=[smem, smem, smem, pl.BlockSpec(memory_space=pltpu.HBM)],
            out_specs=(smem, vmem),
            scratch_shapes=[pltpu.VMEM((FLIGHT, TILE, TILE), jnp.float32), pltpu.SemaphoreType.DMA((FLIGHT,))],
            compiler_params=params,
            cost_estimate=pl.CostEstimate(flops=0, bytes_accessed=8 << 20, transcendentals=0),
            name="pick",
        )(in_hbm(block_pattern), in_hbm(ab_irrep), in_hbm(cd_irrep), in_hbm(integrals))

        held = {}
        for span in range(spans):
            own = amplitudes[span : span + 1]
            held[span, 0] = own
            for pairs, sign in ((ahead, -1), (back, 1)):
                piece = own
                for hop in range(1, far + 1 if (sign < 0) == (span % 2 == 0) else far):
                    piece = lax.ppermute(piece, "ab", pairs)
                    held[span, -far if hop == far else sign * hop] = piece

        block = pltpu.VMEM((spans, half, slab), jnp.float32)
        parts = ()
        for group in [steps[0] + steps[1]] + steps[2:-1]:
            pieces = [held[span, offset] for offset in group for span in range(spans)]
            chunks = [first + offsets.index(offset) for offset in group]
            parts = pl.pallas_call(
                functools.partial(step_kernel, spans, rows, half, cd_tiles, chunks),
                out_shape=(block, block),
                in_specs=[smem] + [vmem] * (1 + len(pieces) + len(parts)),
                out_specs=(vmem, vmem),
                scratch_shapes=[pltpu.VMEM((len(pieces) * rows, slab), jnp.float32)],
                compiler_params=params,
                input_output_aliases={2 + len(pieces): 0, 3 + len(pieces): 1} if parts else {},
                cost_estimate=pl.CostEstimate(flops=1 << 30, bytes_accessed=4 << 20, transcendentals=0),
                name="step",
            )(listed, split, *pieces, *parts)
        mine, send = parts
        swap = [(0, 1), (1, 0)]
        base = mine + lax.ppermute(send, "cd", swap)

        pieces = [held[span, -far] for span in range(spans)]
        last = pl.pallas_call(
            functools.partial(last_kernel, cd_tiles),
            out_shape=pltpu.VMEM((spans * rows, slab), jnp.float32),
            in_specs=[smem] + [vmem] * (1 + len(pieces)),
            out_specs=vmem,
            compiler_params=params,
            cost_estimate=pl.CostEstimate(flops=1 << 34, bytes_accessed=4 << 20, transcendentals=0),
            name="last",
        )(listed, split, *pieces)
        last = last + lax.ppermute(last, "cd", swap)
        place = listed[first + len(offsets) - 1] // rows
        here = (jnp.arange(far, dtype=jnp.int32) == place)[None, :, None, None]
        out = jnp.where(here, last.reshape(spans, 1, rows, slab), base.reshape(spans, far, rows, slab))
        return out.reshape(spans, half, slab)

    in_specs = (
        P("groups", "ab", "cd"),
        P(("groups", "ab"), "cd"),
        P(("groups", "ab")),
        P(("groups", "cd")),
        P(("groups", "ab"), "cd"),
    )
    out_specs = P("groups", "cd", "ab")
    return jax.shard_map(shards, mesh=mesh, in_specs=in_specs, out_specs=out_specs, check_vma=False)
```

```python
import functools

import jax
import jax.numpy as jnp
from jax import lax
from jax.experimental import pallas as pl
from jax.experimental.pallas import tpu as pltpu
from jax.sharding import PartitionSpec as P

TILE = 128
UNROLL = 4
FLIGHT = 32
VMEM_LIMIT = 12 * 2**20


def grid_of(count):
    bits = count.bit_length() - 1
    if count != 1 << bits or bits < 2:
        return count, 1
    rows = 1 << ((bits + 1) // 2)
    return rows, count // rows


def at_ring(place, rows, columns):
    if columns == 1:
        return place
    wide = columns - 1
    beyond = place - rows
    line = beyond // wide
    step = beyond - line * wide
    even = (line % 2) == 0
    if isinstance(place, int):
        back = (rows - 1 - line) * columns + (1 + step if even else columns - 1 - step)
        return place * columns if place < rows else back
    back = (rows - 1 - line) * columns + jnp.where(even, 1 + step, columns - 1 - step)
    return jnp.where(place < rows, place * columns, back)


def ring_of(index, rows, columns):
    if columns == 1:
        return index
    wide = columns - 1
    row = index // columns
    column = index - row * columns
    line = rows - 1 - row
    step = jnp.where((line % 2) == 0, column - 1, columns - 1 - column)
    return jnp.where(column == 0, row, rows + line * wide + step)


def places(count, rows, chunks):
    grid = grid_of(count)
    here = ring_of(lax.axis_index("ab"), *grid)
    core = lax.axis_index("cd")
    whole = rows * count
    found = []
    for chain, hop in chunks:
        away = (2 * core - 1) * hop if chain == 0 else (1 - 2 * core) * hop
        start = at_ring((here + away + count) % count, *grid) * rows + core * (whole // 2)
        found.append(jnp.where(start >= whole, start - whole, start))
    return found


def pick_kernel(ab_tiles, cd_tiles, pattern, ab_irrep, cd_irrep, integrals, amplitudes, listed, split, own, landed, sems, own_sem):
    copy = pltpu.make_async_copy(amplitudes, own, own_sem)
    copy.start()

    def fetch(k):
        tile = listed[1 + k]
        p = tile // cd_tiles
        q = tile - p * cd_tiles
        slot = k % FLIGHT
        return pltpu.make_async_copy(
            integrals.at[pl.ds(pl.multiple_of(p * TILE, TILE), TILE), pl.ds(pl.multiple_of(q * TILE, TILE), TILE)],
            landed.at[slot],
            sems.at[slot],
        )

    def begin(k, carry):
        fetch(k).start()
        return carry

    def row(p, found):
        label = ab_irrep[p]
        before = found
        for q in range(cd_tiles):
            listed[1 + found] = p * cd_tiles + q
            keep = jnp.logical_and(pattern[p, q] == 1, label == cd_irrep[q])
            found = found + keep.astype(jnp.int32)
        lax.fori_loop(jnp.minimum(before, FLIGHT), jnp.minimum(found, FLIGHT), begin, 0)
        return found

    found = lax.fori_loop(0, ab_tiles, row, jnp.int32(0))
    listed[0] = found
    for extra in range(UNROLL):
        listed[1 + found + extra] = 0
        split[found + extra] = jnp.zeros((TILE, 2 * TILE), jnp.bfloat16)

    def part(k, carry):
        fetch(k).wait()
        tile = landed[k % FLIGHT].T
        upper = tile.astype(jnp.bfloat16)
        split[k, :, :TILE] = upper
        split[k, :, TILE:] = (tile - upper.astype(jnp.float32)).astype(jnp.bfloat16)

        @pl.when(k + FLIGHT < found)
        def _():
            fetch(k + FLIGHT).start()

        return carry

    lax.fori_loop(0, found, part, 0)
    copy.wait()


def products(cd_tiles, listed, split, pieces, total):
    total[...] = jnp.zeros_like(total)

    def step(round_at, carry):
        for unrolled in range(UNROLL):
            k = round_at * UNROLL + unrolled
            tile = listed[1 + k]
            p = tile // cd_tiles
            q = tile - p * cd_tiles
            columns = pl.ds(pl.multiple_of(q * TILE, TILE), TILE)
            left = jnp.concatenate([piece[span, :, columns] for piece in pieces for span in range(piece.shape[0])], axis=0)
            upper = left.astype(jnp.bfloat16)
            lower = (left - upper.astype(jnp.float32)).astype(jnp.bfloat16)
            both = jnp.dot(jnp.concatenate([upper, lower], axis=0), split[k], preferred_element_type=jnp.float32)
            high, low = both[: left.shape[0]], both[left.shape[0] :]
            into = pl.ds(pl.multiple_of(p * TILE, TILE), TILE)
            total[:, into] += high[:, :TILE] + (high[:, TILE:] + (low[:, :TILE] + low[:, TILE:]))
        return carry

    lax.fori_loop(0, (listed[0] + UNROLL - 1) // UNROLL, step, 0)


def step_kernel(count, spans, rows, cd_tiles, chunks, listed, split, *refs):
    pieces = refs[: len(chunks)]
    mine, send, total = refs[-3:]
    products(cd_tiles, listed, split, pieces, total)
    half = rows * count // 2
    for at, place in enumerate(places(count, rows, chunks)):
        for span in range(spans):
            from_row = (at * spans + span) * rows
            block = total[from_row : from_row + rows, :]

            @pl.when(place < half)
            def _():
                mine[span, pl.ds(pl.multiple_of(place, rows), rows), :] = block

            @pl.when(place >= half)
            def _():
                send[span, pl.ds(pl.multiple_of(place - half, rows), rows), :] = block


def last_kernel(cd_tiles, listed, split, piece, total):
    products(cd_tiles, listed, split, [piece], total)


def merge_kernel(mine, received, out):
    out[...] = mine[...] + received[...]


def final_kernel(count, spans, rows, last, received, before, out, total, sems):
    del before
    (place,) = places(count, rows, [(0, count // 2)])

    @pl.when(place < rows * count // 2)
    def _():
        total[...] = last[...] + received[...]
        copies = []
        for span in range(spans):
            copies.append(
                pltpu.make_async_copy(
                    total.at[pl.ds(span * rows, rows), :],
                    out.at[span, pl.ds(pl.multiple_of(place, rows), rows), :],
                    sems.at[span],
                )
            )
            copies[-1].start()
        for copy in copies:
            copy.wait()


def solution(mesh):
    count = mesh.shape["ab"]
    cores = mesh.shape["cd"]
    grid = grid_of(count)
    far = count // 2
    around = []
    for chain in range(2):
        pairs = []
        for at in range(count):
            for core in range(cores):
                to = at + 1 if core == chain else at + count - 1
                pairs.append((at_ring(at, *grid) * cores + core, at_ring(to % count, *grid) * cores + core))
        around.append(pairs)
    swap = [(0, 1), (1, 0)]

    def shards(amplitudes, integrals, ab_irrep, cd_irrep, block_pattern):
        spans, rows, depth = amplitudes.shape
        slab = integrals.shape[0]
        ab_tiles, cd_tiles = block_pattern.shape
        tiles = ab_tiles * cd_tiles
        half = rows * far

        in_hbm = functools.partial(pltpu.with_memory_space_constraint, memory_space=pltpu.HBM)
        smem = pl.BlockSpec(memory_space=pltpu.SMEM)
        vmem = pl.BlockSpec(memory_space=pltpu.VMEM)
        hbm = pl.BlockSpec(memory_space=pltpu.HBM)
        params = pltpu.CompilerParams(vmem_limit_bytes=VMEM_LIMIT)

        listed, split, own = pl.pallas_call(
            functools.partial(pick_kernel, ab_tiles, cd_tiles),
            out_shape=(
                jax.ShapeDtypeStruct((1 + tiles + UNROLL,), jnp.int32),
                pltpu.VMEM((tiles + UNROLL, TILE, 2 * TILE), jnp.bfloat16),
                pltpu.VMEM(amplitudes.shape, jnp.float32),
            ),
            in_specs=[smem, smem, smem, hbm, hbm],
            out_specs=(smem, vmem, vmem),
            scratch_shapes=[
                pltpu.VMEM((FLIGHT, TILE, TILE), jnp.float32),
                pltpu.SemaphoreType.DMA((FLIGHT,)),
                pltpu.SemaphoreType.DMA,
            ],
            compiler_params=params,
            cost_estimate=pl.CostEstimate(flops=0, bytes_accessed=8 << 20, transcendentals=0),
            name="pick",
        )(in_hbm(block_pattern), in_hbm(ab_irrep), in_hbm(cd_irrep), in_hbm(integrals), in_hbm(amplitudes))

        held = {(0, 0): own}
        for chain, piece, hops in ((0, amplitudes, far), (1, own, far - 1)):
            for hop in range(1, hops + 1):
                piece = lax.ppermute(piece, ("ab", "cd"), around[chain])
                held[chain, hop] = piece

        block = pltpu.VMEM((spans, half, slab), jnp.float32)
        parts = ()
        for group in [[(0, 0), (0, 1)]] + [[(1, hop - 1), (0, hop)] for hop in range(2, far)] + [[(1, far - 1)]]:
            pieces = [held[chunk] for chunk in group]
            parts = pl.pallas_call(
                functools.partial(step_kernel, count, spans, rows, cd_tiles, group),
                out_shape=(block, block),
                in_specs=[smem] + [vmem] * (1 + len(pieces) + len(parts)),
                out_specs=(vmem, vmem),
                scratch_shapes=[pltpu.VMEM((len(pieces) * spans * rows, slab), jnp.float32)],
                compiler_params=params,
                input_output_aliases={2 + len(pieces): 0, 3 + len(pieces): 1} if parts else {},
                cost_estimate=pl.CostEstimate(flops=1 << 30, bytes_accessed=4 << 20, transcendentals=0),
                name="step",
            )(listed, split, *pieces, *parts)
        mine, send = parts
        base = pl.pallas_call(
            merge_kernel,
            out_shape=pltpu.HBM((spans, half, slab), jnp.float32),
            in_specs=[vmem, vmem],
            out_specs=vmem,
            compiler_params=params,
            name="merge",
        )(mine, lax.ppermute(send, "cd", swap))

        last = pl.pallas_call(
            functools.partial(last_kernel, cd_tiles),
            out_shape=pltpu.VMEM((spans * rows, slab), jnp.float32),
            in_specs=[smem, vmem, vmem],
            out_specs=vmem,
            compiler_params=params,
            cost_estimate=pl.CostEstimate(flops=1 << 34, bytes_accessed=4 << 20, transcendentals=0),
            name="last",
        )(listed, split, held[0, far])
        return pl.pallas_call(
            functools.partial(final_kernel, count, spans, rows),
            out_shape=pltpu.HBM((spans, half, slab), jnp.float32),
            in_specs=[vmem, vmem, hbm],
            out_specs=hbm,
            scratch_shapes=[pltpu.VMEM((spans * rows, slab), jnp.float32), pltpu.SemaphoreType.DMA((spans,))],
            compiler_params=params,
            input_output_aliases={2: 0},
            name="final",
        )(last, lax.ppermute(last, "cd", swap), base)

    in_specs = (
        P("groups", "ab", "cd"),
        P(("groups", "ab"), "cd"),
        P(("groups", "ab")),
        P(("groups", "cd")),
        P(("groups", "ab"), "cd"),
    )
    out_specs = P("groups", "cd", "ab")
    return jax.shard_map(shards, mesh=mesh, in_specs=in_specs, out_specs=out_specs, check_vma=False)
```

```python
import functools

import jax
import jax.numpy as jnp
from jax import lax
from jax.experimental import pallas as pl
from jax.experimental.pallas import tpu as pltpu
from jax.sharding import PartitionSpec as P

TILE = 128
UNROLL = 4
FLIGHT = 32
GROUP = 4
VMEM_LIMIT = 12 * 2**20


def grid_of(count):
    bits = count.bit_length() - 1
    if count != 1 << bits or bits < 2:
        return count, 1
    rows = 1 << ((bits + 1) // 2)
    return rows, count // rows


def at_ring(place, rows, columns):
    if columns == 1:
        return place
    wide = columns - 1
    beyond = place - rows
    line = beyond // wide
    step = beyond - line * wide
    even = (line % 2) == 0
    if isinstance(place, int):
        back = (rows - 1 - line) * columns + (1 + step if even else columns - 1 - step)
        return place * columns if place < rows else back
    back = (rows - 1 - line) * columns + jnp.where(even, 1 + step, columns - 1 - step)
    return jnp.where(place < rows, place * columns, back)


def ring_of(index, rows, columns):
    if columns == 1:
        return index
    wide = columns - 1
    row = index // columns
    column = index - row * columns
    line = rows - 1 - row
    step = jnp.where((line % 2) == 0, column - 1, columns - 1 - column)
    return jnp.where(column == 0, row, rows + line * wide + step)


def places(count, rows, chunks):
    grid = grid_of(count)
    here = ring_of(lax.axis_index("ab"), *grid)
    core = lax.axis_index("cd")
    whole = rows * count
    found = []
    for chain, hop in chunks:
        away = (2 * core - 1) * hop if chain == 0 else (1 - 2 * core) * hop
        start = at_ring((here + away + count) % count, *grid) * rows + core * (whole // 2)
        found.append(jnp.where(start >= whole, start - whole, start))
    return found


def pick_kernel(ab_tiles, cd_tiles, pattern, ab_irrep, cd_irrep, integrals, amplitudes, listed, split, own, landed, sems, own_sem):
    copy = pltpu.make_async_copy(amplitudes, own, own_sem)
    copy.start()

    def fetch(k):
        tile = listed[1 + k]
        p = tile // cd_tiles
        q = tile - p * cd_tiles
        slot = k % FLIGHT
        return pltpu.make_async_copy(
            integrals.at[pl.ds(pl.multiple_of(p * TILE, TILE), TILE), pl.ds(pl.multiple_of(q * TILE, TILE), TILE)],
            landed.at[slot],
            sems.at[slot],
        )

    def begin(k, carry):
        fetch(k).start()
        return carry

    def row(p, found):
        label = ab_irrep[p]
        before = found
        for q in range(cd_tiles):
            listed[1 + found] = p * cd_tiles + q
            keep = jnp.logical_and(pattern[p, q] == 1, label == cd_irrep[q])
            found = found + keep.astype(jnp.int32)
        lax.fori_loop(jnp.minimum(before, FLIGHT), jnp.minimum(found, FLIGHT), begin, 0)
        return found

    found = lax.fori_loop(0, ab_tiles, row, jnp.int32(0))
    listed[0] = found
    for extra in range(UNROLL):
        listed[1 + found + extra] = 0
        split[found + extra] = jnp.zeros((2 * TILE, TILE), jnp.bfloat16)

    def part(k, carry):
        fetch(k).wait()
        tile = landed[k % FLIGHT]
        upper = tile.astype(jnp.bfloat16)
        split[k, :TILE] = upper
        split[k, TILE:] = (tile - upper.astype(jnp.float32)).astype(jnp.bfloat16)

        @pl.when(k + FLIGHT < found)
        def _():
            fetch(k + FLIGHT).start()

        return carry

    lax.fori_loop(0, found, part, 0)
    copy.wait()


def products(cd_tiles, listed, split, pieces, total):
    total[...] = jnp.zeros_like(total)

    def step(round_at, carry):
        sums = []
        for unrolled in range(UNROLL):
            k = round_at * UNROLL + unrolled
            tile = listed[1 + k]
            p = tile // cd_tiles
            q = tile - p * cd_tiles
            columns = pl.ds(pl.multiple_of(q * TILE, TILE), TILE)
            left = jnp.concatenate([piece[span, :, columns] for piece in pieces for span in range(piece.shape[0])], axis=0)
            upper = left.astype(jnp.bfloat16)
            lower = (left - upper.astype(jnp.float32)).astype(jnp.bfloat16)
            both = lax.dot_general(
                jnp.concatenate([upper, lower], axis=0),
                split[k],
                (((1,), (1,)), ((), ())),
                preferred_element_type=jnp.float32,
            )
            high, low = both[: left.shape[0]], both[left.shape[0] :]
            sums.append((p, high[:, :TILE] + (high[:, TILE:] + (low[:, :TILE] + low[:, TILE:]))))
        for p, term in sums:
            total[:, pl.ds(pl.multiple_of(p * TILE, TILE), TILE)] += term
        return carry

    lax.fori_loop(0, (listed[0] + UNROLL - 1) // UNROLL, step, 0)


def step_kernel(count, spans, rows, cd_tiles, chunks, listed, split, *refs):
    pieces = refs[: len(chunks)]
    mine, send, total = refs[-3:]
    products(cd_tiles, listed, split, pieces, total)
    half = rows * count // 2
    for at, place in enumerate(places(count, rows, chunks)):
        for span in range(spans):
            from_row = (at * spans + span) * rows
            block = total[from_row : from_row + rows, :]

            @pl.when(place < half)
            def _():
                mine[span, pl.ds(pl.multiple_of(place, rows), rows), :] = block

            @pl.when(place >= half)
            def _():
                send[span, pl.ds(pl.multiple_of(place - half, rows), rows), :] = block


def last_kernel(cd_tiles, listed, split, piece, total):
    products(cd_tiles, listed, split, [piece], total)


def merge_kernel(mine, received, out):
    out[...] = mine[...] + received[...]


def final_kernel(count, spans, rows, last, received, before, out, total, sems):
    del before
    (place,) = places(count, rows, [(0, count // 2)])

    @pl.when(place < rows * count // 2)
    def _():
        total[...] = last[...] + received[...]
        copies = []
        for span in range(spans):
            copies.append(
                pltpu.make_async_copy(
                    total.at[pl.ds(span * rows, rows), :],
                    out.at[span, pl.ds(pl.multiple_of(place, rows), rows), :],
                    sems.at[span],
                )
            )
            copies[-1].start()
        for copy in copies:
            copy.wait()


def solution(mesh):
    count = mesh.shape["ab"]
    cores = mesh.shape["cd"]
    grid = grid_of(count)
    far = count // 2
    around = []
    for chain in range(2):
        pairs = []
        for at in range(count):
            for core in range(cores):
                to = at + 1 if core == chain else at + count - 1
                pairs.append((at_ring(at, *grid) * cores + core, at_ring(to % count, *grid) * cores + core))
        around.append(pairs)
    swap = [(0, 1), (1, 0)]

    def shards(amplitudes, integrals, ab_irrep, cd_irrep, block_pattern):
        spans, rows, depth = amplitudes.shape
        slab = integrals.shape[0]
        ab_tiles, cd_tiles = block_pattern.shape
        tiles = ab_tiles * cd_tiles
        half = rows * far

        in_hbm = functools.partial(pltpu.with_memory_space_constraint, memory_space=pltpu.HBM)
        smem = pl.BlockSpec(memory_space=pltpu.SMEM)
        vmem = pl.BlockSpec(memory_space=pltpu.VMEM)
        hbm = pl.BlockSpec(memory_space=pltpu.HBM)
        params = pltpu.CompilerParams(vmem_limit_bytes=VMEM_LIMIT)

        listed, split, own = pl.pallas_call(
            functools.partial(pick_kernel, ab_tiles, cd_tiles),
            out_shape=(
                jax.ShapeDtypeStruct((1 + tiles + UNROLL,), jnp.int32),
                pltpu.VMEM((tiles + UNROLL, 2 * TILE, TILE), jnp.bfloat16),
                pltpu.VMEM(amplitudes.shape, jnp.float32),
            ),
            in_specs=[smem, smem, smem, hbm, hbm],
            out_specs=(smem, vmem, vmem),
            scratch_shapes=[
                pltpu.VMEM((FLIGHT, TILE, TILE), jnp.float32),
                pltpu.SemaphoreType.DMA((FLIGHT,)),
                pltpu.SemaphoreType.DMA,
            ],
            compiler_params=params,
            cost_estimate=pl.CostEstimate(flops=0, bytes_accessed=8 << 20, transcendentals=0),
            name="pick",
        )(in_hbm(block_pattern), in_hbm(ab_irrep), in_hbm(cd_irrep), in_hbm(integrals), in_hbm(amplitudes))

        held = {(0, 0): own}
        for chain, piece, hops in ((0, amplitudes, far), (1, own, far - 1)):
            for hop in range(1, hops + 1):
                piece = lax.ppermute(piece, ("ab", "cd"), around[chain])
                held[chain, hop] = piece

        block = pltpu.VMEM((spans, half, slab), jnp.float32)
        parts = ()
        arrivals = [(0, 0)] + [(chain, hop) for hop in range(1, far) for chain in range(2)]
        for at in range(0, len(arrivals), GROUP):
            group = arrivals[at : at + GROUP]
            pieces = [held[chunk] for chunk in group]
            parts = pl.pallas_call(
                functools.partial(step_kernel, count, spans, rows, cd_tiles, group),
                out_shape=(block, block),
                in_specs=[smem] + [vmem] * (1 + len(pieces) + len(parts)),
                out_specs=(vmem, vmem),
                scratch_shapes=[pltpu.VMEM((len(pieces) * spans * rows, slab), jnp.float32)],
                compiler_params=params,
                input_output_aliases={2 + len(pieces): 0, 3 + len(pieces): 1} if parts else {},
                cost_estimate=pl.CostEstimate(flops=1 << 30, bytes_accessed=4 << 20, transcendentals=0),
                name="step",
            )(listed, split, *pieces, *parts)
        mine, send = parts
        base = pl.pallas_call(
            merge_kernel,
            out_shape=pltpu.HBM((spans, half, slab), jnp.float32),
            in_specs=[vmem, vmem],
            out_specs=vmem,
            compiler_params=params,
            name="merge",
        )(mine, lax.ppermute(send, "cd", swap))

        last = pl.pallas_call(
            functools.partial(last_kernel, cd_tiles),
            out_shape=pltpu.VMEM((spans * rows, slab), jnp.float32),
            in_specs=[smem, vmem, vmem],
            out_specs=vmem,
            compiler_params=params,
            cost_estimate=pl.CostEstimate(flops=1 << 34, bytes_accessed=4 << 20, transcendentals=0),
            name="last",
        )(listed, split, held[0, far])
        return pl.pallas_call(
            functools.partial(final_kernel, count, spans, rows),
            out_shape=pltpu.HBM((spans, half, slab), jnp.float32),
            in_specs=[vmem, vmem, hbm],
            out_specs=hbm,
            scratch_shapes=[pltpu.VMEM((spans * rows, slab), jnp.float32), pltpu.SemaphoreType.DMA((spans,))],
            compiler_params=params,
            input_output_aliases={2: 0},
            name="final",
        )(last, lax.ppermute(last, "cd", swap), base)

    in_specs = (
        P("groups", "ab", "cd"),
        P(("groups", "ab"), "cd"),
        P(("groups", "ab")),
        P(("groups", "cd")),
        P(("groups", "ab"), "cd"),
    )
    out_specs = P("groups", "cd", "ab")
    return jax.shard_map(shards, mesh=mesh, in_specs=in_specs, out_specs=out_specs, check_vma=False)
```

```python
import functools

import jax
import jax.numpy as jnp
from jax import lax
from jax.experimental import pallas as pl
from jax.experimental.pallas import tpu as pltpu
from jax.sharding import PartitionSpec as P

TILE = 128
UNROLL = 4
FLIGHT = 32
STEP_FLOPS = 1 << 30
VMEM_LIMIT = 12 * 2**20


def grid_of(count):
    bits = count.bit_length() - 1
    if count != 1 << bits or bits < 2:
        return count, 1
    rows = 1 << ((bits + 1) // 2)
    return rows, count // rows


def at_ring(place, rows, columns):
    if columns == 1:
        return place
    wide = columns - 1
    beyond = place - rows
    line = beyond // wide
    step = beyond - line * wide
    even = (line % 2) == 0
    if isinstance(place, int):
        back = (rows - 1 - line) * columns + (1 + step if even else columns - 1 - step)
        return place * columns if place < rows else back
    back = (rows - 1 - line) * columns + jnp.where(even, 1 + step, columns - 1 - step)
    return jnp.where(place < rows, place * columns, back)


def ring_of(index, rows, columns):
    if columns == 1:
        return index
    wide = columns - 1
    row = index // columns
    column = index - row * columns
    line = rows - 1 - row
    step = jnp.where((line % 2) == 0, column - 1, columns - 1 - column)
    return jnp.where(column == 0, row, rows + line * wide + step)


def place_of(count, rows, offset):
    grid = grid_of(count)
    here = ring_of(lax.axis_index("ab"), *grid)
    whole = rows * count
    start = at_ring((here + offset + count) % count, *grid) * rows + lax.axis_index("cd") * (whole // 2)
    return jnp.where(start >= whole, start - whole, start)


def cut_kernel(amplitudes, *refs):
    spans, sems = refs[:-1], refs[-1]
    copies = [pltpu.make_async_copy(amplitudes.at[pl.ds(at, 1)], span, sems.at[at]) for at, span in enumerate(spans)]
    for copy in copies:
        copy.start()
    for copy in copies:
        copy.wait()


def pick_kernel(ab_tiles, cd_tiles, spans, pattern, ab_irrep, cd_irrep, integrals, amplitudes, listed, split, *refs):
    owns, (landed, sems, own_sems) = refs[:spans], refs[spans:]
    copies = [pltpu.make_async_copy(amplitudes.at[pl.ds(at, 1)], own, own_sems.at[at]) for at, own in enumerate(owns)]
    for copy in copies:
        copy.start()
    second = 1 + ab_tiles * cd_tiles + UNROLL

    def fetch(k):
        slot = k % FLIGHT
        return pltpu.make_async_copy(
            integrals.at[pl.ds(pl.multiple_of(listed[1 + k], TILE), TILE), pl.ds(pl.multiple_of(listed[second + k], TILE), TILE)],
            landed.at[slot],
            sems.at[slot],
        )

    def begin(k, carry):
        fetch(k).start()
        return carry

    def row(p, found):
        label = ab_irrep[p]
        before = found
        for q in range(cd_tiles):
            listed[1 + found] = p * TILE
            listed[second + found] = q * TILE
            keep = jnp.logical_and(pattern[p, q] == 1, label == cd_irrep[q])
            found = found + keep.astype(jnp.int32)
        lax.fori_loop(jnp.minimum(before, FLIGHT), jnp.minimum(found, FLIGHT), begin, 0)
        return found

    found = lax.fori_loop(0, ab_tiles, row, jnp.int32(0))
    rounds = (found + UNROLL - 1) // UNROLL
    listed[0] = rounds
    for extra in range(UNROLL):
        listed[1 + found + extra] = 0
        listed[second + found + extra] = 0
    lax.fori_loop(jnp.minimum(found, FLIGHT), jnp.minimum(rounds * UNROLL, FLIGHT), begin, 0)

    def part(round_at, carry):
        first = round_at * UNROLL
        for unrolled in range(UNROLL):
            fetch(first + unrolled).wait()
        for unrolled in range(UNROLL):
            k = first + unrolled
            tile = jnp.where(k < found, landed[k % FLIGHT], 0.0).T
            upper = tile.astype(jnp.bfloat16)
            split[k, :, :TILE] = upper
            split[k, :, TILE:] = (tile - upper.astype(jnp.float32)).astype(jnp.bfloat16)
        lax.fori_loop(
            jnp.minimum(first + FLIGHT, rounds * UNROLL), jnp.minimum(first + UNROLL + FLIGHT, rounds * UNROLL), begin, 0
        )
        return carry

    lax.fori_loop(0, rounds, part, 0)
    for copy in copies:
        copy.wait()


def products(tiles, listed, split, pieces, total):
    total[...] = jnp.zeros_like(total)

    def step(round_at, carry):
        sums = []
        for unrolled in range(UNROLL):
            k = round_at * UNROLL + unrolled
            columns = pl.ds(pl.multiple_of(listed[1 + tiles + UNROLL + k], TILE), TILE)
            left = jnp.concatenate([piece[0, :, columns] for piece in pieces], axis=0)
            upper = left.astype(jnp.bfloat16)
            lower = (left - upper.astype(jnp.float32)).astype(jnp.bfloat16)
            both = jnp.dot(jnp.concatenate([upper, lower], axis=0), split[k], preferred_element_type=jnp.float32)
            high, low = both[: left.shape[0]], both[left.shape[0] :]
            sums.append((listed[1 + k], high[:, :TILE] + (high[:, TILE:] + (low[:, :TILE] + low[:, TILE:]))))
        for start, term in sums:
            total[:, pl.ds(pl.multiple_of(start, TILE), TILE)] += term
        return carry

    lax.fori_loop(0, listed[0], step, 0)


def step_kernel(count, rows, tiles, group, listed, split, *refs):
    pieces = refs[: len(group)]
    mine, send, total = refs[-3:]
    products(tiles, listed, split, pieces, total)
    half = rows * count // 2
    for at, (span, offset) in enumerate(group):
        place = place_of(count, rows, offset)
        block = total[at * rows : (at + 1) * rows, :]

        @pl.when(place < half)
        def _():
            mine[span, pl.ds(pl.multiple_of(place, rows), rows), :] = block

        @pl.when(place >= half)
        def _():
            send[span, pl.ds(pl.multiple_of(place - half, rows), rows), :] = block


def last_kernel(tiles, listed, split, *refs):
    products(tiles, listed, split, refs[:-1], refs[-1])


def merge_kernel(mine, received, out):
    out[...] = mine[...] + received[...]


def final_kernel(count, spans, rows, last, received, before, out, total, sems):
    del before
    place = place_of(count, rows, -(count // 2))

    @pl.when(place < rows * count // 2)
    def _():
        total[...] = last[...] + received[...]
        copies = []
        for span in range(spans):
            copies.append(
                pltpu.make_async_copy(
                    total.at[pl.ds(span * rows, rows), :],
                    out.at[span, pl.ds(pl.multiple_of(place, rows), rows), :],
                    sems.at[span],
                )
            )
            copies[-1].start()
        for copy in copies:
            copy.wait()


def solution(mesh):
    count = mesh.shape["ab"]
    grid = grid_of(count)
    far = count // 2
    ahead = [(at_ring(at, *grid), at_ring((at + 1) % count, *grid)) for at in range(count)]
    back = [(to, start) for start, to in ahead]
    swap = [(0, 1), (1, 0)]

    def shards(amplitudes, integrals, ab_irrep, cd_irrep, block_pattern):
        spans, rows, depth = amplitudes.shape
        slab = integrals.shape[0]
        ab_tiles, cd_tiles = block_pattern.shape
        tiles = ab_tiles * cd_tiles
        half = rows * far

        in_hbm = functools.partial(pltpu.with_memory_space_constraint, memory_space=pltpu.HBM)
        smem = pl.BlockSpec(memory_space=pltpu.SMEM)
        vmem = pl.BlockSpec(memory_space=pltpu.VMEM)
        hbm = pl.BlockSpec(memory_space=pltpu.HBM)
        params = pltpu.CompilerParams(vmem_limit_bytes=VMEM_LIMIT)
        piece = pltpu.VMEM((1, rows, depth), jnp.float32)

        early = pl.pallas_call(
            cut_kernel,
            out_shape=(piece,) * spans,
            in_specs=[hbm],
            out_specs=(vmem,) * spans,
            scratch_shapes=[pltpu.SemaphoreType.DMA((spans,))],
            compiler_params=params,
            name="cut",
        )(in_hbm(amplitudes))

        listed, split, *late = pl.pallas_call(
            functools.partial(pick_kernel, ab_tiles, cd_tiles, spans),
            out_shape=(
                jax.ShapeDtypeStruct((1 + 2 * (tiles + UNROLL),), jnp.int32),
                pltpu.VMEM((tiles + UNROLL, TILE, 2 * TILE), jnp.bfloat16),
            )
            + (piece,) * spans,
            in_specs=[smem, smem, smem, hbm, hbm],
            out_specs=(smem, vmem) + (vmem,) * spans,
            scratch_shapes=[
                pltpu.VMEM((FLIGHT, TILE, TILE), jnp.float32),
                pltpu.SemaphoreType.DMA((FLIGHT,)),
                pltpu.SemaphoreType.DMA((spans,)),
            ],
            compiler_params=params,
            cost_estimate=pl.CostEstimate(flops=0, bytes_accessed=8 << 20, transcendentals=0),
            name="pick",
        )(in_hbm(block_pattern), in_hbm(ab_irrep), in_hbm(cd_irrep), in_hbm(integrals), in_hbm(amplitudes))

        held = {}
        for span in range(spans):
            held[span, 0] = late[span]
            for pairs, sign in ((ahead, -1), (back, 1)):
                long = (sign < 0) == (span % 2 == 0)
                moved = early[span] if long else late[span]
                for hop in range(1, far + 1 if long else far):
                    moved = lax.ppermute(moved, "ab", pairs)
                    held[span, -far if hop == far else sign * hop] = moved

        def offset_of(span, hop, long):
            return -hop if (span % 2 == 0) == long else hop

        block = pltpu.VMEM((spans, half, slab), jnp.float32)
        parts = ()
        for hop in range(1, far + 1):
            group = [(span, offset_of(span, hop - 1, False)) for span in range(spans)]
            if hop < far:
                group += [(span, offset_of(span, hop, True)) for span in range(spans)]
            pieces = [held[key] for key in group]
            parts = pl.pallas_call(
                functools.partial(step_kernel, count, rows, tiles, group),
                out_shape=(block, block),
                in_specs=[smem] + [vmem] * (1 + len(pieces) + len(parts)),
                out_specs=(vmem, vmem),
                scratch_shapes=[pltpu.VMEM((len(pieces) * rows, slab), jnp.float32)],
                compiler_params=params,
                input_output_aliases={2 + len(pieces): 0, 3 + len(pieces): 1} if parts else {},
                cost_estimate=pl.CostEstimate(flops=STEP_FLOPS, bytes_accessed=4 << 20, transcendentals=0),
                name="step",
            )(listed, split, *pieces, *parts)
        mine, send = parts
        base = pl.pallas_call(
            merge_kernel,
            out_shape=pltpu.HBM((spans, half, slab), jnp.float32),
            in_specs=[vmem, vmem],
            out_specs=vmem,
            compiler_params=params,
            name="merge",
        )(mine, lax.ppermute(send, "cd", swap))

        last = pl.pallas_call(
            functools.partial(last_kernel, tiles),
            out_shape=pltpu.VMEM((spans * rows, slab), jnp.float32),
            in_specs=[smem, vmem] + [vmem] * spans,
            out_specs=vmem,
            compiler_params=params,
            cost_estimate=pl.CostEstimate(flops=1 << 34, bytes_accessed=4 << 20, transcendentals=0),
            name="last",
        )(listed, split, *[held[span, -far] for span in range(spans)])
        return pl.pallas_call(
            functools.partial(final_kernel, count, spans, rows),
            out_shape=pltpu.HBM((spans, half, slab), jnp.float32),
            in_specs=[vmem, vmem, hbm],
            out_specs=hbm,
            scratch_shapes=[pltpu.VMEM((spans * rows, slab), jnp.float32), pltpu.SemaphoreType.DMA((spans,))],
            compiler_params=params,
            input_output_aliases={2: 0},
            name="final",
        )(last, lax.ppermute(last, "cd", swap), base)

    in_specs = (
        P("groups", "ab", "cd"),
        P(("groups", "ab"), "cd"),
        P(("groups", "ab")),
        P(("groups", "cd")),
        P(("groups", "ab"), "cd"),
    )
    out_specs = P("groups", "cd", "ab")
    return jax.shard_map(shards, mesh=mesh, in_specs=in_specs, out_specs=out_specs, check_vma=False)
```

```python
import functools

import jax
import jax.numpy as jnp
from jax import lax
from jax.experimental import pallas as pl
from jax.experimental.pallas import tpu as pltpu
from jax.sharding import PartitionSpec as P

TILE = 128
UNROLL = 4
FLIGHT = 32
GROUP = 12
STEP_FLOPS = 1 << 30
VMEM_LIMIT = 12 * 2**20


def grid_of(count):
    bits = count.bit_length() - 1
    if count != 1 << bits or bits < 2:
        return count, 1
    rows = 1 << ((bits + 1) // 2)
    return rows, count // rows


def at_ring(place, rows, columns):
    if columns == 1:
        return place
    wide = columns - 1
    beyond = place - rows
    line = beyond // wide
    step = beyond - line * wide
    even = (line % 2) == 0
    if isinstance(place, int):
        back = (rows - 1 - line) * columns + (1 + step if even else columns - 1 - step)
        return place * columns if place < rows else back
    back = (rows - 1 - line) * columns + jnp.where(even, 1 + step, columns - 1 - step)
    return jnp.where(place < rows, place * columns, back)


def ring_of(index, rows, columns):
    if columns == 1:
        return index
    wide = columns - 1
    row = index // columns
    column = index - row * columns
    line = rows - 1 - row
    step = jnp.where((line % 2) == 0, column - 1, columns - 1 - column)
    return jnp.where(column == 0, row, rows + line * wide + step)


def place_of(count, rows, offset):
    grid = grid_of(count)
    here = ring_of(lax.axis_index("ab"), *grid)
    whole = rows * count
    start = at_ring((here + offset + count) % count, *grid) * rows + lax.axis_index("cd") * (whole // 2)
    return jnp.where(start >= whole, start - whole, start)


def cut_kernel(amplitudes, *refs):
    spans, sems = refs[:-1], refs[-1]
    copies = [pltpu.make_async_copy(amplitudes.at[pl.ds(at, 1)], span, sems.at[at]) for at, span in enumerate(spans)]
    for copy in copies:
        copy.start()
    for copy in copies:
        copy.wait()


def pick_kernel(ab_tiles, cd_tiles, pattern, ab_irrep, cd_irrep, integrals, listed, split, landed, sems):
    second = 1 + ab_tiles * cd_tiles + UNROLL

    def fetch(k):
        slot = k % FLIGHT
        return pltpu.make_async_copy(
            integrals.at[pl.ds(pl.multiple_of(listed[1 + k], TILE), TILE), pl.ds(pl.multiple_of(listed[second + k], TILE), TILE)],
            landed.at[slot],
            sems.at[slot],
        )

    def begin(k, carry):
        fetch(k).start()
        return carry

    def row(p, found):
        label = ab_irrep[p]
        before = found
        for q in range(cd_tiles):
            listed[1 + found] = p * TILE
            listed[second + found] = q * TILE
            keep = jnp.logical_and(pattern[p, q] == 1, label == cd_irrep[q])
            found = found + keep.astype(jnp.int32)
        lax.fori_loop(jnp.minimum(before, FLIGHT), jnp.minimum(found, FLIGHT), begin, 0)
        return found

    found = lax.fori_loop(0, ab_tiles, row, jnp.int32(0))
    rounds = (found + UNROLL - 1) // UNROLL
    listed[0] = rounds
    for extra in range(UNROLL):
        listed[1 + found + extra] = 0
        listed[second + found + extra] = 0
    lax.fori_loop(jnp.minimum(found, FLIGHT), jnp.minimum(rounds * UNROLL, FLIGHT), begin, 0)

    def part(round_at, carry):
        first = round_at * UNROLL
        for unrolled in range(UNROLL):
            fetch(first + unrolled).wait()
        for unrolled in range(UNROLL):
            k = first + unrolled
            tile = jnp.where(k < found, landed[k % FLIGHT], 0.0).T
            upper = tile.astype(jnp.bfloat16)
            split[k, :, :TILE] = upper
            split[k, :, TILE:] = (tile - upper.astype(jnp.float32)).astype(jnp.bfloat16)
        lax.fori_loop(
            jnp.minimum(first + FLIGHT, rounds * UNROLL), jnp.minimum(first + UNROLL + FLIGHT, rounds * UNROLL), begin, 0
        )
        return carry

    lax.fori_loop(0, rounds, part, 0)


def products(tiles, listed, split, pieces, total):
    total[...] = jnp.zeros_like(total)

    def step(round_at, carry):
        sums = []
        for unrolled in range(UNROLL):
            k = round_at * UNROLL + unrolled
            columns = pl.ds(pl.multiple_of(listed[1 + tiles + UNROLL + k], TILE), TILE)
            left = jnp.concatenate([piece[0, :, columns] for piece in pieces], axis=0)
            upper = left.astype(jnp.bfloat16)
            lower = (left - upper.astype(jnp.float32)).astype(jnp.bfloat16)
            both = jnp.dot(jnp.concatenate([upper, lower], axis=0), split[k], preferred_element_type=jnp.float32)
            high, low = both[: left.shape[0]], both[left.shape[0] :]
            sums.append((listed[1 + k], high[:, :TILE] + (high[:, TILE:] + (low[:, :TILE] + low[:, TILE:]))))
        for start, term in sums:
            total[:, pl.ds(pl.multiple_of(start, TILE), TILE)] += term
        return carry

    lax.fori_loop(0, listed[0], step, 0)


def step_kernel(count, rows, tiles, group, listed, split, *refs):
    pieces = refs[: len(group)]
    mine, send, total = refs[-3:]
    products(tiles, listed, split, pieces, total)
    half = rows * count // 2
    for at, (span, offset) in enumerate(group):
        place = place_of(count, rows, offset)
        block = total[at * rows : (at + 1) * rows, :]

        @pl.when(place < half)
        def _():
            mine[span, pl.ds(pl.multiple_of(place, rows), rows), :] = block

        @pl.when(place >= half)
        def _():
            send[span, pl.ds(pl.multiple_of(place - half, rows), rows), :] = block


def last_kernel(tiles, listed, split, *refs):
    products(tiles, listed, split, refs[:-1], refs[-1])


def merge_kernel(mine, received, out):
    out[...] = mine[...] + received[...]


def final_kernel(count, spans, rows, last, received, before, out, total, sems):
    del before
    place = place_of(count, rows, -(count // 2))

    @pl.when(place < rows * count // 2)
    def _():
        total[...] = last[...] + received[...]
        copies = []
        for span in range(spans):
            copies.append(
                pltpu.make_async_copy(
                    total.at[pl.ds(span * rows, rows), :],
                    out.at[span, pl.ds(pl.multiple_of(place, rows), rows), :],
                    sems.at[span],
                )
            )
            copies[-1].start()
        for copy in copies:
            copy.wait()


def solution(mesh):
    count = mesh.shape["ab"]
    grid = grid_of(count)
    far = count // 2
    ahead = [(at_ring(at, *grid), at_ring((at + 1) % count, *grid)) for at in range(count)]
    back = [(to, start) for start, to in ahead]
    swap = [(0, 1), (1, 0)]

    def shards(amplitudes, integrals, ab_irrep, cd_irrep, block_pattern):
        spans, rows, depth = amplitudes.shape
        slab = integrals.shape[0]
        ab_tiles, cd_tiles = block_pattern.shape
        tiles = ab_tiles * cd_tiles
        half = rows * far

        in_hbm = functools.partial(pltpu.with_memory_space_constraint, memory_space=pltpu.HBM)
        smem = pl.BlockSpec(memory_space=pltpu.SMEM)
        vmem = pl.BlockSpec(memory_space=pltpu.VMEM)
        hbm = pl.BlockSpec(memory_space=pltpu.HBM)
        params = pltpu.CompilerParams(vmem_limit_bytes=VMEM_LIMIT)
        piece = pltpu.VMEM((1, rows, depth), jnp.float32)

        own = pl.pallas_call(
            cut_kernel,
            out_shape=(piece,) * spans,
            in_specs=[hbm],
            out_specs=(vmem,) * spans,
            scratch_shapes=[pltpu.SemaphoreType.DMA((spans,))],
            compiler_params=params,
            name="cut",
        )(in_hbm(amplitudes))

        listed, split = pl.pallas_call(
            functools.partial(pick_kernel, ab_tiles, cd_tiles),
            out_shape=(
                jax.ShapeDtypeStruct((1 + 2 * (tiles + UNROLL),), jnp.int32),
                pltpu.VMEM((tiles + UNROLL, TILE, 2 * TILE), jnp.bfloat16),
            ),
            in_specs=[smem, smem, smem, hbm],
            out_specs=(smem, vmem),
            scratch_shapes=[
                pltpu.VMEM((FLIGHT, TILE, TILE), jnp.float32),
                pltpu.SemaphoreType.DMA((FLIGHT,)),
            ],
            compiler_params=params,
            cost_estimate=pl.CostEstimate(flops=0, bytes_accessed=8 << 20, transcendentals=0),
            name="pick",
        )(in_hbm(block_pattern), in_hbm(ab_irrep), in_hbm(cd_irrep), in_hbm(integrals))

        held = {}
        for span in range(spans):
            held[span, 0] = own[span]
            for pairs, sign in ((ahead, -1), (back, 1)):
                moved = own[span]
                for hop in range(1, far + 1 if (sign < 0) == (span % 2 == 0) else far):
                    if hop == 2:
                        moved, _ = lax.optimization_barrier((moved, listed))
                    moved = lax.ppermute(moved, "ab", pairs)
                    held[span, -far if hop == far else sign * hop] = moved

        def offset_of(span, hop, long):
            return -hop if (span % 2 == 0) == long else hop

        arrivals = [(span, 0) for span in range(spans)]
        for hop in range(1, far):
            arrivals += [(span, offset_of(span, hop, long)) for long in (True, False) for span in range(spans)]
        block = pltpu.VMEM((spans, half, slab), jnp.float32)
        parts = ()
        cuts = sorted({*range(0, len(arrivals) - spans, GROUP), len(arrivals) - spans, len(arrivals)})
        for start, stop in zip(cuts, cuts[1:]):
            group = arrivals[start:stop]
            pieces = [held[key] for key in group]
            parts = pl.pallas_call(
                functools.partial(step_kernel, count, rows, tiles, group),
                out_shape=(block, block),
                in_specs=[smem] + [vmem] * (1 + len(pieces) + len(parts)),
                out_specs=(vmem, vmem),
                scratch_shapes=[pltpu.VMEM((len(pieces) * rows, slab), jnp.float32)],
                compiler_params=params,
                input_output_aliases={2 + len(pieces): 0, 3 + len(pieces): 1} if parts else {},
                cost_estimate=pl.CostEstimate(flops=STEP_FLOPS, bytes_accessed=4 << 20, transcendentals=0),
                name="step",
            )(listed, split, *pieces, *parts)
        mine, send = parts
        base = pl.pallas_call(
            merge_kernel,
            out_shape=pltpu.HBM((spans, half, slab), jnp.float32),
            in_specs=[vmem, vmem],
            out_specs=vmem,
            compiler_params=params,
            name="merge",
        )(mine, lax.ppermute(send, "cd", swap))

        last = pl.pallas_call(
            functools.partial(last_kernel, tiles),
            out_shape=pltpu.VMEM((spans * rows, slab), jnp.float32),
            in_specs=[smem, vmem] + [vmem] * spans,
            out_specs=vmem,
            compiler_params=params,
            cost_estimate=pl.CostEstimate(flops=1 << 34, bytes_accessed=4 << 20, transcendentals=0),
            name="last",
        )(listed, split, *[held[span, -far] for span in range(spans)])
        return pl.pallas_call(
            functools.partial(final_kernel, count, spans, rows),
            out_shape=pltpu.HBM((spans, half, slab), jnp.float32),
            in_specs=[vmem, vmem, hbm],
            out_specs=hbm,
            scratch_shapes=[pltpu.VMEM((spans * rows, slab), jnp.float32), pltpu.SemaphoreType.DMA((spans,))],
            compiler_params=params,
            input_output_aliases={2: 0},
            name="final",
        )(last, lax.ppermute(last, "cd", swap), base)

    in_specs = (
        P("groups", "ab", "cd"),
        P(("groups", "ab"), "cd"),
        P(("groups", "ab")),
        P(("groups", "cd")),
        P(("groups", "ab"), "cd"),
    )
    out_specs = P("groups", "cd", "ab")
    return jax.shard_map(shards, mesh=mesh, in_specs=in_specs, out_specs=out_specs, check_vma=False)
```

```python
import functools

import jax
import jax.numpy as jnp
from jax import lax
from jax.experimental import pallas as pl
from jax.experimental.pallas import tpu as pltpu
from jax.sharding import PartitionSpec as P

TILE = 128
UNROLL = 4
FLIGHT = 32
GROUP = 12
STEP_FLOPS = 1 << 30
VMEM_LIMIT = 12 * 2**20


def grid_of(count):
    bits = count.bit_length() - 1
    if count != 1 << bits or bits < 2:
        return count, 1
    rows = 1 << ((bits + 1) // 2)
    return rows, count // rows


def at_ring(place, rows, columns):
    if columns == 1:
        return place
    wide = columns - 1
    beyond = place - rows
    line = beyond // wide
    step = beyond - line * wide
    even = (line % 2) == 0
    if isinstance(place, int):
        back = (rows - 1 - line) * columns + (1 + step if even else columns - 1 - step)
        return place * columns if place < rows else back
    back = (rows - 1 - line) * columns + jnp.where(even, 1 + step, columns - 1 - step)
    return jnp.where(place < rows, place * columns, back)


def ring_of(index, rows, columns):
    if columns == 1:
        return index
    wide = columns - 1
    row = index // columns
    column = index - row * columns
    line = rows - 1 - row
    step = jnp.where((line % 2) == 0, column - 1, columns - 1 - column)
    return jnp.where(column == 0, row, rows + line * wide + step)


def place_of(count, rows, chain, hop):
    grid = grid_of(count)
    here = ring_of(lax.axis_index("ab"), *grid)
    core = lax.axis_index("cd")
    away = (2 * core - 1) * hop if chain == 0 else (1 - 2 * core) * hop
    whole = rows * count
    start = at_ring((here + away + count) % count, *grid) * rows + core * (whole // 2)
    return jnp.where(start >= whole, start - whole, start)


def cut_kernel(chunk, *spans):
    for at, span in enumerate(spans):
        span[0] = chunk[at]


def pick_kernel(ab_tiles, cd_tiles, pattern, ab_irrep, cd_irrep, integrals, amplitudes, listed, split, own, landed, sems, own_sem):
    copy = pltpu.make_async_copy(amplitudes, own, own_sem)
    copy.start()
    second = 1 + ab_tiles * cd_tiles + UNROLL

    def fetch(k):
        slot = k % FLIGHT
        return pltpu.make_async_copy(
            integrals.at[pl.ds(pl.multiple_of(listed[1 + k], TILE), TILE), pl.ds(pl.multiple_of(listed[second + k], TILE), TILE)],
            landed.at[slot],
            sems.at[slot],
        )

    def begin(k, carry):
        fetch(k).start()
        return carry

    def row(p, found):
        label = ab_irrep[p]
        before = found
        for q in range(cd_tiles):
            listed[1 + found] = p * TILE
            listed[second + found] = q * TILE
            keep = jnp.logical_and(pattern[p, q] == 1, label == cd_irrep[q])
            found = found + keep.astype(jnp.int32)
        lax.fori_loop(jnp.minimum(before, FLIGHT), jnp.minimum(found, FLIGHT), begin, 0)
        return found

    found = lax.fori_loop(0, ab_tiles, row, jnp.int32(0))
    rounds = (found + UNROLL - 1) // UNROLL
    listed[0] = rounds
    for extra in range(UNROLL):
        listed[1 + found + extra] = 0
        listed[second + found + extra] = 0
    lax.fori_loop(jnp.minimum(found, FLIGHT), jnp.minimum(rounds * UNROLL, FLIGHT), begin, 0)

    def part(round_at, carry):
        first = round_at * UNROLL
        for unrolled in range(UNROLL):
            fetch(first + unrolled).wait()
        for unrolled in range(UNROLL):
            k = first + unrolled
            tile = jnp.where(k < found, landed[k % FLIGHT], 0.0).T
            upper = tile.astype(jnp.bfloat16)
            split[k, :, :TILE] = upper
            split[k, :, TILE:] = (tile - upper.astype(jnp.float32)).astype(jnp.bfloat16)
        lax.fori_loop(
            jnp.minimum(first + FLIGHT, rounds * UNROLL), jnp.minimum(first + UNROLL + FLIGHT, rounds * UNROLL), begin, 0
        )
        return carry

    lax.fori_loop(0, rounds, part, 0)
    copy.wait()


def products(tiles, listed, split, pieces, total):
    total[...] = jnp.zeros_like(total)

    def step(round_at, carry):
        sums = []
        for unrolled in range(UNROLL):
            k = round_at * UNROLL + unrolled
            columns = pl.ds(pl.multiple_of(listed[1 + tiles + UNROLL + k], TILE), TILE)
            left = jnp.concatenate([piece[span, :, columns] for piece in pieces for span in range(piece.shape[0])], axis=0)
            upper = left.astype(jnp.bfloat16)
            lower = (left - upper.astype(jnp.float32)).astype(jnp.bfloat16)
            both = jnp.dot(jnp.concatenate([upper, lower], axis=0), split[k], preferred_element_type=jnp.float32)
            high, low = both[: left.shape[0]], both[left.shape[0] :]
            sums.append((listed[1 + k], high[:, :TILE] + (high[:, TILE:] + (low[:, :TILE] + low[:, TILE:]))))
        for start, term in sums:
            total[:, pl.ds(pl.multiple_of(start, TILE), TILE)] += term
        return carry

    lax.fori_loop(0, listed[0], step, 0)


def step_kernel(count, rows, tiles, group, listed, split, *refs):
    pieces = refs[: len(group)]
    mine, send, total = refs[-3:]
    products(tiles, listed, split, pieces, total)
    half = rows * count // 2
    at = 0
    for chain, hop, spans in group:
        place = place_of(count, rows, chain, hop)
        for span in spans:
            block = total[at * rows : (at + 1) * rows, :]
            at += 1

            @pl.when(place < half)
            def _():
                mine[span, pl.ds(pl.multiple_of(place, rows), rows), :] = block

            @pl.when(place >= half)
            def _():
                send[span, pl.ds(pl.multiple_of(place - half, rows), rows), :] = block


def last_kernel(tiles, listed, split, *refs):
    products(tiles, listed, split, refs[:-1], refs[-1])


def merge_kernel(mine, received, out):
    out[...] = mine[...] + received[...]


def final_kernel(count, spans, rows, last, received, before, out, total, sems):
    del before
    place = place_of(count, rows, 0, count // 2)

    @pl.when(place < rows * count // 2)
    def _():
        total[...] = last[...] + received[...]
        copies = []
        for span in range(spans):
            copies.append(
                pltpu.make_async_copy(
                    total.at[pl.ds(span * rows, rows), :],
                    out.at[span, pl.ds(pl.multiple_of(place, rows), rows), :],
                    sems.at[span],
                )
            )
            copies[-1].start()
        for copy in copies:
            copy.wait()


def solution(mesh):
    count = mesh.shape["ab"]
    cores = mesh.shape["cd"]
    grid = grid_of(count)
    far = count // 2
    around = []
    for chain in range(2):
        pairs = []
        for at in range(count):
            for core in range(cores):
                to = at + 1 if core == chain else at + count - 1
                pairs.append((at_ring(at, *grid) * cores + core, at_ring(to % count, *grid) * cores + core))
        around.append(pairs)
    swap = [(0, 1), (1, 0)]

    def shards(amplitudes, integrals, ab_irrep, cd_irrep, block_pattern):
        spans, rows, depth = amplitudes.shape
        slab = integrals.shape[0]
        ab_tiles, cd_tiles = block_pattern.shape
        tiles = ab_tiles * cd_tiles
        half = rows * far

        in_hbm = functools.partial(pltpu.with_memory_space_constraint, memory_space=pltpu.HBM)
        smem = pl.BlockSpec(memory_space=pltpu.SMEM)
        vmem = pl.BlockSpec(memory_space=pltpu.VMEM)
        hbm = pl.BlockSpec(memory_space=pltpu.HBM)
        params = pltpu.CompilerParams(vmem_limit_bytes=VMEM_LIMIT)

        listed, split, own = pl.pallas_call(
            functools.partial(pick_kernel, ab_tiles, cd_tiles),
            out_shape=(
                jax.ShapeDtypeStruct((1 + 2 * (tiles + UNROLL),), jnp.int32),
                pltpu.VMEM((tiles + UNROLL, TILE, 2 * TILE), jnp.bfloat16),
                pltpu.VMEM(amplitudes.shape, jnp.float32),
            ),
            in_specs=[smem, smem, smem, hbm, hbm],
            out_specs=(smem, vmem, vmem),
            scratch_shapes=[
                pltpu.VMEM((FLIGHT, TILE, TILE), jnp.float32),
                pltpu.SemaphoreType.DMA((FLIGHT,)),
                pltpu.SemaphoreType.DMA,
            ],
            compiler_params=params,
            cost_estimate=pl.CostEstimate(flops=0, bytes_accessed=8 << 20, transcendentals=0),
            name="pick",
        )(in_hbm(block_pattern), in_hbm(ab_irrep), in_hbm(cd_irrep), in_hbm(integrals), in_hbm(amplitudes))

        block = pltpu.VMEM((spans, half, slab), jnp.float32)

        def step(group, parts):
            pieces = [piece for *_, piece in group]
            height = sum(piece.shape[0] for piece in pieces) * rows
            return pl.pallas_call(
                functools.partial(step_kernel, count, rows, tiles, [key for *key, _ in group]),
                out_shape=(block, block),
                in_specs=[smem] + [vmem] * (1 + len(pieces) + len(parts)),
                out_specs=(vmem, vmem),
                scratch_shapes=[pltpu.VMEM((height, slab), jnp.float32)],
                compiler_params=params,
                input_output_aliases={2 + len(pieces): 0, 3 + len(pieces): 1} if parts else {},
                cost_estimate=pl.CostEstimate(flops=STEP_FLOPS, bytes_accessed=4 << 20, transcendentals=0),
                name="step",
            )(listed, split, *pieces, *parts)

        def send_on(piece, chain):
            return lax.ppermute(piece, ("ab", "cd"), around[chain])

        both = tuple(range(spans))
        parts = step([(0, 0, both, own)], ())
        first = []
        for chain in range(2):
            arrived, _ = lax.optimization_barrier((send_on(amplitudes, chain), parts[0]))
            first.append(arrived)
        moving = {}
        for chain in range(2):
            cut = pl.pallas_call(
                cut_kernel,
                out_shape=(pltpu.VMEM((1, rows, depth), jnp.float32),) * spans,
                in_specs=[vmem],
                out_specs=(vmem,) * spans,
                compiler_params=params,
                name="cut",
            )(first[chain])
            for span in both:
                moving[chain, span] = cut[span]
        order = [(chain, span) for short in (False, True) for chain in range(2) for span in both if (span % 2 != chain) == short]
        arrivals = [(chain, 1, both, first[chain]) for chain in range(2)]
        final = {}
        for hop in range(2, far + 1):
            for chain, span in order:
                if hop < far or span % 2 == chain:
                    moving[chain, span] = send_on(moving[chain, span], chain)
                    if hop < far:
                        arrivals.append((chain, hop, (span,), moving[chain, span]))
                    else:
                        final[span] = moving[chain, span]
        short = len(arrivals) - spans
        cuts = sorted({*range(0, short, GROUP), short, len(arrivals)})
        for start, stop in zip(cuts, cuts[1:]):
            parts = step(arrivals[start:stop], parts)
        mine, send = parts
        base = pl.pallas_call(
            merge_kernel,
            out_shape=pltpu.HBM((spans, half, slab), jnp.float32),
            in_specs=[vmem, vmem],
            out_specs=vmem,
            compiler_params=params,
            name="merge",
        )(mine, lax.ppermute(send, "cd", swap))

        last = pl.pallas_call(
            functools.partial(last_kernel, tiles),
            out_shape=pltpu.VMEM((spans * rows, slab), jnp.float32),
            in_specs=[smem, vmem] + [vmem] * spans,
            out_specs=vmem,
            compiler_params=params,
            cost_estimate=pl.CostEstimate(flops=1 << 34, bytes_accessed=4 << 20, transcendentals=0),
            name="last",
        )(listed, split, *[final[span] for span in both])
        return pl.pallas_call(
            functools.partial(final_kernel, count, spans, rows),
            out_shape=pltpu.HBM((spans, half, slab), jnp.float32),
            in_specs=[vmem, vmem, hbm],
            out_specs=hbm,
            scratch_shapes=[pltpu.VMEM((spans * rows, slab), jnp.float32), pltpu.SemaphoreType.DMA((spans,))],
            compiler_params=params,
            input_output_aliases={2: 0},
            name="final",
        )(last, lax.ppermute(last, "cd", swap), base)

    in_specs = (
        P("groups", "ab", "cd"),
        P(("groups", "ab"), "cd"),
        P(("groups", "ab")),
        P(("groups", "cd")),
        P(("groups", "ab"), "cd"),
    )
    out_specs = P("groups", "cd", "ab")
    return jax.shard_map(shards, mesh=mesh, in_specs=in_specs, out_specs=out_specs, check_vma=False)
```

```python
import functools

import jax
import jax.numpy as jnp
from jax import lax
from jax.experimental import pallas as pl
from jax.experimental.pallas import tpu as pltpu
from jax.sharding import PartitionSpec as P

TILE = 128
UNROLL = 4
PLACE_BITS = 12
FLIGHT = 32
PLACES = 1 << PLACE_BITS
GROUP = 12
STEP_FLOPS = 1 << 30
VMEM_LIMIT = 12 * 2**20


def grid_of(count):
    bits = count.bit_length() - 1
    if count != 1 << bits or bits < 2:
        return count, 1
    rows = 1 << ((bits + 1) // 2)
    return rows, count // rows


def at_ring(place, rows, columns):
    if columns == 1:
        return place
    wide = columns - 1
    beyond = place - rows
    line = beyond // wide
    step = beyond - line * wide
    even = (line % 2) == 0
    if isinstance(place, int):
        back = (rows - 1 - line) * columns + (1 + step if even else columns - 1 - step)
        return place * columns if place < rows else back
    back = (rows - 1 - line) * columns + jnp.where(even, 1 + step, columns - 1 - step)
    return jnp.where(place < rows, place * columns, back)


def ring_of(index, rows, columns):
    if columns == 1:
        return index
    wide = columns - 1
    row = index // columns
    column = index - row * columns
    line = rows - 1 - row
    step = jnp.where((line % 2) == 0, column - 1, columns - 1 - column)
    return jnp.where(column == 0, row, rows + line * wide + step)


def place_of(count, rows, offset):
    grid = grid_of(count)
    here = ring_of(lax.axis_index("ab"), *grid)
    whole = rows * count
    start = at_ring((here + offset + count) % count, *grid) * rows + lax.axis_index("cd") * (whole // 2)
    return jnp.where(start >= whole, start - whole, start)


def cut_kernel(amplitudes, pattern, ab_irrep, cd_irrep, *refs):
    *outs, sems = refs
    spans = len(outs) - 3
    pairs = [(amplitudes.at[pl.ds(at, 1)], outs[at]) for at in range(spans)]
    pairs += list(zip((pattern, ab_irrep, cd_irrep), outs[spans:]))
    copies = [pltpu.make_async_copy(start, end, sems.at[at]) for at, (start, end) in enumerate(pairs)]
    for copy in copies:
        copy.start()
    for copy in copies:
        copy.wait()


def pick_kernel(ab_tiles, cd_tiles, pattern, ab_irrep, cd_irrep, integrals, listed, split, landed, sems):
    columns = [cd_irrep[q] for q in range(cd_tiles)]

    def fetch(k):
        start, column = place_in(listed[1 + k])
        slot = lax.rem(k, FLIGHT)
        return pltpu.make_async_copy(
            integrals.at[pl.ds(start, TILE), pl.ds(column, TILE)], landed.at[slot], sems.at[slot]
        )

    def begin(k, carry):
        fetch(k).start()
        return carry

    def row(p, found):
        label = ab_irrep[p]
        before = found
        for q in range(cd_tiles):
            listed[1 + found] = p * PLACES + q
            keep = jnp.logical_and(pattern[p, q] == 1, label == columns[q])
            found = found + keep.astype(jnp.int32)
        lax.fori_loop(jnp.minimum(before, FLIGHT), jnp.minimum(found, FLIGHT), begin, 0)
        return found

    found = lax.fori_loop(0, ab_tiles, row, jnp.int32(0))
    rounds = lax.div(found + (UNROLL - 1), UNROLL)
    last = rounds * UNROLL
    listed[0] = rounds
    for extra in range(UNROLL):
        listed[1 + found + extra] = 0
    lax.fori_loop(jnp.minimum(found, FLIGHT), jnp.minimum(last, FLIGHT), begin, 0)

    def part(round_at, carry):
        first = round_at * UNROLL
        for unrolled in range(UNROLL):
            fetch(first + unrolled).wait()
        for unrolled in range(UNROLL):
            k = first + unrolled
            tile = jnp.where(k < found, landed[lax.rem(k, FLIGHT)], 0.0).T
            upper = tile.astype(jnp.bfloat16)
            split[k, :, :TILE] = upper
            split[k, :, TILE:] = (tile - upper.astype(jnp.float32)).astype(jnp.bfloat16)
        lax.fori_loop(jnp.minimum(first + FLIGHT, last), jnp.minimum(first + UNROLL + FLIGHT, last), begin, 0)
        return carry

    lax.fori_loop(0, rounds, part, 0)


def place_in(code):
    return (
        pl.multiple_of(lax.shift_right_logical(code, PLACE_BITS) * TILE, TILE),
        pl.multiple_of(lax.bitwise_and(code, PLACES - 1) * TILE, TILE),
    )


def products(listed, split, pieces, total):
    total[...] = jnp.zeros_like(total)

    def some(first, many):
        sums = []
        for unrolled in range(many):
            start, column = place_in(listed[1 + first + unrolled])
            left = jnp.concatenate([piece[0, :, pl.ds(column, TILE)] for piece in pieces], axis=0)
            upper = left.astype(jnp.bfloat16)
            lower = (left - upper.astype(jnp.float32)).astype(jnp.bfloat16)
            tile = split[first + unrolled]
            both = jnp.dot(jnp.concatenate([upper, lower], axis=0), tile, preferred_element_type=jnp.float32)
            high, low = both[: left.shape[0]], both[left.shape[0] :]
            sums.append((start, high[:, :TILE] + (high[:, TILE:] + (low[:, :TILE] + low[:, TILE:]))))
        for start, term in sums:
            total[:, pl.ds(start, TILE)] += term

    def step(at, carry):
        some(at * 2 * UNROLL, 2 * UNROLL)
        return carry

    rounds = listed[0]
    lax.fori_loop(0, rounds // 2, step, 0)

    @pl.when(rounds % 2 == 1)
    def _():
        some((rounds - 1) * UNROLL, UNROLL)


def step_kernel(count, rows, group, listed, split, *refs):
    pieces = refs[: len(group)]
    mine, send, total = refs[-3:]
    products(listed, split, pieces, total)
    half = rows * count // 2
    for at, (span, offset) in enumerate(group):
        place = place_of(count, rows, offset)
        block = total[at * rows : (at + 1) * rows, :]

        @pl.when(place < half)
        def _():
            mine[span, pl.ds(pl.multiple_of(place, rows), rows), :] = block

        @pl.when(place >= half)
        def _():
            send[span, pl.ds(pl.multiple_of(place - half, rows), rows), :] = block


def last_kernel(listed, split, *refs):
    products(listed, split, refs[:-1], refs[-1])


def merge_kernel(mine, received, out):
    out[...] = mine[...] + received[...]


def final_kernel(count, spans, rows, last, received, before, out, total, sems):
    del before
    place = place_of(count, rows, -(count // 2))

    @pl.when(place < rows * count // 2)
    def _():
        total[...] = last[...] + received[...]
        copies = []
        for span in range(spans):
            copies.append(
                pltpu.make_async_copy(
                    total.at[pl.ds(span * rows, rows), :],
                    out.at[span, pl.ds(pl.multiple_of(place, rows), rows), :],
                    sems.at[span],
                )
            )
            copies[-1].start()
        for copy in copies:
            copy.wait()


def solution(mesh):
    count = mesh.shape["ab"]
    grid = grid_of(count)
    far = count // 2
    ahead = [(at_ring(at, *grid), at_ring((at + 1) % count, *grid)) for at in range(count)]
    back = [(to, start) for start, to in ahead]
    swap = [(0, 1), (1, 0)]

    def shards(amplitudes, integrals, ab_irrep, cd_irrep, block_pattern):
        spans, rows, depth = amplitudes.shape
        slab = integrals.shape[0]
        ab_tiles, cd_tiles = block_pattern.shape
        tiles = ab_tiles * cd_tiles
        half = rows * far

        in_hbm = functools.partial(pltpu.with_memory_space_constraint, memory_space=pltpu.HBM)
        smem = pl.BlockSpec(memory_space=pltpu.SMEM)
        vmem = pl.BlockSpec(memory_space=pltpu.VMEM)
        hbm = pl.BlockSpec(memory_space=pltpu.HBM)
        params = pltpu.CompilerParams(vmem_limit_bytes=VMEM_LIMIT)
        piece = pltpu.VMEM((1, rows, depth), jnp.float32)

        labels = (block_pattern, ab_irrep, cd_irrep)
        *own, near_pattern, near_ab, near_cd = pl.pallas_call(
            cut_kernel,
            out_shape=(piece,) * spans + tuple(pltpu.VMEM(label.shape, label.dtype) for label in labels),
            in_specs=[hbm] * 4,
            out_specs=(vmem,) * (spans + 3),
            scratch_shapes=[pltpu.SemaphoreType.DMA((spans + 3,))],
            compiler_params=params,
            name="cut",
        )(in_hbm(amplitudes), *map(in_hbm, labels))

        listed, split = pl.pallas_call(
            functools.partial(pick_kernel, ab_tiles, cd_tiles),
            out_shape=(
                jax.ShapeDtypeStruct((1 + tiles + UNROLL,), jnp.int32),
                pltpu.VMEM((tiles + UNROLL, TILE, 2 * TILE), jnp.bfloat16),
            ),
            in_specs=[smem, smem, smem, hbm],
            out_specs=(smem, vmem),
            scratch_shapes=[pltpu.VMEM((FLIGHT, TILE, TILE), jnp.float32), pltpu.SemaphoreType.DMA((FLIGHT,))],
            compiler_params=params,
            cost_estimate=pl.CostEstimate(flops=0, bytes_accessed=8 << 20, transcendentals=0),
            name="pick",
        )(near_pattern, near_ab, near_cd, in_hbm(integrals))

        held = {}
        for span in range(spans):
            held[span, 0] = own[span]
            for pairs, sign in ((ahead, -1), (back, 1)):
                moved = own[span]
                for hop in range(1, far + 1 if (sign < 0) == (span % 2 == 0) else far):
                    if hop == 2:
                        moved, _ = lax.optimization_barrier((moved, listed))
                    moved = lax.ppermute(moved, "ab", pairs)
                    held[span, -far if hop == far else sign * hop] = moved

        def offset_of(span, hop, long):
            return -hop if (span % 2 == 0) == long else hop

        arrivals = [(span, 0) for span in range(spans)]
        for hop in range(1, far):
            arrivals += [(span, offset_of(span, hop, long)) for long in (True, False) for span in range(spans)]
        block = pltpu.VMEM((spans, half, slab), jnp.float32)
        parts = ()
        cuts = sorted({*range(0, len(arrivals) - spans, GROUP), len(arrivals) - spans, len(arrivals)})
        for start, stop in zip(cuts, cuts[1:]):
            group = arrivals[start:stop]
            pieces = [held[key] for key in group]
            parts = pl.pallas_call(
                functools.partial(step_kernel, count, rows, group),
                out_shape=(block, block),
                in_specs=[smem] + [vmem] * (1 + len(pieces) + len(parts)),
                out_specs=(vmem, vmem),
                scratch_shapes=[pltpu.VMEM((len(pieces) * rows, slab), jnp.float32)],
                compiler_params=params,
                input_output_aliases={2 + len(pieces): 0, 3 + len(pieces): 1} if parts else {},
                cost_estimate=pl.CostEstimate(flops=STEP_FLOPS, bytes_accessed=4 << 20, transcendentals=0),
                name="step",
            )(listed, split, *pieces, *parts)
        mine, send = parts
        base = pl.pallas_call(
            merge_kernel,
            out_shape=pltpu.HBM((spans, half, slab), jnp.float32),
            in_specs=[vmem, vmem],
            out_specs=vmem,
            compiler_params=params,
            name="merge",
        )(mine, lax.ppermute(send, "cd", swap))

        last = pl.pallas_call(
            last_kernel,
            out_shape=pltpu.VMEM((spans * rows, slab), jnp.float32),
            in_specs=[smem, vmem] + [vmem] * spans,
            out_specs=vmem,
            compiler_params=params,
            cost_estimate=pl.CostEstimate(flops=1 << 34, bytes_accessed=4 << 20, transcendentals=0),
            name="last",
        )(listed, split, *[held[span, -far] for span in range(spans)])
        return pl.pallas_call(
            functools.partial(final_kernel, count, spans, rows),
            out_shape=pltpu.HBM((spans, half, slab), jnp.float32),
            in_specs=[vmem, vmem, hbm],
            out_specs=hbm,
            scratch_shapes=[pltpu.VMEM((spans * rows, slab), jnp.float32), pltpu.SemaphoreType.DMA((spans,))],
            compiler_params=params,
            input_output_aliases={2: 0},
            name="final",
        )(last, lax.ppermute(last, "cd", swap), base)

    in_specs = (
        P("groups", "ab", "cd"),
        P(("groups", "ab"), "cd"),
        P(("groups", "ab")),
        P(("groups", "cd")),
        P(("groups", "ab"), "cd"),
    )
    out_specs = P("groups", "cd", "ab")
    return jax.shard_map(shards, mesh=mesh, in_specs=in_specs, out_specs=out_specs, check_vma=False)
```

```python
import functools

import jax
import jax.numpy as jnp
from jax import lax
from jax.experimental import pallas as pl
from jax.experimental.pallas import tpu as pltpu
from jax.sharding import PartitionSpec as P

TILE = 128
UNROLL = 4
LANES = 128
FLIGHT = 32
GROUP = 12
STEP_FLOPS = 1 << 30
VMEM_LIMIT = 12 * 2**20


def grid_of(count):
    bits = count.bit_length() - 1
    if count != 1 << bits or bits < 2:
        return count, 1
    rows = 1 << ((bits + 1) // 2)
    return rows, count // rows


def at_ring(place, rows, columns):
    if columns == 1:
        return place
    wide = columns - 1
    beyond = place - rows
    line = beyond // wide
    step = beyond - line * wide
    even = (line % 2) == 0
    if isinstance(place, int):
        back = (rows - 1 - line) * columns + (1 + step if even else columns - 1 - step)
        return place * columns if place < rows else back
    back = (rows - 1 - line) * columns + jnp.where(even, 1 + step, columns - 1 - step)
    return jnp.where(place < rows, place * columns, back)


def ring_of(index, rows, columns):
    if columns == 1:
        return index
    wide = columns - 1
    row = index // columns
    column = index - row * columns
    line = rows - 1 - row
    step = jnp.where((line % 2) == 0, column - 1, columns - 1 - column)
    return jnp.where(column == 0, row, rows + line * wide + step)


def place_of(count, rows, offset):
    grid = grid_of(count)
    here = ring_of(lax.axis_index("ab"), *grid)
    whole = rows * count
    start = at_ring((here + offset + count) % count, *grid) * rows + lax.axis_index("cd") * (whole // 2)
    return jnp.where(start >= whole, start - whole, start)


def cut_kernel(amplitudes, pattern, ab_irrep, cd_irrep, *refs):
    *outs, sems = refs
    spans = len(outs) - 3
    pairs = [(amplitudes.at[pl.ds(at, 1)], outs[at]) for at in range(spans)]
    pairs += list(zip((pattern, ab_irrep, cd_irrep), outs[spans:]))
    copies = [pltpu.make_async_copy(start, end, sems.at[at]) for at, (start, end) in enumerate(pairs)]
    for copy in copies:
        copy.start()
    for copy in copies:
        copy.wait()


def list_kernel(ab_tiles, cd_tiles, ab_irrep, cd_irrep, pattern, listed):
    shape = (ab_tiles, LANES)
    lane = lax.broadcasted_iota(jnp.int32, shape, 1)
    line = lax.broadcasted_iota(jnp.int32, shape, 0)
    rows = jnp.full(shape, -1, jnp.int32)
    columns = jnp.full(shape, -2, jnp.int32)
    for p in range(ab_tiles):
        rows = jnp.where(line == p, ab_irrep[p], rows)
    for q in range(cd_tiles):
        columns = jnp.where(lane == q, cd_irrep[q], columns)
    stored = jnp.concatenate([pattern[...], jnp.zeros((ab_tiles, LANES - cd_tiles), jnp.int32)], axis=1)
    keep = jnp.where(jnp.logical_and(stored == 1, rows == columns), 1.0, 0.0)

    upto = keep
    reach = 1
    while reach < cd_tiles:
        upto += jnp.where(lane >= reach, pltpu.roll(upto, reach, 1), 0.0)
        reach *= 2
    whole = jnp.broadcast_to(jnp.sum(keep, axis=1, keepdims=True), shape)
    before = whole
    reach = 1
    while reach < ab_tiles:
        before += jnp.where(line >= reach, pltpu.roll(before, reach, 0), 0.0)
        reach *= 2
    found = before[ab_tiles - 1 :, :]
    upto += before - whole

    turned = upto.T
    order = lax.broadcasted_iota(jnp.int32, (cd_tiles, LANES), 1).astype(jnp.float32)
    passed = jnp.zeros((cd_tiles, LANES), jnp.float32)
    for p in range(ab_tiles):
        passed += jnp.where(turned[:cd_tiles, p : p + 1] <= order, 1.0, 0.0)
    places = jnp.sum(passed, axis=0, keepdims=True)
    listed[0:1, :] = jnp.where(order[0:1, :] < found, places, 0.0).astype(jnp.int32)
    listed[1:2, :] = ((found + (UNROLL - 1)) * (1.0 / UNROLL)).astype(jnp.int32)


def part_kernel(cd_tiles, listed, integrals, split, landed, sems):
    last = listed[1, 0] * UNROLL

    def fetch(k):
        start, column = place_in(listed[0, k], cd_tiles)
        slot = lax.rem(k, FLIGHT)
        return pltpu.make_async_copy(
            integrals.at[pl.ds(start, TILE), pl.ds(column, TILE)], landed.at[slot], sems.at[slot]
        )

    def begin(k, carry):
        fetch(k).start()
        return carry

    lax.fori_loop(0, jnp.minimum(last, FLIGHT), begin, 0)

    def part(round_at, carry):
        first = round_at * UNROLL
        for unrolled in range(UNROLL):
            fetch(first + unrolled).wait()
        for unrolled in range(UNROLL):
            k = first + unrolled
            real = jnp.logical_or(k == 0, listed[0, k] > 0)
            tile = jnp.where(real, landed[lax.rem(k, FLIGHT)], 0.0).T
            upper = tile.astype(jnp.bfloat16)
            split[k, :, :TILE] = upper
            split[k, :, TILE:] = (tile - upper.astype(jnp.float32)).astype(jnp.bfloat16)
        lax.fori_loop(jnp.minimum(first + FLIGHT, last), jnp.minimum(first + UNROLL + FLIGHT, last), begin, 0)
        return carry

    lax.fori_loop(0, listed[1, 0], part, 0)


def place_in(place, cd_tiles):
    row = lax.div(place, cd_tiles)
    return pl.multiple_of(row * TILE, TILE), pl.multiple_of((place - row * cd_tiles) * TILE, TILE)


def products(cd_tiles, listed, split, pieces, total):
    total[...] = jnp.zeros_like(total)

    def some(first, many):
        sums = []
        for unrolled in range(many):
            start, column = place_in(listed[0, first + unrolled], cd_tiles)
            left = jnp.concatenate([piece[0, :, pl.ds(column, TILE)] for piece in pieces], axis=0)
            upper = left.astype(jnp.bfloat16)
            lower = (left - upper.astype(jnp.float32)).astype(jnp.bfloat16)
            tile = split[first + unrolled]
            both = jnp.dot(jnp.concatenate([upper, lower], axis=0), tile, preferred_element_type=jnp.float32)
            high, low = both[: left.shape[0]], both[left.shape[0] :]
            sums.append((start, high[:, :TILE] + (high[:, TILE:] + (low[:, :TILE] + low[:, TILE:]))))
        for start, term in sums:
            total[:, pl.ds(start, TILE)] += term

    def step(at, carry):
        some(at * 2 * UNROLL, 2 * UNROLL)
        return carry

    rounds = listed[1, 0]
    lax.fori_loop(0, lax.div(rounds, 2), step, 0)

    @pl.when(lax.rem(rounds, 2) == 1)
    def _():
        some((rounds - 1) * UNROLL, UNROLL)


def step_kernel(count, rows, cd_tiles, group, listed, split, *refs):
    pieces = refs[: len(group)]
    mine, send, total = refs[-3:]
    products(cd_tiles, listed, split, pieces, total)
    half = rows * count // 2
    for at, (span, offset) in enumerate(group):
        place = place_of(count, rows, offset)
        block = total[at * rows : (at + 1) * rows, :]

        @pl.when(place < half)
        def _():
            mine[span, pl.ds(pl.multiple_of(place, rows), rows), :] = block

        @pl.when(place >= half)
        def _():
            send[span, pl.ds(pl.multiple_of(place - half, rows), rows), :] = block


def last_kernel(cd_tiles, listed, split, *refs):
    products(cd_tiles, listed, split, refs[:-1], refs[-1])


def merge_kernel(mine, received, out):
    out[...] = mine[...] + received[...]


def final_kernel(count, spans, rows, last, received, before, out, total, sems):
    del before
    place = place_of(count, rows, -(count // 2))

    @pl.when(place < rows * count // 2)
    def _():
        total[...] = last[...] + received[...]
        copies = []
        for span in range(spans):
            copies.append(
                pltpu.make_async_copy(
                    total.at[pl.ds(span * rows, rows), :],
                    out.at[span, pl.ds(pl.multiple_of(place, rows), rows), :],
                    sems.at[span],
                )
            )
            copies[-1].start()
        for copy in copies:
            copy.wait()


def solution(mesh):
    count = mesh.shape["ab"]
    grid = grid_of(count)
    far = count // 2
    ahead = [(at_ring(at, *grid), at_ring((at + 1) % count, *grid)) for at in range(count)]
    back = [(to, start) for start, to in ahead]
    swap = [(0, 1), (1, 0)]

    def shards(amplitudes, integrals, ab_irrep, cd_irrep, block_pattern):
        spans, rows, depth = amplitudes.shape
        slab = integrals.shape[0]
        ab_tiles, cd_tiles = block_pattern.shape
        tiles = ab_tiles * cd_tiles
        half = rows * far

        in_hbm = functools.partial(pltpu.with_memory_space_constraint, memory_space=pltpu.HBM)
        smem = pl.BlockSpec(memory_space=pltpu.SMEM)
        vmem = pl.BlockSpec(memory_space=pltpu.VMEM)
        hbm = pl.BlockSpec(memory_space=pltpu.HBM)
        params = pltpu.CompilerParams(vmem_limit_bytes=VMEM_LIMIT)
        piece = pltpu.VMEM((1, rows, depth), jnp.float32)

        labels = (block_pattern, ab_irrep, cd_irrep)
        *own, near_pattern, near_ab, near_cd = pl.pallas_call(
            cut_kernel,
            out_shape=(piece,) * spans + tuple(pltpu.VMEM(label.shape, label.dtype) for label in labels),
            in_specs=[hbm] * 4,
            out_specs=(vmem,) * (spans + 3),
            scratch_shapes=[pltpu.SemaphoreType.DMA((spans + 3,))],
            compiler_params=params,
            name="cut",
        )(in_hbm(amplitudes), *map(in_hbm, labels))

        listed = pl.pallas_call(
            functools.partial(list_kernel, ab_tiles, cd_tiles),
            out_shape=pltpu.VMEM((2, LANES), jnp.int32),
            in_specs=[smem, smem, vmem],
            out_specs=vmem,
            compiler_params=params,
            cost_estimate=pl.CostEstimate(flops=0, bytes_accessed=4 << 20, transcendentals=0),
            name="list",
        )(near_ab, near_cd, near_pattern)
        split = pl.pallas_call(
            functools.partial(part_kernel, cd_tiles),
            out_shape=pltpu.VMEM((tiles, TILE, 2 * TILE), jnp.bfloat16),
            in_specs=[smem, hbm],
            out_specs=vmem,
            scratch_shapes=[pltpu.VMEM((FLIGHT, TILE, TILE), jnp.float32), pltpu.SemaphoreType.DMA((FLIGHT,))],
            compiler_params=params,
            cost_estimate=pl.CostEstimate(flops=0, bytes_accessed=8 << 20, transcendentals=0),
            name="part",
        )(listed, in_hbm(integrals))

        held = {}
        for span in range(spans):
            held[span, 0] = own[span]
            for pairs, sign in ((ahead, -1), (back, 1)):
                moved = own[span]
                for hop in range(1, far + 1 if (sign < 0) == (span % 2 == 0) else far):
                    if hop in (2, 3):
                        moved, _ = lax.optimization_barrier((moved, listed if hop == 2 else split))
                    moved = lax.ppermute(moved, "ab", pairs)
                    held[span, -far if hop == far else sign * hop] = moved

        def offset_of(span, hop, long):
            return -hop if (span % 2 == 0) == long else hop

        arrivals = [(span, 0) for span in range(spans)]
        for hop in range(1, far):
            arrivals += [(span, offset_of(span, hop, long)) for long in (True, False) for span in range(spans)]
        block = pltpu.VMEM((spans, half, slab), jnp.float32)
        parts = ()
        cuts = sorted({*range(0, len(arrivals) - spans, GROUP), len(arrivals) - spans, len(arrivals)})
        for start, stop in zip(cuts, cuts[1:]):
            group = arrivals[start:stop]
            pieces = [held[key] for key in group]
            parts = pl.pallas_call(
                functools.partial(step_kernel, count, rows, cd_tiles, group),
                out_shape=(block, block),
                in_specs=[smem] + [vmem] * (1 + len(pieces) + len(parts)),
                out_specs=(vmem, vmem),
                scratch_shapes=[pltpu.VMEM((len(pieces) * rows, slab), jnp.float32)],
                compiler_params=params,
                input_output_aliases={2 + len(pieces): 0, 3 + len(pieces): 1} if parts else {},
                cost_estimate=pl.CostEstimate(flops=STEP_FLOPS, bytes_accessed=4 << 20, transcendentals=0),
                name="step",
            )(listed, split, *pieces, *parts)
        mine, send = parts
        base = pl.pallas_call(
            merge_kernel,
            out_shape=pltpu.HBM((spans, half, slab), jnp.float32),
            in_specs=[vmem, vmem],
            out_specs=vmem,
            compiler_params=params,
            name="merge",
        )(mine, lax.ppermute(send, "cd", swap))

        last = pl.pallas_call(
            functools.partial(last_kernel, cd_tiles),
            out_shape=pltpu.VMEM((spans * rows, slab), jnp.float32),
            in_specs=[smem, vmem] + [vmem] * spans,
            out_specs=vmem,
            compiler_params=params,
            cost_estimate=pl.CostEstimate(flops=1 << 34, bytes_accessed=4 << 20, transcendentals=0),
            name="last",
        )(listed, split, *[held[span, -far] for span in range(spans)])
        return pl.pallas_call(
            functools.partial(final_kernel, count, spans, rows),
            out_shape=pltpu.HBM((spans, half, slab), jnp.float32),
            in_specs=[vmem, vmem, hbm],
            out_specs=hbm,
            scratch_shapes=[pltpu.VMEM((spans * rows, slab), jnp.float32), pltpu.SemaphoreType.DMA((spans,))],
            compiler_params=params,
            input_output_aliases={2: 0},
            name="final",
        )(last, lax.ppermute(last, "cd", swap), base)

    in_specs = (
        P("groups", "ab", "cd"),
        P(("groups", "ab"), "cd"),
        P(("groups", "ab")),
        P(("groups", "cd")),
        P(("groups", "ab"), "cd"),
    )
    out_specs = P("groups", "cd", "ab")
    return jax.shard_map(shards, mesh=mesh, in_specs=in_specs, out_specs=out_specs, check_vma=False)
```

```python
import functools

import jax
import jax.numpy as jnp
from jax import lax
from jax.experimental import pallas as pl
from jax.experimental.pallas import tpu as pltpu
from jax.sharding import PartitionSpec as P

TILE = 128
UNROLL = 4
LANES = 128
FLIGHT = 32
GROUP = 12
STEP_FLOPS = 1 << 30
VMEM_LIMIT = 12 * 2**20


def grid_of(count):
    bits = count.bit_length() - 1
    if count != 1 << bits or bits < 2:
        return count, 1
    rows = 1 << ((bits + 1) // 2)
    return rows, count // rows


def at_ring(place, rows, columns):
    if columns == 1:
        return place
    wide = columns - 1
    beyond = place - rows
    line = beyond // wide
    step = beyond - line * wide
    even = (line % 2) == 0
    if isinstance(place, int):
        back = (rows - 1 - line) * columns + (1 + step if even else columns - 1 - step)
        return place * columns if place < rows else back
    back = (rows - 1 - line) * columns + jnp.where(even, 1 + step, columns - 1 - step)
    return jnp.where(place < rows, place * columns, back)


def ring_of(index, rows, columns):
    if columns == 1:
        return index
    wide = columns - 1
    row = index // columns
    column = index - row * columns
    line = rows - 1 - row
    step = jnp.where((line % 2) == 0, column - 1, columns - 1 - column)
    return jnp.where(column == 0, row, rows + line * wide + step)


def place_of(count, rows, offset):
    grid = grid_of(count)
    here = ring_of(lax.axis_index("ab"), *grid)
    whole = rows * count
    start = at_ring((here + offset + count) % count, *grid) * rows + lax.axis_index("cd") * (whole // 2)
    return jnp.where(start >= whole, start - whole, start)


def cut_kernel(chunk, *spans):
    for at, span in enumerate(spans):
        span[0] = chunk[at]


def list_kernel(ab_tiles, cd_tiles, ab_irrep, cd_irrep, pattern, amplitudes, listed, own, own_sem):
    copy = pltpu.make_async_copy(amplitudes, own, own_sem)
    copy.start()
    shape = (ab_tiles, LANES)
    lane = lax.broadcasted_iota(jnp.int32, shape, 1)
    line = lax.broadcasted_iota(jnp.int32, shape, 0)
    rows = jnp.full(shape, -1, jnp.int32)
    columns = jnp.full(shape, -2, jnp.int32)
    for p in range(ab_tiles):
        rows = jnp.where(line == p, ab_irrep[p], rows)
    for q in range(cd_tiles):
        columns = jnp.where(lane == q, cd_irrep[q], columns)
    stored = jnp.concatenate([pattern[...], jnp.zeros((ab_tiles, LANES - cd_tiles), jnp.int32)], axis=1)
    keep = jnp.where(jnp.logical_and(stored == 1, rows == columns), 1.0, 0.0)

    upto = keep
    reach = 1
    while reach < cd_tiles:
        upto += jnp.where(lane >= reach, pltpu.roll(upto, reach, 1), 0.0)
        reach *= 2
    whole = jnp.broadcast_to(jnp.sum(keep, axis=1, keepdims=True), shape)
    before = whole
    reach = 1
    while reach < ab_tiles:
        before += jnp.where(line >= reach, pltpu.roll(before, reach, 0), 0.0)
        reach *= 2
    found = before[ab_tiles - 1 :, :]
    upto += before - whole

    turned = upto.T
    order = lax.broadcasted_iota(jnp.int32, (cd_tiles, LANES), 1).astype(jnp.float32)
    passed = jnp.zeros((cd_tiles, LANES), jnp.float32)
    for p in range(ab_tiles):
        passed += jnp.where(turned[:cd_tiles, p : p + 1] <= order, 1.0, 0.0)
    places = jnp.sum(passed, axis=0, keepdims=True)
    listed[0:1, :] = jnp.where(order[0:1, :] < found, places, 0.0).astype(jnp.int32)
    listed[1:2, :] = ((found + (UNROLL - 1)) * (1.0 / UNROLL)).astype(jnp.int32)
    copy.wait()


def part_kernel(cd_tiles, listed, integrals, split, landed, sems):
    last = listed[1, 0] * UNROLL

    def fetch(k):
        start, column = place_in(listed[0, k], cd_tiles)
        slot = lax.rem(k, FLIGHT)
        return pltpu.make_async_copy(
            integrals.at[pl.ds(start, TILE), pl.ds(column, TILE)], landed.at[slot], sems.at[slot]
        )

    def begin(k, carry):
        fetch(k).start()
        return carry

    lax.fori_loop(0, jnp.minimum(last, FLIGHT), begin, 0)

    def part(round_at, carry):
        first = round_at * UNROLL
        for unrolled in range(UNROLL):
            fetch(first + unrolled).wait()
        for unrolled in range(UNROLL):
            k = first + unrolled
            real = jnp.logical_or(k == 0, listed[0, k] > 0)
            tile = jnp.where(real, landed[lax.rem(k, FLIGHT)], 0.0).T
            upper = tile.astype(jnp.bfloat16)
            split[k, :, :TILE] = upper
            split[k, :, TILE:] = (tile - upper.astype(jnp.float32)).astype(jnp.bfloat16)
        lax.fori_loop(jnp.minimum(first + FLIGHT, last), jnp.minimum(first + UNROLL + FLIGHT, last), begin, 0)
        return carry

    lax.fori_loop(0, listed[1, 0], part, 0)


def place_in(place, cd_tiles):
    row = lax.div(place, cd_tiles)
    return pl.multiple_of(row * TILE, TILE), pl.multiple_of((place - row * cd_tiles) * TILE, TILE)


def products(cd_tiles, listed, split, pieces, total):
    total[...] = jnp.zeros_like(total)

    def some(first, many):
        sums = []
        for unrolled in range(many):
            start, column = place_in(listed[0, first + unrolled], cd_tiles)
            rows = [piece[span, :, pl.ds(column, TILE)] for piece in pieces for span in range(piece.shape[0])]
            left = jnp.concatenate(rows, axis=0)
            upper = left.astype(jnp.bfloat16)
            lower = (left - upper.astype(jnp.float32)).astype(jnp.bfloat16)
            tile = split[first + unrolled]
            both = jnp.dot(jnp.concatenate([upper, lower], axis=0), tile, preferred_element_type=jnp.float32)
            high, low = both[: left.shape[0]], both[left.shape[0] :]
            sums.append((start, high[:, :TILE] + (high[:, TILE:] + (low[:, :TILE] + low[:, TILE:]))))
        for start, term in sums:
            total[:, pl.ds(start, TILE)] += term

    def step(at, carry):
        some(at * 2 * UNROLL, 2 * UNROLL)
        return carry

    rounds = listed[1, 0]
    lax.fori_loop(0, lax.div(rounds, 2), step, 0)

    @pl.when(lax.rem(rounds, 2) == 1)
    def _():
        some((rounds - 1) * UNROLL, UNROLL)


def step_kernel(count, rows, cd_tiles, group, listed, split, *refs):
    pieces = refs[: len(group)]
    mine, send, total = refs[-3:]
    products(cd_tiles, listed, split, pieces, total)
    half = rows * count // 2
    at = 0
    for offset, spans in group:
        place = place_of(count, rows, offset)
        for span in spans:
            block = total[at * rows : (at + 1) * rows, :]
            at += 1

            @pl.when(place < half)
            def _():
                mine[span, pl.ds(pl.multiple_of(place, rows), rows), :] = block

            @pl.when(place >= half)
            def _():
                send[span, pl.ds(pl.multiple_of(place - half, rows), rows), :] = block


def last_kernel(cd_tiles, listed, split, *refs):
    products(cd_tiles, listed, split, refs[:-1], refs[-1])


def merge_kernel(mine, received, out):
    out[...] = mine[...] + received[...]


def final_kernel(count, spans, rows, last, received, before, out, total, sems):
    del before
    place = place_of(count, rows, -(count // 2))

    @pl.when(place < rows * count // 2)
    def _():
        total[...] = last[...] + received[...]
        copies = []
        for span in range(spans):
            copies.append(
                pltpu.make_async_copy(
                    total.at[pl.ds(span * rows, rows), :],
                    out.at[span, pl.ds(pl.multiple_of(place, rows), rows), :],
                    sems.at[span],
                )
            )
            copies[-1].start()
        for copy in copies:
            copy.wait()


def solution(mesh):
    count = mesh.shape["ab"]
    grid = grid_of(count)
    far = count // 2
    ahead = [(at_ring(at, *grid), at_ring((at + 1) % count, *grid)) for at in range(count)]
    back = [(to, start) for start, to in ahead]
    swap = [(0, 1), (1, 0)]

    def shards(amplitudes, integrals, ab_irrep, cd_irrep, block_pattern):
        spans, rows, depth = amplitudes.shape
        slab = integrals.shape[0]
        ab_tiles, cd_tiles = block_pattern.shape
        tiles = ab_tiles * cd_tiles
        half = rows * far

        in_hbm = functools.partial(pltpu.with_memory_space_constraint, memory_space=pltpu.HBM)
        smem = pl.BlockSpec(memory_space=pltpu.SMEM)
        vmem = pl.BlockSpec(memory_space=pltpu.VMEM)
        hbm = pl.BlockSpec(memory_space=pltpu.HBM)
        params = pltpu.CompilerParams(vmem_limit_bytes=VMEM_LIMIT)
        listed, own = pl.pallas_call(
            functools.partial(list_kernel, ab_tiles, cd_tiles),
            out_shape=(pltpu.VMEM((2, LANES), jnp.int32), pltpu.VMEM(amplitudes.shape, jnp.float32)),
            in_specs=[smem, smem, vmem, hbm],
            out_specs=(vmem, vmem),
            scratch_shapes=[pltpu.SemaphoreType.DMA],
            compiler_params=params,
            cost_estimate=pl.CostEstimate(flops=0, bytes_accessed=4 << 20, transcendentals=0),
            name="list",
        )(*map(in_hbm, (ab_irrep, cd_irrep, block_pattern, amplitudes)))
        split = pl.pallas_call(
            functools.partial(part_kernel, cd_tiles),
            out_shape=pltpu.VMEM((tiles, TILE, 2 * TILE), jnp.bfloat16),
            in_specs=[smem, hbm],
            out_specs=vmem,
            scratch_shapes=[pltpu.VMEM((FLIGHT, TILE, TILE), jnp.float32), pltpu.SemaphoreType.DMA((FLIGHT,))],
            compiler_params=params,
            cost_estimate=pl.CostEstimate(flops=0, bytes_accessed=8 << 20, transcendentals=0),
            name="part",
        )(listed, in_hbm(integrals))

        block = pltpu.VMEM((spans, half, slab), jnp.float32)

        def step(group, parts):
            pieces = [piece for *_, piece in group]
            height = sum(piece.shape[0] for piece in pieces) * rows
            return pl.pallas_call(
                functools.partial(step_kernel, count, rows, cd_tiles, [key for *key, _ in group]),
                out_shape=(block, block),
                in_specs=[smem] + [vmem] * (1 + len(pieces) + len(parts)),
                out_specs=(vmem, vmem),
                scratch_shapes=[pltpu.VMEM((height, slab), jnp.float32)],
                compiler_params=params,
                input_output_aliases={2 + len(pieces): 0, 3 + len(pieces): 1} if parts else {},
                cost_estimate=pl.CostEstimate(flops=STEP_FLOPS, bytes_accessed=4 << 20, transcendentals=0),
                name="step",
            )(listed, split, *pieces, *parts)

        both = tuple(range(spans))
        ways = ((ahead, -1), (back, 1))
        parts = step([(0, both, own)], ())
        arrivals, moving = [], {}
        for way, (pairs, sign) in enumerate(ways):
            chunk, _ = lax.optimization_barrier((lax.ppermute(amplitudes, "ab", pairs), parts[0]))
            arrivals.append((sign, both, chunk))
            cut = pl.pallas_call(
                cut_kernel,
                out_shape=(pltpu.VMEM((1, rows, depth), jnp.float32),) * spans,
                in_specs=[vmem],
                out_specs=(vmem,) * spans,
                compiler_params=params,
                name="cut",
            )(chunk)
            moving.update({(way, span): cut[span] for span in both})
        order = [(way, span) for short in (False, True) for way in range(2) for span in both if (span % 2 != way) == short]
        final = {}
        for hop in range(2, far + 1):
            for way, span in order:
                if hop < far or span % 2 == way:
                    pairs, sign = ways[way]
                    moving[way, span] = lax.ppermute(moving[way, span], "ab", pairs)
                    if hop < far:
                        arrivals.append((sign * hop, (span,), moving[way, span]))
                    else:
                        final[span] = moving[way, span]
        short = len(arrivals) - spans
        cuts = sorted({*range(0, short, GROUP), short, len(arrivals)})
        for start, stop in zip(cuts, cuts[1:]):
            parts = step(arrivals[start:stop], parts)
        mine, send = parts
        base = pl.pallas_call(
            merge_kernel,
            out_shape=pltpu.HBM((spans, half, slab), jnp.float32),
            in_specs=[vmem, vmem],
            out_specs=vmem,
            compiler_params=params,
            name="merge",
        )(mine, lax.ppermute(send, "cd", swap))

        last = pl.pallas_call(
            functools.partial(last_kernel, cd_tiles),
            out_shape=pltpu.VMEM((spans * rows, slab), jnp.float32),
            in_specs=[smem, vmem] + [vmem] * spans,
            out_specs=vmem,
            compiler_params=params,
            cost_estimate=pl.CostEstimate(flops=1 << 34, bytes_accessed=4 << 20, transcendentals=0),
            name="last",
        )(listed, split, *[final[span] for span in both])
        return pl.pallas_call(
            functools.partial(final_kernel, count, spans, rows),
            out_shape=pltpu.HBM((spans, half, slab), jnp.float32),
            in_specs=[vmem, vmem, hbm],
            out_specs=hbm,
            scratch_shapes=[pltpu.VMEM((spans * rows, slab), jnp.float32), pltpu.SemaphoreType.DMA((spans,))],
            compiler_params=params,
            input_output_aliases={2: 0},
            name="final",
        )(last, lax.ppermute(last, "cd", swap), base)

    in_specs = (
        P("groups", "ab", "cd"),
        P(("groups", "ab"), "cd"),
        P(("groups", "ab")),
        P(("groups", "cd")),
        P(("groups", "ab"), "cd"),
    )
    out_specs = P("groups", "cd", "ab")
    return jax.shard_map(shards, mesh=mesh, in_specs=in_specs, out_specs=out_specs, check_vma=False)
```

```python
import functools

import jax
import jax.numpy as jnp
from jax import lax
from jax.experimental import pallas as pl
from jax.experimental.pallas import tpu as pltpu
from jax.sharding import PartitionSpec as P

TILE = 128
UNROLL = 4
LANES = 128
FLIGHT = 32
GROUP = 12
STEP_FLOPS = 1 << 30
VMEM_LIMIT = 12 * 2**20


def grid_of(count):
    bits = count.bit_length() - 1
    if count != 1 << bits or bits < 2:
        return count, 1
    rows = 1 << ((bits + 1) // 2)
    return rows, count // rows


def at_ring(place, rows, columns):
    if columns == 1:
        return place
    wide = columns - 1
    beyond = place - rows
    line = beyond // wide
    step = beyond - line * wide
    even = (line % 2) == 0
    if isinstance(place, int):
        back = (rows - 1 - line) * columns + (1 + step if even else columns - 1 - step)
        return place * columns if place < rows else back
    back = (rows - 1 - line) * columns + jnp.where(even, 1 + step, columns - 1 - step)
    return jnp.where(place < rows, place * columns, back)


def ring_of(index, rows, columns):
    if columns == 1:
        return index
    wide = columns - 1
    row = index // columns
    column = index - row * columns
    line = rows - 1 - row
    step = jnp.where((line % 2) == 0, column - 1, columns - 1 - column)
    return jnp.where(column == 0, row, rows + line * wide + step)


def place_of(count, rows, chain, hop):
    grid = grid_of(count)
    here = ring_of(lax.axis_index("ab"), *grid)
    core = lax.axis_index("cd")
    away = (2 * core - 1) * hop if chain == 0 else (1 - 2 * core) * hop
    whole = rows * count
    start = at_ring((here + away + count) % count, *grid) * rows + core * (whole // 2)
    return jnp.where(start >= whole, start - whole, start)


def cut_kernel(spans, chunk, *refs):
    outs, pack = refs[-spans - 1 : -1], refs[-1]
    first = spans if len(refs) > spans + 1 else 0
    for at, out in enumerate(outs):
        out[0] = chunk[at]
        pack[first + at] = chunk[at]


def list_kernel(ab_tiles, cd_tiles, ab_irrep, cd_irrep, pattern, amplitudes, listed, own, own_sem):
    copy = pltpu.make_async_copy(amplitudes, own, own_sem)
    copy.start()
    shape = (ab_tiles, LANES)
    lane = lax.broadcasted_iota(jnp.int32, shape, 1)
    line = lax.broadcasted_iota(jnp.int32, shape, 0)
    rows = jnp.full(shape, -1, jnp.int32)
    columns = jnp.full(shape, -2, jnp.int32)
    for p in range(ab_tiles):
        rows = jnp.where(line == p, ab_irrep[p], rows)
    for q in range(cd_tiles):
        columns = jnp.where(lane == q, cd_irrep[q], columns)
    stored = jnp.concatenate([pattern[...], jnp.zeros((ab_tiles, LANES - cd_tiles), jnp.int32)], axis=1)
    keep = jnp.where(jnp.logical_and(stored == 1, rows == columns), 1.0, 0.0)

    upto = keep
    reach = 1
    while reach < cd_tiles:
        upto += jnp.where(lane >= reach, pltpu.roll(upto, reach, 1), 0.0)
        reach *= 2
    whole = jnp.broadcast_to(jnp.sum(keep, axis=1, keepdims=True), shape)
    before = whole
    reach = 1
    while reach < ab_tiles:
        before += jnp.where(line >= reach, pltpu.roll(before, reach, 0), 0.0)
        reach *= 2
    found = before[ab_tiles - 1 :, :]
    upto += before - whole

    turned = upto.T
    order = lax.broadcasted_iota(jnp.int32, (cd_tiles, LANES), 1).astype(jnp.float32)
    passed = jnp.zeros((cd_tiles, LANES), jnp.float32)
    for p in range(ab_tiles):
        passed += jnp.where(turned[:cd_tiles, p : p + 1] <= order, 1.0, 0.0)
    places = jnp.sum(passed, axis=0, keepdims=True)
    listed[0:1, :] = jnp.where(order[0:1, :] < found, places, 0.0).astype(jnp.int32)
    listed[1:2, :] = ((found + (UNROLL - 1)) * (1.0 / UNROLL)).astype(jnp.int32)
    copy.wait()


def part_kernel(cd_tiles, listed, integrals, split, landed, sems):
    last = listed[1, 0] * UNROLL

    def fetch(k):
        start, column = place_in(listed[0, k], cd_tiles)
        slot = lax.rem(k, FLIGHT)
        return pltpu.make_async_copy(
            integrals.at[pl.ds(start, TILE), pl.ds(column, TILE)], landed.at[slot], sems.at[slot]
        )

    def begin(k, carry):
        fetch(k).start()
        return carry

    lax.fori_loop(0, jnp.minimum(last, FLIGHT), begin, 0)

    def part(round_at, carry):
        first = round_at * UNROLL
        for unrolled in range(UNROLL):
            fetch(first + unrolled).wait()
        for unrolled in range(UNROLL):
            k = first + unrolled
            real = jnp.logical_or(k == 0, listed[0, k] > 0)
            tile = jnp.where(real, landed[lax.rem(k, FLIGHT)], 0.0).T
            upper = tile.astype(jnp.bfloat16)
            split[k, :, :TILE] = upper
            split[k, :, TILE:] = (tile - upper.astype(jnp.float32)).astype(jnp.bfloat16)
        lax.fori_loop(jnp.minimum(first + FLIGHT, last), jnp.minimum(first + UNROLL + FLIGHT, last), begin, 0)
        return carry

    lax.fori_loop(0, listed[1, 0], part, 0)


def place_in(place, cd_tiles):
    row = lax.div(place, cd_tiles)
    return pl.multiple_of(row * TILE, TILE), pl.multiple_of((place - row * cd_tiles) * TILE, TILE)


def products(cd_tiles, listed, split, pieces, total):
    total[...] = jnp.zeros_like(total)

    def some(first, many):
        sums = []
        for unrolled in range(many):
            start, column = place_in(listed[0, first + unrolled], cd_tiles)
            rows = [piece[span, :, pl.ds(column, TILE)] for piece in pieces for span in range(piece.shape[0])]
            left = jnp.concatenate(rows, axis=0)
            upper = left.astype(jnp.bfloat16)
            lower = (left - upper.astype(jnp.float32)).astype(jnp.bfloat16)
            tile = split[first + unrolled]
            both = jnp.dot(jnp.concatenate([upper, lower], axis=0), tile, preferred_element_type=jnp.float32)
            high, low = both[: left.shape[0]], both[left.shape[0] :]
            sums.append((start, high[:, :TILE] + (high[:, TILE:] + (low[:, :TILE] + low[:, TILE:]))))
        for start, term in sums:
            total[:, pl.ds(start, TILE)] += term

    def step(at, carry):
        some(at * 2 * UNROLL, 2 * UNROLL)
        return carry

    rounds = listed[1, 0]
    lax.fori_loop(0, lax.div(rounds, 2), step, 0)

    @pl.when(lax.rem(rounds, 2) == 1)
    def _():
        some((rounds - 1) * UNROLL, UNROLL)


def step_kernel(count, rows, cd_tiles, group, many, listed, split, *refs):
    pieces = refs[:many]
    mine, send, total = refs[-3:]
    products(cd_tiles, listed, split, pieces, total)
    half = rows * count // 2
    at = 0
    for chain, hop, spans in group:
        place = place_of(count, rows, chain, hop)
        for span in spans:
            block = total[at * rows : (at + 1) * rows, :]
            at += 1

            @pl.when(place < half)
            def _():
                mine[span, pl.ds(pl.multiple_of(place, rows), rows), :] = block

            @pl.when(place >= half)
            def _():
                send[span, pl.ds(pl.multiple_of(place - half, rows), rows), :] = block


def last_kernel(cd_tiles, listed, split, *refs):
    products(cd_tiles, listed, split, refs[:-1], refs[-1])


def merge_kernel(mine, received, out):
    out[...] = mine[...] + received[...]


def final_kernel(count, spans, rows, last, received, before, out, total, sems):
    del before
    place = place_of(count, rows, 0, count // 2)

    @pl.when(place < rows * count // 2)
    def _():
        total[...] = last[...] + received[...]
        copies = []
        for span in range(spans):
            copies.append(
                pltpu.make_async_copy(
                    total.at[pl.ds(span * rows, rows), :],
                    out.at[span, pl.ds(pl.multiple_of(place, rows), rows), :],
                    sems.at[span],
                )
            )
            copies[-1].start()
        for copy in copies:
            copy.wait()


def solution(mesh):
    count = mesh.shape["ab"]
    cores = mesh.shape["cd"]
    grid = grid_of(count)
    far = count // 2

    def around(chain, before, after):
        pairs = []
        for at in range(count):
            for half in range(cores):
                to = at + 1 if half == chain else at + count - 1
                start, end = at_ring(at, *grid), at_ring(to % count, *grid)
                pairs.append((start * cores + (half + before) % cores, end * cores + (half + after) % cores))
        return pairs

    swap = [(0, 1), (1, 0)]

    def shards(amplitudes, integrals, ab_irrep, cd_irrep, block_pattern):
        spans, rows, depth = amplitudes.shape
        slab = integrals.shape[0]
        ab_tiles, cd_tiles = block_pattern.shape
        tiles = ab_tiles * cd_tiles
        half = rows * far

        in_hbm = functools.partial(pltpu.with_memory_space_constraint, memory_space=pltpu.HBM)
        smem = pl.BlockSpec(memory_space=pltpu.SMEM)
        vmem = pl.BlockSpec(memory_space=pltpu.VMEM)
        hbm = pl.BlockSpec(memory_space=pltpu.HBM)
        params = pltpu.CompilerParams(vmem_limit_bytes=VMEM_LIMIT)
        listed, own = pl.pallas_call(
            functools.partial(list_kernel, ab_tiles, cd_tiles),
            out_shape=(pltpu.VMEM((2, LANES), jnp.int32), pltpu.VMEM(amplitudes.shape, jnp.float32)),
            in_specs=[smem, smem, vmem, hbm],
            out_specs=(vmem, vmem),
            scratch_shapes=[pltpu.SemaphoreType.DMA],
            compiler_params=params,
            cost_estimate=pl.CostEstimate(flops=0, bytes_accessed=4 << 20, transcendentals=0),
            name="list",
        )(*map(in_hbm, (ab_irrep, cd_irrep, block_pattern, amplitudes)))
        split = pl.pallas_call(
            functools.partial(part_kernel, cd_tiles),
            out_shape=pltpu.VMEM((tiles, TILE, 2 * TILE), jnp.bfloat16),
            in_specs=[smem, hbm],
            out_specs=vmem,
            scratch_shapes=[pltpu.VMEM((FLIGHT, TILE, TILE), jnp.float32), pltpu.SemaphoreType.DMA((FLIGHT,))],
            compiler_params=params,
            cost_estimate=pl.CostEstimate(flops=0, bytes_accessed=8 << 20, transcendentals=0),
            name="part",
        )(listed, in_hbm(integrals))

        block = pltpu.VMEM((spans, half, slab), jnp.float32)

        def step(group, parts):
            pieces = [piece for *_, piece in group if piece is not None]
            height = sum(piece.shape[0] for piece in pieces) * rows
            return pl.pallas_call(
                functools.partial(step_kernel, count, rows, cd_tiles, [key for *key, _ in group], len(pieces)),
                out_shape=(block, block),
                in_specs=[smem] + [vmem] * (1 + len(pieces) + len(parts)),
                out_specs=(vmem, vmem),
                scratch_shapes=[pltpu.VMEM((height, slab), jnp.float32)],
                compiler_params=params,
                input_output_aliases={2 + len(pieces): 0, 3 + len(pieces): 1} if parts else {},
                cost_estimate=pl.CostEstimate(flops=STEP_FLOPS, bytes_accessed=4 << 20, transcendentals=0),
                name="step",
            )(listed, split, *pieces, *parts)

        def send_on(piece, chain, hop):
            return lax.ppermute(piece, ("ab", "cd"), around(chain, min(hop - 1, 2), min(hop, 2)))

        both = tuple(range(spans))
        parts = step([(0, 0, both, own)], ())
        pack, moving = (), {}
        for chain in range(2):
            chunk, _ = lax.optimization_barrier((send_on(amplitudes, chain, 1), parts[0]))
            *cut, packed = pl.pallas_call(
                functools.partial(cut_kernel, spans),
                out_shape=(pltpu.VMEM((1, rows, depth), jnp.float32),) * spans
                + (pltpu.VMEM((2 * spans, rows, depth), jnp.float32),),
                in_specs=[vmem] * (1 + len(pack)),
                out_specs=(vmem,) * (spans + 1),
                compiler_params=params,
                input_output_aliases={1: spans} if pack else {},
                name="cut",
            )(chunk, *pack)
            pack = (packed,)
            moving.update({(chain, span): cut[span] for span in both})
        order = [(chain, span) for long in (True, False) for chain in range(2) for span in both if (span % 2 == chain) == long]
        arrivals, over, final = [], [], {}
        for hop in range(2, far + 1):
            for chain, span in order:
                if hop < far or span % 2 == chain:
                    moving[chain, span] = send_on(moving[chain, span], chain, hop)
                    if hop < far:
                        arrivals.append((chain, hop, (span,), moving[chain, span]))
                    else:
                        final[span] = moving[chain, span]
            if hop == 2:
                packed = lax.ppermute(packed, "cd", swap)
                over += [(0, 1, both, packed), (1, 1, both, None)]
        late = len(arrivals) - spans
        arrivals += over
        cuts = sorted({*range(0, late, GROUP), late, len(arrivals)})
        for start, stop in zip(cuts, cuts[1:]):
            parts = step(arrivals[start:stop], parts)
        mine, send = parts
        base = pl.pallas_call(
            merge_kernel,
            out_shape=pltpu.HBM((spans, half, slab), jnp.float32),
            in_specs=[vmem, vmem],
            out_specs=vmem,
            compiler_params=params,
            name="merge",
        )(mine, lax.ppermute(send, "cd", swap))

        last = pl.pallas_call(
            functools.partial(last_kernel, cd_tiles),
            out_shape=pltpu.VMEM((spans * rows, slab), jnp.float32),
            in_specs=[smem, vmem] + [vmem] * spans,
            out_specs=vmem,
            compiler_params=params,
            cost_estimate=pl.CostEstimate(flops=1 << 34, bytes_accessed=4 << 20, transcendentals=0),
            name="last",
        )(listed, split, *[final[span] for span in both])
        return pl.pallas_call(
            functools.partial(final_kernel, count, spans, rows),
            out_shape=pltpu.HBM((spans, half, slab), jnp.float32),
            in_specs=[vmem, vmem, hbm],
            out_specs=hbm,
            scratch_shapes=[pltpu.VMEM((spans * rows, slab), jnp.float32), pltpu.SemaphoreType.DMA((spans,))],
            compiler_params=params,
            input_output_aliases={2: 0},
            name="final",
        )(last, lax.ppermute(last, "cd", swap), base)

    in_specs = (
        P("groups", "ab", "cd"),
        P(("groups", "ab"), "cd"),
        P(("groups", "ab")),
        P(("groups", "cd")),
        P(("groups", "ab"), "cd"),
    )
    out_specs = P("groups", "cd", "ab")
    return jax.shard_map(shards, mesh=mesh, in_specs=in_specs, out_specs=out_specs, check_vma=False)
```

```python
import functools

import jax
import jax.numpy as jnp
from jax import lax
from jax.experimental import pallas as pl
from jax.experimental.pallas import tpu as pltpu
from jax.sharding import PartitionSpec as P

TILE = 128
UNROLL = 4
LANES = 128
FLIGHT = 32
GROUP = 12
STEP_FLOPS = 1 << 30
VMEM_LIMIT = 12 * 2**20


def grid_of(count):
    bits = count.bit_length() - 1
    if count != 1 << bits or bits < 2:
        return count, 1
    rows = 1 << ((bits + 1) // 2)
    return rows, count // rows


def at_ring(place, rows, columns):
    if columns == 1:
        return place
    wide = columns - 1
    beyond = place - rows
    line = beyond // wide
    step = beyond - line * wide
    even = (line % 2) == 0
    if isinstance(place, int):
        back = (rows - 1 - line) * columns + (1 + step if even else columns - 1 - step)
        return place * columns if place < rows else back
    back = (rows - 1 - line) * columns + jnp.where(even, 1 + step, columns - 1 - step)
    return jnp.where(place < rows, place * columns, back)


def ring_of(index, rows, columns):
    if columns == 1:
        return index
    wide = columns - 1
    row = index // columns
    column = index - row * columns
    line = rows - 1 - row
    step = jnp.where((line % 2) == 0, column - 1, columns - 1 - column)
    return jnp.where(column == 0, row, rows + line * wide + step)


def place_of(count, rows, chain, hop):
    grid = grid_of(count)
    here = ring_of(lax.axis_index("ab"), *grid)
    core = lax.axis_index("cd")
    away = (2 * core - 1) * hop if chain == 0 else (1 - 2 * core) * hop
    whole = rows * count
    start = at_ring((here + away + count) % count, *grid) * rows + core * (whole // 2)
    return jnp.where(start >= whole, start - whole, start)


def cut_kernel(spans, chunk, *refs):
    outs, pack = refs[-spans - 1 : -1], refs[-1]
    first = spans if len(refs) > spans + 1 else 0
    for at, out in enumerate(outs):
        out[0] = chunk[at]
        pack[first + at] = chunk[at]


def list_kernel(ab_tiles, cd_tiles, ab_irrep, cd_irrep, pattern, amplitudes, listed, own, own_sem):
    copy = pltpu.make_async_copy(amplitudes, own, own_sem)
    copy.start()
    shape = (ab_tiles, LANES)
    lane = lax.broadcasted_iota(jnp.int32, shape, 1)
    line = lax.broadcasted_iota(jnp.int32, shape, 0)
    rows = jnp.full(shape, -1, jnp.int32)
    columns = jnp.full(shape, -2, jnp.int32)
    for p in range(ab_tiles):
        rows = jnp.where(line == p, ab_irrep[p], rows)
    for q in range(cd_tiles):
        columns = jnp.where(lane == q, cd_irrep[q], columns)
    stored = jnp.concatenate([pattern[...], jnp.zeros((ab_tiles, LANES - cd_tiles), jnp.int32)], axis=1)
    keep = jnp.where(jnp.logical_and(stored == 1, rows == columns), 1.0, 0.0)

    upto = keep
    reach = 1
    while reach < cd_tiles:
        upto += jnp.where(lane >= reach, pltpu.roll(upto, reach, 1), 0.0)
        reach *= 2
    whole = jnp.broadcast_to(jnp.sum(keep, axis=1, keepdims=True), shape)
    before = whole
    reach = 1
    while reach < ab_tiles:
        before += jnp.where(line >= reach, pltpu.roll(before, reach, 0), 0.0)
        reach *= 2
    found = before[ab_tiles - 1 :, :]
    upto += before - whole

    turned = upto.T
    order = lax.broadcasted_iota(jnp.int32, (cd_tiles, LANES), 1).astype(jnp.float32)
    passed = jnp.zeros((cd_tiles, LANES), jnp.float32)
    for p in range(ab_tiles):
        passed += jnp.where(turned[:cd_tiles, p : p + 1] <= order, 1.0, 0.0)
    places = jnp.sum(passed, axis=0, keepdims=True)
    listed[0:1, :] = jnp.where(order[0:1, :] < found, places, 0.0).astype(jnp.int32)
    listed[1:2, :] = ((found + (UNROLL - 1)) * (1.0 / UNROLL)).astype(jnp.int32)
    copy.wait()


def part_kernel(cd_tiles, listed, integrals, split, landed, sems):
    last = listed[1, 0] * UNROLL

    def fetch(k):
        start, column = place_in(listed[0, k], cd_tiles)
        slot = lax.rem(k, FLIGHT)
        return pltpu.make_async_copy(
            integrals.at[pl.ds(start, TILE), pl.ds(column, TILE)], landed.at[slot], sems.at[slot]
        )

    def begin(k, carry):
        fetch(k).start()
        return carry

    lax.fori_loop(0, jnp.minimum(last, FLIGHT), begin, 0)

    def part(round_at, carry):
        first = round_at * UNROLL
        for unrolled in range(UNROLL):
            fetch(first + unrolled).wait()
        for unrolled in range(UNROLL):
            k = first + unrolled
            real = jnp.logical_or(k == 0, listed[0, k] > 0)
            tile = jnp.where(real, landed[lax.rem(k, FLIGHT)], 0.0).T
            upper = tile.astype(jnp.bfloat16)
            split[k, :, :TILE] = upper
            split[k, :, TILE:] = (tile - upper.astype(jnp.float32)).astype(jnp.bfloat16)
        lax.fori_loop(jnp.minimum(first + FLIGHT, last), jnp.minimum(first + UNROLL + FLIGHT, last), begin, 0)
        return carry

    lax.fori_loop(0, listed[1, 0], part, 0)


def place_in(place, cd_tiles):
    row = lax.div(place, cd_tiles)
    return pl.multiple_of(row * TILE, TILE), pl.multiple_of((place - row * cd_tiles) * TILE, TILE)


def products(cd_tiles, listed, split, pieces, total):
    total[...] = jnp.zeros_like(total)

    def some(first, many):
        sums = []
        for unrolled in range(many):
            start, column = place_in(listed[0, first + unrolled], cd_tiles)
            rows = [piece[span, :, pl.ds(column, TILE)] for piece in pieces for span in range(piece.shape[0])]
            left = jnp.concatenate(rows, axis=0)
            upper = left.astype(jnp.bfloat16)
            lower = (left - upper.astype(jnp.float32)).astype(jnp.bfloat16)
            tile = split[first + unrolled]
            both = jnp.dot(jnp.concatenate([upper, lower], axis=0), tile, preferred_element_type=jnp.float32)
            high, low = both[: left.shape[0]], both[left.shape[0] :]
            sums.append((start, high[:, :TILE] + (high[:, TILE:] + (low[:, :TILE] + low[:, TILE:]))))
        for start, term in sums:
            total[:, pl.ds(start, TILE)] += term

    def step(at, carry):
        some(at * 2 * UNROLL, 2 * UNROLL)
        return carry

    rounds = listed[1, 0]
    lax.fori_loop(0, lax.div(rounds, 2), step, 0)

    @pl.when(lax.rem(rounds, 2) == 1)
    def _():
        some((rounds - 1) * UNROLL, UNROLL)


def step_kernel(count, rows, cd_tiles, group, many, listed, split, *refs):
    pieces = refs[:many]
    mine, send, total = refs[-3:]
    if len(refs) == many + 3:
        mine[...] = jnp.zeros_like(mine)
        send[...] = jnp.zeros_like(send)
    products(cd_tiles, listed, split, pieces, total)
    half = rows * count // 2
    at = 0
    for chain, hop, spans in group:
        place = place_of(count, rows, chain, hop)
        for span in spans:
            block = total[at * rows : (at + 1) * rows, :]
            at += 1

            @pl.when(place < half)
            def _():
                mine[span, pl.ds(pl.multiple_of(place, rows), rows), :] = block

            @pl.when(place >= half)
            def _():
                send[span, pl.ds(pl.multiple_of(place - half, rows), rows), :] = block


def last_kernel(cd_tiles, listed, split, *refs):
    products(cd_tiles, listed, split, refs[:-1], refs[-1])


def merge_kernel(mine, received, base, out):
    base[...] = mine[...] + received[...]
    out[...] = base[...]


def final_kernel(count, rows, keys, last, received, base, before, out, total, sems):
    del before
    far = count // 2
    half = rows * far

    def block(at):
        return pl.ds(at * rows, rows)

    def put(slot, key_hop, chain, span, value):
        place = place_of(count, rows, chain, key_hop)

        def to():
            return out.at[span, pl.ds(pl.multiple_of(place, rows), rows), :]

        copy = pltpu.make_async_copy(total.at[block(slot), :], to(), sems.at[slot])

        @pl.when(place < half)
        def _():
            rest = base[span, pl.ds(pl.multiple_of(place, rows), rows), :]
            total[block(slot), :] = rest + value()
            copy.start()

        return place < half, copy

    copies = []
    for at, (chain, hop, span) in enumerate(keys):
        if hop == far:
            copies.append(put(len(copies), hop, chain, span, lambda at=at: last[block(at), :] + received[block(at), :]))
        else:
            copies.append(put(len(copies), hop, chain, span, lambda at=at: last[block(at), :]))
            copies.append(put(len(copies), hop, 1 - chain, span, lambda at=at: received[block(at), :]))
    for here, copy in copies:

        @pl.when(here)
        def _():
            copy.wait()


def solution(mesh):
    count = mesh.shape["ab"]
    cores = mesh.shape["cd"]
    grid = grid_of(count)
    far = count // 2

    def around(chain, before, after):
        pairs = []
        for at in range(count):
            for half in range(cores):
                to = at + 1 if half == chain else at + count - 1
                start, end = at_ring(at, *grid), at_ring(to % count, *grid)
                pairs.append((start * cores + (half + before) % cores, end * cores + (half + after) % cores))
        return pairs

    swap = [(0, 1), (1, 0)]

    def shards(amplitudes, integrals, ab_irrep, cd_irrep, block_pattern):
        spans, rows, depth = amplitudes.shape
        slab = integrals.shape[0]
        ab_tiles, cd_tiles = block_pattern.shape
        tiles = ab_tiles * cd_tiles
        half = rows * far

        in_hbm = functools.partial(pltpu.with_memory_space_constraint, memory_space=pltpu.HBM)
        smem = pl.BlockSpec(memory_space=pltpu.SMEM)
        vmem = pl.BlockSpec(memory_space=pltpu.VMEM)
        hbm = pl.BlockSpec(memory_space=pltpu.HBM)
        params = pltpu.CompilerParams(vmem_limit_bytes=VMEM_LIMIT)
        listed, own = pl.pallas_call(
            functools.partial(list_kernel, ab_tiles, cd_tiles),
            out_shape=(pltpu.VMEM((2, LANES), jnp.int32), pltpu.VMEM(amplitudes.shape, jnp.float32)),
            in_specs=[smem, smem, vmem, hbm],
            out_specs=(vmem, vmem),
            scratch_shapes=[pltpu.SemaphoreType.DMA],
            compiler_params=params,
            cost_estimate=pl.CostEstimate(flops=0, bytes_accessed=4 << 20, transcendentals=0),
            name="list",
        )(*map(in_hbm, (ab_irrep, cd_irrep, block_pattern, amplitudes)))
        split = pl.pallas_call(
            functools.partial(part_kernel, cd_tiles),
            out_shape=pltpu.VMEM((tiles, TILE, 2 * TILE), jnp.bfloat16),
            in_specs=[smem, hbm],
            out_specs=vmem,
            scratch_shapes=[pltpu.VMEM((FLIGHT, TILE, TILE), jnp.float32), pltpu.SemaphoreType.DMA((FLIGHT,))],
            compiler_params=params,
            cost_estimate=pl.CostEstimate(flops=0, bytes_accessed=8 << 20, transcendentals=0),
            name="part",
        )(listed, in_hbm(integrals))

        block = pltpu.VMEM((spans, half, slab), jnp.float32)

        def step(group, parts):
            pieces = [piece for *_, piece in group if piece is not None]
            height = sum(piece.shape[0] for piece in pieces) * rows
            return pl.pallas_call(
                functools.partial(step_kernel, count, rows, cd_tiles, [key for *key, _ in group], len(pieces)),
                out_shape=(block, block),
                in_specs=[smem] + [vmem] * (1 + len(pieces) + len(parts)),
                out_specs=(vmem, vmem),
                scratch_shapes=[pltpu.VMEM((height, slab), jnp.float32)],
                compiler_params=params,
                input_output_aliases={2 + len(pieces): 0, 3 + len(pieces): 1} if parts else {},
                cost_estimate=pl.CostEstimate(flops=STEP_FLOPS, bytes_accessed=4 << 20, transcendentals=0),
                name="step",
            )(listed, split, *pieces, *parts)

        def send_on(piece, chain, hop):
            return lax.ppermute(piece, ("ab", "cd"), around(chain, min(hop - 1, 2), min(hop, 2)))

        both = tuple(range(spans))
        parts = step([(0, 0, both, own)], ())
        pack, moving = (), {}
        for chain in range(2):
            chunk, _ = lax.optimization_barrier((send_on(amplitudes, chain, 1), parts[0]))
            *cut, packed = pl.pallas_call(
                functools.partial(cut_kernel, spans),
                out_shape=(pltpu.VMEM((1, rows, depth), jnp.float32),) * spans
                + (pltpu.VMEM((2 * spans, rows, depth), jnp.float32),),
                in_specs=[vmem] * (1 + len(pack)),
                out_specs=(vmem,) * (spans + 1),
                compiler_params=params,
                input_output_aliases={1: spans} if pack else {},
                name="cut",
            )(chunk, *pack)
            pack = (packed,)
            moving.update({(chain, span): cut[span] for span in both})
        order = [(chain, span) for long in (True, False) for chain in range(2) for span in both if (span % 2 == chain) == long]
        arrivals, closing = [], []
        for hop in range(2, far + 1):
            for chain, span in order:
                long = span % 2 == chain
                if hop < far or long:
                    piece = moving[chain, span] = send_on(moving[chain, span], chain, hop)
                    ends = hop == far or (hop == far - 1 and not long)
                    (closing if ends else arrivals).append((chain, hop, (span,), piece))
            if hop == 2:
                packed = lax.ppermute(packed, "cd", swap)
                arrivals += [(0, 1, both, packed), (1, 1, both, None)]
        for start in range(0, len(arrivals), GROUP):
            parts = step(arrivals[start : start + GROUP], parts)
        mine, send = parts
        base, out = pl.pallas_call(
            merge_kernel,
            out_shape=(
                pltpu.VMEM((spans, half, slab), jnp.float32),
                pltpu.HBM((spans, half, slab), jnp.float32),
            ),
            in_specs=[vmem, vmem],
            out_specs=(vmem, vmem),
            compiler_params=params,
            name="merge",
        )(mine, lax.ppermute(send, "cd", swap))

        keys = [(chain, hop, some[0]) for chain, hop, some, _ in closing]
        last = pl.pallas_call(
            functools.partial(last_kernel, cd_tiles),
            out_shape=pltpu.VMEM((len(keys) * rows, slab), jnp.float32),
            in_specs=[smem, vmem] + [vmem] * len(keys),
            out_specs=vmem,
            compiler_params=params,
            cost_estimate=pl.CostEstimate(flops=1 << 34, bytes_accessed=4 << 20, transcendentals=0),
            name="last",
        )(listed, split, *[piece for *_, piece in closing])
        blocks = sum(1 if hop == far else 2 for _, hop, _ in keys)
        return pl.pallas_call(
            functools.partial(final_kernel, count, rows, keys),
            out_shape=pltpu.HBM((spans, half, slab), jnp.float32),
            in_specs=[vmem, vmem, vmem, hbm],
            out_specs=hbm,
            scratch_shapes=[pltpu.VMEM((blocks * rows, slab), jnp.float32), pltpu.SemaphoreType.DMA((blocks,))],
            compiler_params=params,
            input_output_aliases={3: 0},
            name="final",
        )(last, lax.ppermute(last, "cd", swap), base, out)

    in_specs = (
        P("groups", "ab", "cd"),
        P(("groups", "ab"), "cd"),
        P(("groups", "ab")),
        P(("groups", "cd")),
        P(("groups", "ab"), "cd"),
    )
    out_specs = P("groups", "cd", "ab")
    return jax.shard_map(shards, mesh=mesh, in_specs=in_specs, out_specs=out_specs, check_vma=False)
```

```python
import functools

import jax
import jax.numpy as jnp
from jax import lax
from jax.experimental import pallas as pl
from jax.experimental.pallas import tpu as pltpu
from jax.sharding import PartitionSpec as P

TILE = 128
UNROLL = 4
LANES = 128
AHEAD = 8
FLIGHT = AHEAD * UNROLL
GROUP = 12
STEP_FLOPS = 1 << 30
VMEM_LIMIT = 12 * 2**20


def grid_of(count):
    bits = count.bit_length() - 1
    if count != 1 << bits or bits < 2:
        return count, 1
    rows = 1 << ((bits + 1) // 2)
    return rows, count // rows


def at_ring(place, rows, columns):
    if columns == 1:
        return place
    wide = columns - 1
    beyond = place - rows
    line = beyond // wide
    step = beyond - line * wide
    even = (line % 2) == 0
    if isinstance(place, int):
        back = (rows - 1 - line) * columns + (1 + step if even else columns - 1 - step)
        return place * columns if place < rows else back
    back = (rows - 1 - line) * columns + jnp.where(even, 1 + step, columns - 1 - step)
    return jnp.where(place < rows, place * columns, back)


def ring_of(index, rows, columns):
    if columns == 1:
        return index
    wide = columns - 1
    row = index // columns
    column = index - row * columns
    line = rows - 1 - row
    step = jnp.where((line % 2) == 0, column - 1, columns - 1 - column)
    return jnp.where(column == 0, row, rows + line * wide + step)


def place_of(count, rows, offset):
    grid = grid_of(count)
    here = ring_of(lax.axis_index("ab"), *grid)
    whole = rows * count
    start = at_ring((here + offset + count) % count, *grid) * rows + lax.axis_index("cd") * (whole // 2)
    return jnp.where(start >= whole, start - whole, start)


def cut_kernel(amplitudes, pattern, ab_irrep, cd_irrep, *refs):
    *outs, sems = refs
    spans = len(outs) - 3
    pairs = [(amplitudes.at[pl.ds(at, 1)], outs[at]) for at in range(spans)]
    pairs += list(zip((pattern, ab_irrep, cd_irrep), outs[spans:]))
    copies = [pltpu.make_async_copy(start, end, sems.at[at]) for at, (start, end) in enumerate(pairs)]
    for copy in copies:
        copy.start()
    for copy in copies:
        copy.wait()


def list_kernel(ab_tiles, cd_tiles, ab_irrep, cd_irrep, pattern, listed):
    shape = (ab_tiles, LANES)
    lane = lax.broadcasted_iota(jnp.int32, shape, 1)
    line = lax.broadcasted_iota(jnp.int32, shape, 0)
    rows = jnp.full(shape, -1, jnp.int32)
    columns = jnp.full(shape, -2, jnp.int32)
    for p in range(ab_tiles):
        rows = jnp.where(line == p, ab_irrep[p], rows)
    for q in range(cd_tiles):
        columns = jnp.where(lane == q, cd_irrep[q], columns)
    stored = jnp.concatenate([pattern[...], jnp.zeros((ab_tiles, LANES - cd_tiles), jnp.int32)], axis=1)
    keep = jnp.where(jnp.logical_and(stored == 1, rows == columns), 1.0, 0.0)

    upto = keep
    reach = 1
    while reach < cd_tiles:
        upto += jnp.where(lane >= reach, pltpu.roll(upto, reach, 1), 0.0)
        reach *= 2
    whole = jnp.broadcast_to(jnp.sum(keep, axis=1, keepdims=True), shape)
    before = whole
    reach = 1
    while reach < ab_tiles:
        before += jnp.where(line >= reach, pltpu.roll(before, reach, 0), 0.0)
        reach *= 2
    found = before[ab_tiles - 1 :, :]
    upto += before - whole

    turned = upto.T
    order = lax.broadcasted_iota(jnp.int32, (cd_tiles, LANES), 1).astype(jnp.float32)
    passed = jnp.zeros((cd_tiles, LANES), jnp.float32)
    for p in range(ab_tiles):
        passed += jnp.where(turned[:cd_tiles, p : p + 1] <= order, 1.0, 0.0)
    places = jnp.sum(passed, axis=0, keepdims=True)
    listed[0:1, :] = jnp.where(order[0:1, :] < found, places, 0.0).astype(jnp.int32)
    listed[1:2, :] = ((found + (UNROLL - 1)) * (1.0 / UNROLL)).astype(jnp.int32)


def part_kernel(cd_tiles, listed, integrals, split, landed, sems):
    def fetch(k):
        start, column = place_in(listed[0, k], cd_tiles)
        slot = lax.bitwise_and(k, FLIGHT - 1)
        return pltpu.make_async_copy(
            integrals.at[pl.ds(start, TILE), pl.ds(column, TILE)], landed.at[slot], sems.at[slot]
        )

    def begin(round_at, carry):
        for unrolled in range(UNROLL):
            fetch(round_at * UNROLL + unrolled).start()
        return carry

    rounds = listed[1, 0]
    lax.fori_loop(0, jnp.minimum(rounds, AHEAD), begin, 0)

    def part(round_at, carry):
        first = round_at * UNROLL
        for unrolled in range(UNROLL):
            fetch(first + unrolled).wait()
        for unrolled in range(UNROLL):
            k = first + unrolled
            real = jnp.logical_or(k == 0, listed[0, k] > 0)
            tile = jnp.where(real, landed[lax.bitwise_and(k, FLIGHT - 1)], 0.0).T
            upper = tile.astype(jnp.bfloat16)
            split[k, :, :TILE] = upper
            split[k, :, TILE:] = (tile - upper.astype(jnp.float32)).astype(jnp.bfloat16)

        @pl.when(round_at + AHEAD < rounds)
        def _():
            begin(round_at + AHEAD, 0)

        return carry

    lax.fori_loop(0, rounds, part, 0)


def place_in(place, cd_tiles):
    bits = cd_tiles.bit_length() - 1
    if cd_tiles == 1 << bits:
        row, column = lax.shift_right_logical(place, bits), lax.bitwise_and(place, cd_tiles - 1)
    else:
        row, column = lax.div(place, cd_tiles), lax.rem(place, cd_tiles)
    return pl.multiple_of(row * TILE, TILE), pl.multiple_of(column * TILE, TILE)


def products(cd_tiles, listed, split, pieces, total):
    total[...] = jnp.zeros_like(total)

    def some(first, many):
        sums = []
        for unrolled in range(many):
            start, column = place_in(listed[0, first + unrolled], cd_tiles)
            left = jnp.concatenate([piece[0, :, pl.ds(column, TILE)] for piece in pieces], axis=0)
            upper = left.astype(jnp.bfloat16)
            lower = (left - upper.astype(jnp.float32)).astype(jnp.bfloat16)
            tile = split[first + unrolled]
            both = jnp.dot(jnp.concatenate([upper, lower], axis=0), tile, preferred_element_type=jnp.float32)
            high, low = both[: left.shape[0]], both[left.shape[0] :]
            sums.append((start, high[:, :TILE] + (high[:, TILE:] + (low[:, :TILE] + low[:, TILE:]))))
        for start, term in sums:
            total[:, pl.ds(start, TILE)] += term

    def step(at, carry):
        some(at * 2 * UNROLL, 2 * UNROLL)
        return carry

    rounds = listed[1, 0]
    lax.fori_loop(0, lax.shift_right_logical(rounds, 1), step, 0)

    @pl.when(lax.bitwise_and(rounds, 1) == 1)
    def _():
        some((rounds - 1) * UNROLL, UNROLL)


def step_kernel(count, rows, cd_tiles, group, listed, split, *refs):
    pieces = refs[: len(group)]
    mine, send, total = refs[-3:]
    products(cd_tiles, listed, split, pieces, total)
    half = rows * count // 2
    for at, (span, offset) in enumerate(group):
        place = place_of(count, rows, offset)
        block = total[at * rows : (at + 1) * rows, :]

        @pl.when(place < half)
        def _():
            mine[span, pl.ds(pl.multiple_of(place, rows), rows), :] = block

        @pl.when(place >= half)
        def _():
            send[span, pl.ds(pl.multiple_of(place - half, rows), rows), :] = block


def last_kernel(cd_tiles, listed, split, *refs):
    products(cd_tiles, listed, split, refs[:-1], refs[-1])


def merge_kernel(mine, received, out):
    out[...] = mine[...] + received[...]


def final_kernel(count, spans, rows, last, received, before, out, total, sems):
    del before
    place = place_of(count, rows, -(count // 2))

    @pl.when(place < rows * count // 2)
    def _():
        total[...] = last[...] + received[...]
        copies = []
        for span in range(spans):
            copies.append(
                pltpu.make_async_copy(
                    total.at[pl.ds(span * rows, rows), :],
                    out.at[span, pl.ds(pl.multiple_of(place, rows), rows), :],
                    sems.at[span],
                )
            )
            copies[-1].start()
        for copy in copies:
            copy.wait()


def solution(mesh):
    count = mesh.shape["ab"]
    grid = grid_of(count)
    far = count // 2
    ahead = [(at_ring(at, *grid), at_ring((at + 1) % count, *grid)) for at in range(count)]
    back = [(to, start) for start, to in ahead]
    swap = [(0, 1), (1, 0)]

    def shards(amplitudes, integrals, ab_irrep, cd_irrep, block_pattern):
        spans, rows, depth = amplitudes.shape
        slab = integrals.shape[0]
        ab_tiles, cd_tiles = block_pattern.shape
        tiles = ab_tiles * cd_tiles
        half = rows * far

        in_hbm = functools.partial(pltpu.with_memory_space_constraint, memory_space=pltpu.HBM)
        smem = pl.BlockSpec(memory_space=pltpu.SMEM)
        vmem = pl.BlockSpec(memory_space=pltpu.VMEM)
        hbm = pl.BlockSpec(memory_space=pltpu.HBM)
        params = pltpu.CompilerParams(vmem_limit_bytes=VMEM_LIMIT)
        piece = pltpu.VMEM((1, rows, depth), jnp.float32)

        labels = (block_pattern, ab_irrep, cd_irrep)
        *own, near_pattern, near_ab, near_cd = pl.pallas_call(
            cut_kernel,
            out_shape=(piece,) * spans + tuple(pltpu.VMEM(label.shape, label.dtype) for label in labels),
            in_specs=[hbm] * 4,
            out_specs=(vmem,) * (spans + 3),
            scratch_shapes=[pltpu.SemaphoreType.DMA((spans + 3,))],
            compiler_params=params,
            name="cut",
        )(in_hbm(amplitudes), *map(in_hbm, labels))

        listed = pl.pallas_call(
            functools.partial(list_kernel, ab_tiles, cd_tiles),
            out_shape=pltpu.VMEM((2, LANES), jnp.int32),
            in_specs=[smem, smem, vmem],
            out_specs=vmem,
            compiler_params=params,
            cost_estimate=pl.CostEstimate(flops=0, bytes_accessed=4 << 20, transcendentals=0),
            name="list",
        )(near_ab, near_cd, near_pattern)
        split = pl.pallas_call(
            functools.partial(part_kernel, cd_tiles),
            out_shape=pltpu.VMEM((tiles, TILE, 2 * TILE), jnp.bfloat16),
            in_specs=[smem, hbm],
            out_specs=vmem,
            scratch_shapes=[pltpu.VMEM((FLIGHT, TILE, TILE), jnp.float32), pltpu.SemaphoreType.DMA((FLIGHT,))],
            compiler_params=params,
            cost_estimate=pl.CostEstimate(flops=0, bytes_accessed=8 << 20, transcendentals=0),
            name="part",
        )(listed, in_hbm(integrals))

        held = {}
        for span in range(spans):
            held[span, 0] = own[span]
            for pairs, sign in ((ahead, -1), (back, 1)):
                moved = own[span]
                for hop in range(1, far + 1 if (sign < 0) == (span % 2 == 0) else far):
                    if hop in (2, 3):
                        moved, _ = lax.optimization_barrier((moved, listed if hop == 2 else split))
                    moved = lax.ppermute(moved, "ab", pairs)
                    held[span, -far if hop == far else sign * hop] = moved

        def offset_of(span, hop, long):
            return -hop if (span % 2 == 0) == long else hop

        arrivals = [(span, 0) for span in range(spans)]
        for hop in range(1, far):
            arrivals += [(span, offset_of(span, hop, long)) for long in (True, False) for span in range(spans)]
        block = pltpu.VMEM((spans, half, slab), jnp.float32)
        parts = ()
        cuts = sorted({*range(0, len(arrivals) - spans, GROUP), len(arrivals) - spans, len(arrivals)})
        for start, stop in zip(cuts, cuts[1:]):
            group = arrivals[start:stop]
            pieces = [held[key] for key in group]
            parts = pl.pallas_call(
                functools.partial(step_kernel, count, rows, cd_tiles, group),
                out_shape=(block, block),
                in_specs=[smem] + [vmem] * (1 + len(pieces) + len(parts)),
                out_specs=(vmem, vmem),
                scratch_shapes=[pltpu.VMEM((len(pieces) * rows, slab), jnp.float32)],
                compiler_params=params,
                input_output_aliases={2 + len(pieces): 0, 3 + len(pieces): 1} if parts else {},
                cost_estimate=pl.CostEstimate(flops=STEP_FLOPS, bytes_accessed=4 << 20, transcendentals=0),
                name="step",
            )(listed, split, *pieces, *parts)
        mine, send = parts
        base = pl.pallas_call(
            merge_kernel,
            out_shape=pltpu.HBM((spans, half, slab), jnp.float32),
            in_specs=[vmem, vmem],
            out_specs=vmem,
            compiler_params=params,
            name="merge",
        )(mine, lax.ppermute(send, "cd", swap))

        last = pl.pallas_call(
            functools.partial(last_kernel, cd_tiles),
            out_shape=pltpu.VMEM((spans * rows, slab), jnp.float32),
            in_specs=[smem, vmem] + [vmem] * spans,
            out_specs=vmem,
            compiler_params=params,
            cost_estimate=pl.CostEstimate(flops=1 << 34, bytes_accessed=4 << 20, transcendentals=0),
            name="last",
        )(listed, split, *[held[span, -far] for span in range(spans)])
        return pl.pallas_call(
            functools.partial(final_kernel, count, spans, rows),
            out_shape=pltpu.HBM((spans, half, slab), jnp.float32),
            in_specs=[vmem, vmem, hbm],
            out_specs=hbm,
            scratch_shapes=[pltpu.VMEM((spans * rows, slab), jnp.float32), pltpu.SemaphoreType.DMA((spans,))],
            compiler_params=params,
            input_output_aliases={2: 0},
            name="final",
        )(last, lax.ppermute(last, "cd", swap), base)

    in_specs = (
        P("groups", "ab", "cd"),
        P(("groups", "ab"), "cd"),
        P(("groups", "ab")),
        P(("groups", "cd")),
        P(("groups", "ab"), "cd"),
    )
    out_specs = P("groups", "cd", "ab")
    return jax.shard_map(shards, mesh=mesh, in_specs=in_specs, out_specs=out_specs, check_vma=False)
```

```python
import functools

import jax
import jax.numpy as jnp
from jax import lax
from jax.experimental import pallas as pl
from jax.experimental.pallas import tpu as pltpu
from jax.sharding import PartitionSpec as P

TILE = 128
UNROLL = 4
LANES = 128
AHEAD = 8
FLIGHT = AHEAD * UNROLL
GROUP = 12
STEP_FLOPS = 1 << 30
VMEM_LIMIT = 12 * 2**20


def grid_of(count):
    bits = count.bit_length() - 1
    if count != 1 << bits or bits < 2:
        return count, 1
    rows = 1 << ((bits + 1) // 2)
    return rows, count // rows


def at_ring(place, rows, columns):
    if columns == 1:
        return place
    wide = columns - 1
    beyond = place - rows
    line = beyond // wide
    step = beyond - line * wide
    even = (line % 2) == 0
    if isinstance(place, int):
        back = (rows - 1 - line) * columns + (1 + step if even else columns - 1 - step)
        return place * columns if place < rows else back
    back = (rows - 1 - line) * columns + jnp.where(even, 1 + step, columns - 1 - step)
    return jnp.where(place < rows, place * columns, back)


def ring_of(index, rows, columns):
    if columns == 1:
        return index
    wide = columns - 1
    row = index // columns
    column = index - row * columns
    line = rows - 1 - row
    step = jnp.where((line % 2) == 0, column - 1, columns - 1 - column)
    return jnp.where(column == 0, row, rows + line * wide + step)


def place_of(count, rows, offset):
    grid = grid_of(count)
    here = ring_of(lax.axis_index("ab"), *grid)
    whole = rows * count
    start = at_ring((here + offset + count) % count, *grid) * rows + lax.axis_index("cd") * (whole // 2)
    return jnp.where(start >= whole, start - whole, start)


def cut_kernel(amplitudes, pattern, ab_irrep, cd_irrep, *refs):
    *outs, sems = refs
    spans = len(outs) - 3
    pairs = [(amplitudes.at[pl.ds(at, 1)], outs[at]) for at in range(spans)]
    pairs += list(zip((pattern, ab_irrep, cd_irrep), outs[spans:]))
    copies = [pltpu.make_async_copy(start, end, sems.at[at]) for at, (start, end) in enumerate(pairs)]
    for copy in copies:
        copy.start()
    for copy in copies:
        copy.wait()


def list_kernel(ab_tiles, cd_tiles, ab_irrep, cd_irrep, pattern, integrals, listed, landed, near, near_sem, sems):
    shape = (ab_tiles, LANES)
    lane = lax.broadcasted_iota(jnp.int32, shape, 1)
    line = lax.broadcasted_iota(jnp.int32, shape, 0)
    rows = jnp.full(shape, -1, jnp.int32)
    columns = jnp.full(shape, -2, jnp.int32)
    for p in range(ab_tiles):
        rows = jnp.where(line == p, ab_irrep[p], rows)
    for q in range(cd_tiles):
        columns = jnp.where(lane == q, cd_irrep[q], columns)
    stored = jnp.concatenate([pattern[...], jnp.zeros((ab_tiles, LANES - cd_tiles), jnp.int32)], axis=1)
    keep = jnp.where(jnp.logical_and(stored == 1, rows == columns), 1.0, 0.0)

    upto = keep
    reach = 1
    while reach < cd_tiles:
        upto += jnp.where(lane >= reach, pltpu.roll(upto, reach, 1), 0.0)
        reach *= 2
    whole = jnp.broadcast_to(jnp.sum(keep, axis=1, keepdims=True), shape)
    before = whole
    reach = 1
    while reach < ab_tiles:
        before += jnp.where(line >= reach, pltpu.roll(before, reach, 0), 0.0)
        reach *= 2
    found = before[ab_tiles - 1 :, :]
    upto += before - whole

    turned = upto.T
    order = lax.broadcasted_iota(jnp.int32, (cd_tiles, LANES), 1).astype(jnp.float32)
    passed = jnp.zeros((cd_tiles, LANES), jnp.float32)
    for p in range(ab_tiles):
        passed += jnp.where(turned[:cd_tiles, p : p + 1] <= order, 1.0, 0.0)
    places = jnp.sum(passed, axis=0, keepdims=True)
    listed[0:1, :] = jnp.where(order[0:1, :] < found, places, 0.0).astype(jnp.int32)
    listed[1:2, :] = ((found + (UNROLL - 1)) * (1.0 / UNROLL)).astype(jnp.int32)

    copy = pltpu.make_async_copy(listed, near, near_sem)
    copy.start()
    copy.wait()
    rounds = near[1, 0]

    def fetch(k):
        start, column = place_in(near[0, k], cd_tiles)
        return pltpu.make_async_copy(
            integrals.at[pl.ds(start, TILE), pl.ds(column, TILE)],
            landed.at[k],
            sems.at[lax.bitwise_and(k, FLIGHT - 1)],
        )

    def finish(round_at, carry):
        for unrolled in range(UNROLL):
            fetch(round_at * UNROLL + unrolled).wait()
        return carry

    def begin(round_at, carry):
        @pl.when(round_at >= AHEAD)
        def _():
            finish(round_at - AHEAD, 0)

        for unrolled in range(UNROLL):
            fetch(round_at * UNROLL + unrolled).start()
        return carry

    lax.fori_loop(0, rounds, begin, 0)
    lax.fori_loop(jnp.maximum(rounds - AHEAD, 0), rounds, finish, 0)


def part_kernel(listed, landed, split):
    def part(round_at, carry):
        for unrolled in range(UNROLL):
            k = round_at * UNROLL + unrolled
            real = jnp.logical_or(k == 0, listed[0, k] > 0)
            tile = jnp.where(real, landed[k], 0.0).T
            upper = tile.astype(jnp.bfloat16)
            split[k, :, :TILE] = upper
            split[k, :, TILE:] = (tile - upper.astype(jnp.float32)).astype(jnp.bfloat16)
        return carry

    lax.fori_loop(0, listed[1, 0], part, 0)


def place_in(place, cd_tiles):
    bits = cd_tiles.bit_length() - 1
    if cd_tiles == 1 << bits:
        row, column = lax.shift_right_logical(place, bits), lax.bitwise_and(place, cd_tiles - 1)
    else:
        row, column = lax.div(place, cd_tiles), lax.rem(place, cd_tiles)
    return pl.multiple_of(row * TILE, TILE), pl.multiple_of(column * TILE, TILE)


def products(cd_tiles, listed, split, pieces, total):
    total[...] = jnp.zeros_like(total)

    def some(first, many):
        sums = []
        for unrolled in range(many):
            start, column = place_in(listed[0, first + unrolled], cd_tiles)
            left = jnp.concatenate([piece[0, :, pl.ds(column, TILE)] for piece in pieces], axis=0)
            upper = left.astype(jnp.bfloat16)
            lower = (left - upper.astype(jnp.float32)).astype(jnp.bfloat16)
            tile = split[first + unrolled]
            both = jnp.dot(jnp.concatenate([upper, lower], axis=0), tile, preferred_element_type=jnp.float32)
            high, low = both[: left.shape[0]], both[left.shape[0] :]
            sums.append((start, high[:, :TILE] + (high[:, TILE:] + (low[:, :TILE] + low[:, TILE:]))))
        for start, term in sums:
            total[:, pl.ds(start, TILE)] += term

    def step(at, carry):
        some(at * 2 * UNROLL, 2 * UNROLL)
        return carry

    rounds = listed[1, 0]
    lax.fori_loop(0, lax.shift_right_logical(rounds, 1), step, 0)

    @pl.when(lax.bitwise_and(rounds, 1) == 1)
    def _():
        some((rounds - 1) * UNROLL, UNROLL)


def step_kernel(count, rows, cd_tiles, group, listed, split, *refs):
    pieces = refs[: len(group)]
    mine, send, total = refs[-3:]
    products(cd_tiles, listed, split, pieces, total)
    half = rows * count // 2
    for at, (span, offset) in enumerate(group):
        place = place_of(count, rows, offset)
        block = total[at * rows : (at + 1) * rows, :]

        @pl.when(place < half)
        def _():
            mine[span, pl.ds(pl.multiple_of(place, rows), rows), :] = block

        @pl.when(place >= half)
        def _():
            send[span, pl.ds(pl.multiple_of(place - half, rows), rows), :] = block


def last_kernel(cd_tiles, listed, split, *refs):
    products(cd_tiles, listed, split, refs[:-1], refs[-1])


def merge_kernel(mine, received, out):
    out[...] = mine[...] + received[...]


def final_kernel(count, spans, rows, last, received, before, out, total, sems):
    del before
    place = place_of(count, rows, -(count // 2))

    @pl.when(place < rows * count // 2)
    def _():
        total[...] = last[...] + received[...]
        copies = []
        for span in range(spans):
            copies.append(
                pltpu.make_async_copy(
                    total.at[pl.ds(span * rows, rows), :],
                    out.at[span, pl.ds(pl.multiple_of(place, rows), rows), :],
                    sems.at[span],
                )
            )
            copies[-1].start()
        for copy in copies:
            copy.wait()


def solution(mesh):
    count = mesh.shape["ab"]
    grid = grid_of(count)
    far = count // 2
    ahead = [(at_ring(at, *grid), at_ring((at + 1) % count, *grid)) for at in range(count)]
    back = [(to, start) for start, to in ahead]
    swap = [(0, 1), (1, 0)]

    def shards(amplitudes, integrals, ab_irrep, cd_irrep, block_pattern):
        spans, rows, depth = amplitudes.shape
        slab = integrals.shape[0]
        ab_tiles, cd_tiles = block_pattern.shape
        tiles = ab_tiles * cd_tiles
        half = rows * far

        in_hbm = functools.partial(pltpu.with_memory_space_constraint, memory_space=pltpu.HBM)
        smem = pl.BlockSpec(memory_space=pltpu.SMEM)
        vmem = pl.BlockSpec(memory_space=pltpu.VMEM)
        hbm = pl.BlockSpec(memory_space=pltpu.HBM)
        params = pltpu.CompilerParams(vmem_limit_bytes=VMEM_LIMIT)
        piece = pltpu.VMEM((1, rows, depth), jnp.float32)

        labels = (block_pattern, ab_irrep, cd_irrep)
        *own, near_pattern, near_ab, near_cd = pl.pallas_call(
            cut_kernel,
            out_shape=(piece,) * spans + tuple(pltpu.VMEM(label.shape, label.dtype) for label in labels),
            in_specs=[hbm] * 4,
            out_specs=(vmem,) * (spans + 3),
            scratch_shapes=[pltpu.SemaphoreType.DMA((spans + 3,))],
            compiler_params=params,
            name="cut",
        )(in_hbm(amplitudes), *map(in_hbm, labels))

        listed, landed = pl.pallas_call(
            functools.partial(list_kernel, ab_tiles, cd_tiles),
            out_shape=(pltpu.VMEM((2, LANES), jnp.int32), pltpu.VMEM((tiles, TILE, TILE), jnp.float32)),
            in_specs=[smem, smem, vmem, hbm],
            out_specs=(vmem, vmem),
            scratch_shapes=[
                pltpu.SMEM((2, LANES), jnp.int32),
                pltpu.SemaphoreType.DMA,
                pltpu.SemaphoreType.DMA((FLIGHT,)),
            ],
            compiler_params=params,
            cost_estimate=pl.CostEstimate(flops=0, bytes_accessed=4 << 20, transcendentals=0),
            name="list",
        )(near_ab, near_cd, near_pattern, in_hbm(integrals))
        split = pl.pallas_call(
            part_kernel,
            out_shape=pltpu.VMEM((tiles, TILE, 2 * TILE), jnp.bfloat16),
            in_specs=[smem, vmem],
            out_specs=vmem,
            compiler_params=params,
            cost_estimate=pl.CostEstimate(flops=0, bytes_accessed=8 << 20, transcendentals=0),
            name="part",
        )(listed, landed)

        held = {}
        for span in range(spans):
            held[span, 0] = own[span]
            for pairs, sign in ((ahead, -1), (back, 1)):
                moved = own[span]
                for hop in range(1, far + 1 if (sign < 0) == (span % 2 == 0) else far):
                    if hop in (2, 3):
                        moved, _ = lax.optimization_barrier((moved, listed if hop == 2 else split))
                    moved = lax.ppermute(moved, "ab", pairs)
                    held[span, -far if hop == far else sign * hop] = moved

        def offset_of(span, hop, long):
            return -hop if (span % 2 == 0) == long else hop

        arrivals = [(span, 0) for span in range(spans)]
        for hop in range(1, far):
            arrivals += [(span, offset_of(span, hop, long)) for long in (True, False) for span in range(spans)]
        block = pltpu.VMEM((spans, half, slab), jnp.float32)
        parts = ()
        cuts = sorted({*range(0, len(arrivals) - spans, GROUP), len(arrivals) - spans, len(arrivals)})
        for start, stop in zip(cuts, cuts[1:]):
            group = arrivals[start:stop]
            pieces = [held[key] for key in group]
            parts = pl.pallas_call(
                functools.partial(step_kernel, count, rows, cd_tiles, group),
                out_shape=(block, block),
                in_specs=[smem] + [vmem] * (1 + len(pieces) + len(parts)),
                out_specs=(vmem, vmem),
                scratch_shapes=[pltpu.VMEM((len(pieces) * rows, slab), jnp.float32)],
                compiler_params=params,
                input_output_aliases={2 + len(pieces): 0, 3 + len(pieces): 1} if parts else {},
                cost_estimate=pl.CostEstimate(flops=STEP_FLOPS, bytes_accessed=4 << 20, transcendentals=0),
                name="step",
            )(listed, split, *pieces, *parts)
        mine, send = parts
        base = pl.pallas_call(
            merge_kernel,
            out_shape=pltpu.HBM((spans, half, slab), jnp.float32),
            in_specs=[vmem, vmem],
            out_specs=vmem,
            compiler_params=params,
            name="merge",
        )(mine, lax.ppermute(send, "cd", swap))

        last = pl.pallas_call(
            functools.partial(last_kernel, cd_tiles),
            out_shape=pltpu.VMEM((spans * rows, slab), jnp.float32),
            in_specs=[smem, vmem] + [vmem] * spans,
            out_specs=vmem,
            compiler_params=params,
            cost_estimate=pl.CostEstimate(flops=1 << 34, bytes_accessed=4 << 20, transcendentals=0),
            name="last",
        )(listed, split, *[held[span, -far] for span in range(spans)])
        return pl.pallas_call(
            functools.partial(final_kernel, count, spans, rows),
            out_shape=pltpu.HBM((spans, half, slab), jnp.float32),
            in_specs=[vmem, vmem, hbm],
            out_specs=hbm,
            scratch_shapes=[pltpu.VMEM((spans * rows, slab), jnp.float32), pltpu.SemaphoreType.DMA((spans,))],
            compiler_params=params,
            input_output_aliases={2: 0},
            name="final",
        )(last, lax.ppermute(last, "cd", swap), base)

    in_specs = (
        P("groups", "ab", "cd"),
        P(("groups", "ab"), "cd"),
        P(("groups", "ab")),
        P(("groups", "cd")),
        P(("groups", "ab"), "cd"),
    )
    out_specs = P("groups", "cd", "ab")
    return jax.shard_map(shards, mesh=mesh, in_specs=in_specs, out_specs=out_specs, check_vma=False)
```

```python
import functools

import jax
import jax.numpy as jnp
from jax import lax
from jax.experimental import pallas as pl
from jax.experimental.pallas import tpu as pltpu
from jax.sharding import PartitionSpec as P

TILE = 128
UNROLL = 4
LANES = 128
AHEAD = 8
FLIGHT = AHEAD * UNROLL
GROUP = 12
STEP_FLOPS = 1 << 30
VMEM_LIMIT = 12 * 2**20


def grid_of(count):
    bits = count.bit_length() - 1
    if count != 1 << bits or bits < 2:
        return count, 1
    rows = 1 << ((bits + 1) // 2)
    return rows, count // rows


def at_ring(place, rows, columns):
    if columns == 1:
        return place
    wide = columns - 1
    beyond = place - rows
    line = beyond // wide
    step = beyond - line * wide
    even = (line % 2) == 0
    if isinstance(place, int):
        back = (rows - 1 - line) * columns + (1 + step if even else columns - 1 - step)
        return place * columns if place < rows else back
    back = (rows - 1 - line) * columns + jnp.where(even, 1 + step, columns - 1 - step)
    return jnp.where(place < rows, place * columns, back)


def ring_of(index, rows, columns):
    if columns == 1:
        return index
    wide = columns - 1
    row = index // columns
    column = index - row * columns
    line = rows - 1 - row
    step = jnp.where((line % 2) == 0, column - 1, columns - 1 - column)
    return jnp.where(column == 0, row, rows + line * wide + step)


def place_of(count, rows, offset):
    grid = grid_of(count)
    here = ring_of(lax.axis_index("ab"), *grid)
    whole = rows * count
    start = at_ring((here + offset + count) % count, *grid) * rows + lax.axis_index("cd") * (whole // 2)
    return jnp.where(start >= whole, start - whole, start)


def cut_kernel(ab_tiles, cd_tiles, spans, amplitudes, labels_ab, labels_cd, labels_pattern, *refs):
    outs, (listed, ab_irrep, cd_irrep, pattern, sems) = refs[:spans], refs[spans:]
    pairs = [(labels_ab, ab_irrep), (labels_cd, cd_irrep), (labels_pattern, pattern)]
    pairs += [(amplitudes.at[pl.ds(at, 1)], out) for at, out in enumerate(outs)]
    copies = [pltpu.make_async_copy(start, end, sems.at[at]) for at, (start, end) in enumerate(pairs)]
    for copy in copies:
        copy.start()
    for copy in copies[:3]:
        copy.wait()

    shape = (ab_tiles, LANES)
    lane = lax.broadcasted_iota(jnp.int32, shape, 1)
    line = lax.broadcasted_iota(jnp.int32, shape, 0)
    rows = jnp.full(shape, -1, jnp.int32)
    columns = jnp.full(shape, -2, jnp.int32)
    for p in range(ab_tiles):
        rows = jnp.where(line == p, ab_irrep[p], rows)
    for q in range(cd_tiles):
        columns = jnp.where(lane == q, cd_irrep[q], columns)
    stored = jnp.concatenate([pattern[...], jnp.zeros((ab_tiles, LANES - cd_tiles), jnp.int32)], axis=1)
    keep = jnp.where(jnp.logical_and(stored == 1, rows == columns), 1.0, 0.0)

    upto = keep
    reach = 1
    while reach < cd_tiles:
        upto += jnp.where(lane >= reach, pltpu.roll(upto, reach, 1), 0.0)
        reach *= 2
    whole = jnp.broadcast_to(jnp.sum(keep, axis=1, keepdims=True), shape)
    before = whole
    reach = 1
    while reach < ab_tiles:
        before += jnp.where(line >= reach, pltpu.roll(before, reach, 0), 0.0)
        reach *= 2
    found = before[ab_tiles - 1 :, :]
    upto += before - whole

    turned = upto.T
    order = lax.broadcasted_iota(jnp.int32, (cd_tiles, LANES), 1).astype(jnp.float32)
    passed = jnp.zeros((cd_tiles, LANES), jnp.float32)
    for p in range(ab_tiles):
        passed += jnp.where(turned[:cd_tiles, p : p + 1] <= order, 1.0, 0.0)
    places = jnp.sum(passed, axis=0, keepdims=True)
    listed[0:1, :] = jnp.where(order[0:1, :] < found, places, 0.0).astype(jnp.int32)
    listed[1:2, :] = ((found + (UNROLL - 1)) * (1.0 / UNROLL)).astype(jnp.int32)
    for copy in copies[3:]:
        copy.wait()


def part_kernel(cd_tiles, listed, integrals, split, landed, sems):
    def fetch(k):
        start, column = place_in(listed[0, k], cd_tiles)
        slot = lax.bitwise_and(k, FLIGHT - 1)
        return pltpu.make_async_copy(
            integrals.at[pl.ds(start, TILE), pl.ds(column, TILE)], landed.at[slot], sems.at[slot]
        )

    def begin(round_at, carry):
        for unrolled in range(UNROLL):
            fetch(round_at * UNROLL + unrolled).start()
        return carry

    rounds = listed[1, 0]
    lax.fori_loop(0, jnp.minimum(rounds, AHEAD), begin, 0)

    def part(round_at, carry):
        first = round_at * UNROLL
        for unrolled in range(UNROLL):
            fetch(first + unrolled).wait()
        for unrolled in range(UNROLL):
            k = first + unrolled
            real = jnp.logical_or(k == 0, listed[0, k] > 0)
            tile = jnp.where(real, landed[lax.bitwise_and(k, FLIGHT - 1)], 0.0).T
            upper = tile.astype(jnp.bfloat16)
            split[k, :, :TILE] = upper
            split[k, :, TILE:] = (tile - upper.astype(jnp.float32)).astype(jnp.bfloat16)

        @pl.when(round_at + AHEAD < rounds)
        def _():
            begin(round_at + AHEAD, 0)

        return carry

    lax.fori_loop(0, rounds, part, 0)


def place_in(place, cd_tiles):
    bits = cd_tiles.bit_length() - 1
    if cd_tiles == 1 << bits:
        row, column = lax.shift_right_logical(place, bits), lax.bitwise_and(place, cd_tiles - 1)
    else:
        row, column = lax.div(place, cd_tiles), lax.rem(place, cd_tiles)
    return pl.multiple_of(row * TILE, TILE), pl.multiple_of(column * TILE, TILE)


def products(cd_tiles, listed, split, pieces, total):
    total[...] = jnp.zeros_like(total)

    def some(first, many):
        sums = []
        for unrolled in range(many):
            start, column = place_in(listed[0, first + unrolled], cd_tiles)
            left = jnp.concatenate([piece[0, :, pl.ds(column, TILE)] for piece in pieces], axis=0)
            upper = left.astype(jnp.bfloat16)
            lower = (left - upper.astype(jnp.float32)).astype(jnp.bfloat16)
            tile = split[first + unrolled]
            both = jnp.dot(jnp.concatenate([upper, lower], axis=0), tile, preferred_element_type=jnp.float32)
            high, low = both[: left.shape[0]], both[left.shape[0] :]
            sums.append((start, high[:, :TILE] + (high[:, TILE:] + (low[:, :TILE] + low[:, TILE:]))))
        for start, term in sums:
            total[:, pl.ds(start, TILE)] += term

    def step(at, carry):
        some(at * 2 * UNROLL, 2 * UNROLL)
        return carry

    rounds = listed[1, 0]
    lax.fori_loop(0, lax.shift_right_logical(rounds, 1), step, 0)

    @pl.when(lax.bitwise_and(rounds, 1) == 1)
    def _():
        some((rounds - 1) * UNROLL, UNROLL)


def step_kernel(count, rows, cd_tiles, group, listed, split, *refs):
    pieces = refs[: len(group)]
    mine, send, total = refs[-3:]
    products(cd_tiles, listed, split, pieces, total)
    half = rows * count // 2
    for at, (span, offset) in enumerate(group):
        place = place_of(count, rows, offset)
        block = total[at * rows : (at + 1) * rows, :]

        @pl.when(place < half)
        def _():
            mine[span, pl.ds(pl.multiple_of(place, rows), rows), :] = block

        @pl.when(place >= half)
        def _():
            send[span, pl.ds(pl.multiple_of(place - half, rows), rows), :] = block


def last_kernel(cd_tiles, listed, split, *refs):
    products(cd_tiles, listed, split, refs[:-1], refs[-1])


def merge_kernel(mine, received, out):
    out[...] = mine[...] + received[...]


def final_kernel(count, spans, rows, last, received, before, out, total, sems):
    del before
    place = place_of(count, rows, -(count // 2))

    @pl.when(place < rows * count // 2)
    def _():
        total[...] = last[...] + received[...]
        copies = []
        for span in range(spans):
            copies.append(
                pltpu.make_async_copy(
                    total.at[pl.ds(span * rows, rows), :],
                    out.at[span, pl.ds(pl.multiple_of(place, rows), rows), :],
                    sems.at[span],
                )
            )
            copies[-1].start()
        for copy in copies:
            copy.wait()


def solution(mesh):
    count = mesh.shape["ab"]
    grid = grid_of(count)
    far = count // 2
    ahead = [(at_ring(at, *grid), at_ring((at + 1) % count, *grid)) for at in range(count)]
    back = [(to, start) for start, to in ahead]
    swap = [(0, 1), (1, 0)]

    def shards(amplitudes, integrals, ab_irrep, cd_irrep, block_pattern):
        spans, rows, depth = amplitudes.shape
        slab = integrals.shape[0]
        ab_tiles, cd_tiles = block_pattern.shape
        tiles = ab_tiles * cd_tiles
        half = rows * far

        in_hbm = functools.partial(pltpu.with_memory_space_constraint, memory_space=pltpu.HBM)
        smem = pl.BlockSpec(memory_space=pltpu.SMEM)
        vmem = pl.BlockSpec(memory_space=pltpu.VMEM)
        hbm = pl.BlockSpec(memory_space=pltpu.HBM)
        params = pltpu.CompilerParams(vmem_limit_bytes=VMEM_LIMIT)
        piece = pltpu.VMEM((1, rows, depth), jnp.float32)

        *own, listed = pl.pallas_call(
            functools.partial(cut_kernel, ab_tiles, cd_tiles, spans),
            out_shape=(piece,) * spans + (pltpu.VMEM((2, LANES), jnp.int32),),
            in_specs=[hbm] * 4,
            out_specs=(vmem,) * (spans + 1),
            scratch_shapes=[
                pltpu.SMEM(ab_irrep.shape, jnp.int32),
                pltpu.SMEM(cd_irrep.shape, jnp.int32),
                pltpu.VMEM(block_pattern.shape, jnp.int32),
                pltpu.SemaphoreType.DMA((spans + 3,)),
            ],
            compiler_params=params,
            name="cut",
        )(*map(in_hbm, (amplitudes, ab_irrep, cd_irrep, block_pattern)))
        split = pl.pallas_call(
            functools.partial(part_kernel, cd_tiles),
            out_shape=pltpu.VMEM((tiles, TILE, 2 * TILE), jnp.bfloat16),
            in_specs=[smem, hbm],
            out_specs=vmem,
            scratch_shapes=[pltpu.VMEM((FLIGHT, TILE, TILE), jnp.float32), pltpu.SemaphoreType.DMA((FLIGHT,))],
            compiler_params=params,
            cost_estimate=pl.CostEstimate(flops=0, bytes_accessed=8 << 20, transcendentals=0),
            name="part",
        )(listed, in_hbm(integrals))

        held = {}
        for span in range(spans):
            held[span, 0] = own[span]
            for pairs, sign in ((ahead, -1), (back, 1)):
                moved = own[span]
                for hop in range(1, far + 1 if (sign < 0) == (span % 2 == 0) else far):
                    if hop == 2:
                        moved, _ = lax.optimization_barrier((moved, split))
                    moved = lax.ppermute(moved, "ab", pairs)
                    held[span, -far if hop == far else sign * hop] = moved

        def offset_of(span, hop, long):
            return -hop if (span % 2 == 0) == long else hop

        arrivals = [(span, 0) for span in range(spans)]
        for hop in range(1, far):
            arrivals += [(span, offset_of(span, hop, long)) for long in (True, False) for span in range(spans)]
        block = pltpu.VMEM((spans, half, slab), jnp.float32)
        parts = ()
        cuts = sorted({*range(0, len(arrivals) - spans, GROUP), len(arrivals) - spans, len(arrivals)})
        for start, stop in zip(cuts, cuts[1:]):
            group = arrivals[start:stop]
            pieces = [held[key] for key in group]
            parts = pl.pallas_call(
                functools.partial(step_kernel, count, rows, cd_tiles, group),
                out_shape=(block, block),
                in_specs=[smem] + [vmem] * (1 + len(pieces) + len(parts)),
                out_specs=(vmem, vmem),
                scratch_shapes=[pltpu.VMEM((len(pieces) * rows, slab), jnp.float32)],
                compiler_params=params,
                input_output_aliases={2 + len(pieces): 0, 3 + len(pieces): 1} if parts else {},
                cost_estimate=pl.CostEstimate(flops=STEP_FLOPS, bytes_accessed=4 << 20, transcendentals=0),
                name="step",
            )(listed, split, *pieces, *parts)
        mine, send = parts
        base = pl.pallas_call(
            merge_kernel,
            out_shape=pltpu.HBM((spans, half, slab), jnp.float32),
            in_specs=[vmem, vmem],
            out_specs=vmem,
            compiler_params=params,
            name="merge",
        )(mine, lax.ppermute(send, "cd", swap))

        last = pl.pallas_call(
            functools.partial(last_kernel, cd_tiles),
            out_shape=pltpu.VMEM((spans * rows, slab), jnp.float32),
            in_specs=[smem, vmem] + [vmem] * spans,
            out_specs=vmem,
            compiler_params=params,
            cost_estimate=pl.CostEstimate(flops=1 << 34, bytes_accessed=4 << 20, transcendentals=0),
            name="last",
        )(listed, split, *[held[span, -far] for span in range(spans)])
        return pl.pallas_call(
            functools.partial(final_kernel, count, spans, rows),
            out_shape=pltpu.HBM((spans, half, slab), jnp.float32),
            in_specs=[vmem, vmem, hbm],
            out_specs=hbm,
            scratch_shapes=[pltpu.VMEM((spans * rows, slab), jnp.float32), pltpu.SemaphoreType.DMA((spans,))],
            compiler_params=params,
            input_output_aliases={2: 0},
            name="final",
        )(last, lax.ppermute(last, "cd", swap), base)

    in_specs = (
        P("groups", "ab", "cd"),
        P(("groups", "ab"), "cd"),
        P(("groups", "ab")),
        P(("groups", "cd")),
        P(("groups", "ab"), "cd"),
    )
    out_specs = P("groups", "cd", "ab")
    return jax.shard_map(shards, mesh=mesh, in_specs=in_specs, out_specs=out_specs, check_vma=False)
```

```python
import functools

import jax
import jax.numpy as jnp
from jax import lax
from jax.experimental import pallas as pl
from jax.experimental.pallas import tpu as pltpu
from jax.sharding import PartitionSpec as P

TILE = 128
UNROLL = 4
LANES = 128
AHEAD = 8
FLIGHT = AHEAD * UNROLL
GROUP = 12
STEP_FLOPS = 1 << 30
VMEM_LIMIT = 12 * 2**20


def grid_of(count):
    bits = count.bit_length() - 1
    if count != 1 << bits or bits < 2:
        return count, 1
    rows = 1 << ((bits + 1) // 2)
    return rows, count // rows


def at_ring(place, rows, columns):
    if columns == 1:
        return place
    wide = columns - 1
    beyond = place - rows
    line = beyond // wide
    step = beyond - line * wide
    even = (line % 2) == 0
    if isinstance(place, int):
        back = (rows - 1 - line) * columns + (1 + step if even else columns - 1 - step)
        return place * columns if place < rows else back
    back = (rows - 1 - line) * columns + jnp.where(even, 1 + step, columns - 1 - step)
    return jnp.where(place < rows, place * columns, back)


def ring_of(index, rows, columns):
    if columns == 1:
        return index
    wide = columns - 1
    row = index // columns
    column = index - row * columns
    line = rows - 1 - row
    step = jnp.where((line % 2) == 0, column - 1, columns - 1 - column)
    return jnp.where(column == 0, row, rows + line * wide + step)


def place_of(count, rows, offset):
    grid = grid_of(count)
    here = ring_of(lax.axis_index("ab"), *grid)
    whole = rows * count
    start = at_ring((here + offset + count) % count, *grid) * rows + lax.axis_index("cd") * (whole // 2)
    return jnp.where(start >= whole, start - whole, start)


def cut_kernel(ab_tiles, cd_tiles, spans, amplitudes, labels_ab, labels_cd, labels_pattern, *refs):
    outs, (listed, ab_irrep, cd_irrep, pattern, sems) = refs[:spans], refs[spans:]
    pairs = [(labels_ab, ab_irrep), (labels_cd, cd_irrep), (labels_pattern, pattern)]
    pairs += [(amplitudes.at[pl.ds(at, 1)], out) for at, out in enumerate(outs)]
    copies = [pltpu.make_async_copy(start, end, sems.at[at]) for at, (start, end) in enumerate(pairs)]
    for copy in copies:
        copy.start()
    for copy in copies[:3]:
        copy.wait()

    shape = (ab_tiles, LANES)
    lane = lax.broadcasted_iota(jnp.int32, shape, 1)
    line = lax.broadcasted_iota(jnp.int32, shape, 0)
    rows = jnp.full(shape, -1, jnp.int32)
    columns = jnp.full(shape, -2, jnp.int32)
    for p in range(ab_tiles):
        rows = jnp.where(line == p, ab_irrep[p], rows)
    for q in range(cd_tiles):
        columns = jnp.where(lane == q, cd_irrep[q], columns)
    stored = jnp.concatenate([pattern[...], jnp.zeros((ab_tiles, LANES - cd_tiles), jnp.int32)], axis=1)
    keep = jnp.where(jnp.logical_and(stored == 1, rows == columns), 1.0, 0.0)

    upto = keep
    reach = 1
    while reach < cd_tiles:
        upto += jnp.where(lane >= reach, pltpu.roll(upto, reach, 1), 0.0)
        reach *= 2
    whole = jnp.broadcast_to(jnp.sum(keep, axis=1, keepdims=True), shape)
    before = whole
    reach = 1
    while reach < ab_tiles:
        before += jnp.where(line >= reach, pltpu.roll(before, reach, 0), 0.0)
        reach *= 2
    found = before[ab_tiles - 1 :, :]
    upto += before - whole

    turned = upto.T
    order = lax.broadcasted_iota(jnp.int32, (cd_tiles, LANES), 1).astype(jnp.float32)
    passed = jnp.zeros((cd_tiles, LANES), jnp.float32)
    for p in range(ab_tiles):
        passed += jnp.where(turned[:cd_tiles, p : p + 1] <= order, 1.0, 0.0)
    places = jnp.sum(passed, axis=0, keepdims=True)
    listed[0:1, :] = jnp.where(order[0:1, :] < found, places, 0.0).astype(jnp.int32)
    listed[1:2, :] = ((found + (UNROLL - 1)) * (1.0 / UNROLL)).astype(jnp.int32)
    for copy in copies[3:]:
        copy.wait()


def part_kernel(cd_tiles, listed, integrals, split, landed, sems):
    def fetch(k):
        start, column = place_in(listed[0, k], cd_tiles)
        slot = lax.bitwise_and(k, FLIGHT - 1)
        return pltpu.make_async_copy(
            integrals.at[pl.ds(start, TILE), pl.ds(column, TILE)], landed.at[slot], sems.at[slot]
        )

    def begin(round_at, carry):
        for unrolled in range(UNROLL):
            fetch(round_at * UNROLL + unrolled).start()
        return carry

    rounds = listed[1, 0]
    lax.fori_loop(0, jnp.minimum(rounds, AHEAD), begin, 0)

    def part(round_at, carry):
        first = round_at * UNROLL
        for unrolled in range(UNROLL):
            fetch(first + unrolled).wait()
        for unrolled in range(UNROLL):
            k = first + unrolled
            real = jnp.logical_or(k == 0, listed[0, k] > 0)
            tile = jnp.where(real, landed[lax.bitwise_and(k, FLIGHT - 1)], 0.0).T
            upper = tile.astype(jnp.bfloat16)
            split[k, :, :TILE] = upper
            split[k, :, TILE:] = (tile - upper.astype(jnp.float32)).astype(jnp.bfloat16)

        @pl.when(round_at + AHEAD < rounds)
        def _():
            begin(round_at + AHEAD, 0)

        return carry

    lax.fori_loop(0, rounds, part, 0)


def place_in(place, cd_tiles):
    bits = cd_tiles.bit_length() - 1
    if cd_tiles == 1 << bits:
        row, column = lax.shift_right_logical(place, bits), lax.bitwise_and(place, cd_tiles - 1)
    else:
        row, column = lax.div(place, cd_tiles), lax.rem(place, cd_tiles)
    return pl.multiple_of(row * TILE, TILE), pl.multiple_of(column * TILE, TILE)


def products(cd_tiles, listed, split, pieces, total):
    total[...] = jnp.zeros_like(total)

    def some(first, many):
        sums = []
        for unrolled in range(many):
            start, column = place_in(listed[0, first + unrolled], cd_tiles)
            left = jnp.concatenate([piece[0, :, pl.ds(column, TILE)] for piece in pieces], axis=0)
            upper = left.astype(jnp.bfloat16)
            lower = (left - upper.astype(jnp.float32)).astype(jnp.bfloat16)
            tile = split[first + unrolled]
            both = jnp.dot(jnp.concatenate([upper, lower], axis=0), tile, preferred_element_type=jnp.float32)
            high, low = both[: left.shape[0]], both[left.shape[0] :]
            sums.append((start, high[:, :TILE] + (high[:, TILE:] + (low[:, :TILE] + low[:, TILE:]))))
        for start, term in sums:
            total[:, pl.ds(start, TILE)] += term

    def step(at, carry):
        some(at * 2 * UNROLL, 2 * UNROLL)
        return carry

    rounds = listed[1, 0]
    lax.fori_loop(0, lax.shift_right_logical(rounds, 1), step, 0)

    @pl.when(lax.bitwise_and(rounds, 1) == 1)
    def _():
        some((rounds - 1) * UNROLL, UNROLL)


def step_kernel(count, rows, cd_tiles, group, listed, split, *refs):
    pieces = refs[: len(group)]
    mine, send, total = refs[-3:]
    products(cd_tiles, listed, split, pieces, total)
    half = rows * count // 2
    for at, (span, offset) in enumerate(group):
        place = place_of(count, rows, offset)
        block = total[at * rows : (at + 1) * rows, :]

        @pl.when(place < half)
        def _():
            mine[span, pl.ds(pl.multiple_of(place, rows), rows), :] = block

        @pl.when(place >= half)
        def _():
            send[span, pl.ds(pl.multiple_of(place - half, rows), rows), :] = block


def last_kernel(cd_tiles, listed, split, *refs):
    products(cd_tiles, listed, split, refs[:-1], refs[-1])


def merge_kernel(mine, received, out):
    out[...] = mine[...] + received[...]


def final_kernel(count, spans, rows, last, received, before, out, total, sems):
    del before
    place = place_of(count, rows, -(count // 2))

    @pl.when(place < rows * count // 2)
    def _():
        total[...] = last[...] + received[...]
        copies = []
        for span in range(spans):
            copies.append(
                pltpu.make_async_copy(
                    total.at[pl.ds(span * rows, rows), :],
                    out.at[span, pl.ds(pl.multiple_of(place, rows), rows), :],
                    sems.at[span],
                )
            )
            copies[-1].start()
        for copy in copies:
            copy.wait()


def solution(mesh):
    count = mesh.shape["ab"]
    grid = grid_of(count)
    far = count // 2
    ahead = [(at_ring(at, *grid), at_ring((at + 1) % count, *grid)) for at in range(count)]
    back = [(to, start) for start, to in ahead]
    swap = [(0, 1), (1, 0)]

    def shards(amplitudes, integrals, ab_irrep, cd_irrep, block_pattern):
        spans, rows, depth = amplitudes.shape
        slab = integrals.shape[0]
        ab_tiles, cd_tiles = block_pattern.shape
        tiles = ab_tiles * cd_tiles
        half = rows * far

        in_hbm = functools.partial(pltpu.with_memory_space_constraint, memory_space=pltpu.HBM)
        smem = pl.BlockSpec(memory_space=pltpu.SMEM)
        vmem = pl.BlockSpec(memory_space=pltpu.VMEM)
        hbm = pl.BlockSpec(memory_space=pltpu.HBM)
        params = pltpu.CompilerParams(vmem_limit_bytes=VMEM_LIMIT)
        piece = pltpu.VMEM((1, rows, depth), jnp.float32)

        *own, listed = pl.pallas_call(
            functools.partial(cut_kernel, ab_tiles, cd_tiles, spans),
            out_shape=(piece,) * spans + (pltpu.VMEM((2, LANES), jnp.int32),),
            in_specs=[hbm] * 4,
            out_specs=(vmem,) * (spans + 1),
            scratch_shapes=[
                pltpu.SMEM(ab_irrep.shape, jnp.int32),
                pltpu.SMEM(cd_irrep.shape, jnp.int32),
                pltpu.VMEM(block_pattern.shape, jnp.int32),
                pltpu.SemaphoreType.DMA((spans + 3,)),
            ],
            compiler_params=params,
            name="cut",
        )(*map(in_hbm, (amplitudes, ab_irrep, cd_irrep, block_pattern)))
        split = pl.pallas_call(
            functools.partial(part_kernel, cd_tiles),
            out_shape=pltpu.VMEM((tiles, TILE, 2 * TILE), jnp.bfloat16),
            in_specs=[smem, hbm],
            out_specs=vmem,
            scratch_shapes=[pltpu.VMEM((FLIGHT, TILE, TILE), jnp.float32), pltpu.SemaphoreType.DMA((FLIGHT,))],
            compiler_params=params,
            cost_estimate=pl.CostEstimate(flops=0, bytes_accessed=8 << 20, transcendentals=0),
            name="part",
        )(listed, in_hbm(integrals))

        block = pltpu.VMEM((spans, half, slab), jnp.float32)

        def step(group, parts):
            pieces = [held[key] for key in group]
            return pl.pallas_call(
                functools.partial(step_kernel, count, rows, cd_tiles, group),
                out_shape=(block, block),
                in_specs=[smem] + [vmem] * (1 + len(pieces) + len(parts)),
                out_specs=(vmem, vmem),
                scratch_shapes=[pltpu.VMEM((len(pieces) * rows, slab), jnp.float32)],
                compiler_params=params,
                input_output_aliases={2 + len(pieces): 0, 3 + len(pieces): 1} if parts else {},
                cost_estimate=pl.CostEstimate(flops=STEP_FLOPS, bytes_accessed=4 << 20, transcendentals=0),
                name="step",
            )(listed, split, *pieces, *parts)

        held = {(span, 0): own[span] for span in range(spans)}
        flows = [(span, sign) for long in (True, False) for span in range(spans) for sign in (-1, 1) if ((sign < 0) == (span % 2 == 0)) == long]
        moving = {(span, sign): own[span] for span, sign in flows}
        arrivals, parts = [(span, 0) for span in range(spans)], ()
        for hop in range(1, far + 1):
            for span, sign in flows:
                long = (sign < 0) == (span % 2 == 0)
                if hop < far or long:
                    moved = moving[span, sign]
                    if hop == 2:
                        moved, _ = lax.optimization_barrier((moved, split))
                    if hop == 3:
                        moved, _ = lax.optimization_barrier((moved, parts[0]))
                    moved = moving[span, sign] = lax.ppermute(moved, "ab", ahead if sign < 0 else back)
                    offset = -far if hop == far else sign * hop
                    held[span, offset] = moved
                    if hop < far:
                        arrivals.append((span, offset))
            if hop == 1:
                parts = step(arrivals, parts)
                arrivals = []
        late = len(arrivals) - spans
        for start in range(0, late, GROUP):
            parts = step(arrivals[start : min(start + GROUP, late)], parts)
        parts = step(arrivals[late:], parts)
        mine, send = parts
        base = pl.pallas_call(
            merge_kernel,
            out_shape=pltpu.HBM((spans, half, slab), jnp.float32),
            in_specs=[vmem, vmem],
            out_specs=vmem,
            compiler_params=params,
            name="merge",
        )(mine, lax.ppermute(send, "cd", swap))

        last = pl.pallas_call(
            functools.partial(last_kernel, cd_tiles),
            out_shape=pltpu.VMEM((spans * rows, slab), jnp.float32),
            in_specs=[smem, vmem] + [vmem] * spans,
            out_specs=vmem,
            compiler_params=params,
            cost_estimate=pl.CostEstimate(flops=1 << 34, bytes_accessed=4 << 20, transcendentals=0),
            name="last",
        )(listed, split, *[held[span, -far] for span in range(spans)])
        return pl.pallas_call(
            functools.partial(final_kernel, count, spans, rows),
            out_shape=pltpu.HBM((spans, half, slab), jnp.float32),
            in_specs=[vmem, vmem, hbm],
            out_specs=hbm,
            scratch_shapes=[pltpu.VMEM((spans * rows, slab), jnp.float32), pltpu.SemaphoreType.DMA((spans,))],
            compiler_params=params,
            input_output_aliases={2: 0},
            name="final",
        )(last, lax.ppermute(last, "cd", swap), base)

    in_specs = (
        P("groups", "ab", "cd"),
        P(("groups", "ab"), "cd"),
        P(("groups", "ab")),
        P(("groups", "cd")),
        P(("groups", "ab"), "cd"),
    )
    out_specs = P("groups", "cd", "ab")
    return jax.shard_map(shards, mesh=mesh, in_specs=in_specs, out_specs=out_specs, check_vma=False)
```

```python
import functools

import jax
import jax.numpy as jnp
from jax import lax
from jax.experimental import pallas as pl
from jax.experimental.pallas import tpu as pltpu
from jax.sharding import PartitionSpec as P

TILE = 128
UNROLL = 4
LANES = 128
AHEAD = 8
FLIGHT = AHEAD * UNROLL
GROUP = 12
STEP_FLOPS = 1 << 30
VMEM_LIMIT = 12 * 2**20


def grid_of(count):
    bits = count.bit_length() - 1
    if count != 1 << bits or bits < 2:
        return count, 1
    rows = 1 << ((bits + 1) // 2)
    return rows, count // rows


def at_ring(place, rows, columns):
    if columns == 1:
        return place
    wide = columns - 1
    beyond = place - rows
    line = beyond // wide
    step = beyond - line * wide
    even = (line % 2) == 0
    if isinstance(place, int):
        back = (rows - 1 - line) * columns + (1 + step if even else columns - 1 - step)
        return place * columns if place < rows else back
    back = (rows - 1 - line) * columns + jnp.where(even, 1 + step, columns - 1 - step)
    return jnp.where(place < rows, place * columns, back)


def ring_of(index, rows, columns):
    if columns == 1:
        return index
    wide = columns - 1
    row = index // columns
    column = index - row * columns
    line = rows - 1 - row
    step = jnp.where((line % 2) == 0, column - 1, columns - 1 - column)
    return jnp.where(column == 0, row, rows + line * wide + step)


def place_of(count, rows, offset):
    grid = grid_of(count)
    here = ring_of(lax.axis_index("ab"), *grid)
    whole = rows * count
    start = at_ring((here + offset + count) % count, *grid) * rows + lax.axis_index("cd") * (whole // 2)
    return jnp.where(start >= whole, start - whole, start)


def cut_kernel(ab_tiles, cd_tiles, spans, amplitudes, labels_ab, labels_cd, labels_pattern, *refs):
    outs, (listed, ab_irrep, cd_irrep, pattern, sems) = refs[:spans], refs[spans:]
    pairs = [(labels_ab, ab_irrep), (labels_cd, cd_irrep), (labels_pattern, pattern)]
    pairs += [(amplitudes.at[pl.ds(at, 1)], out) for at, out in enumerate(outs)]
    copies = [pltpu.make_async_copy(start, end, sems.at[at]) for at, (start, end) in enumerate(pairs)]
    for copy in copies:
        copy.start()
    for copy in copies[:3]:
        copy.wait()

    shape = (ab_tiles, LANES)
    lane = lax.broadcasted_iota(jnp.int32, shape, 1)
    line = lax.broadcasted_iota(jnp.int32, shape, 0)
    rows = jnp.full(shape, -1, jnp.int32)
    columns = jnp.full(shape, -2, jnp.int32)
    for p in range(ab_tiles):
        rows = jnp.where(line == p, ab_irrep[p], rows)
    for q in range(cd_tiles):
        columns = jnp.where(lane == q, cd_irrep[q], columns)
    stored = jnp.concatenate([pattern[...], jnp.zeros((ab_tiles, LANES - cd_tiles), jnp.int32)], axis=1)
    keep = jnp.where(jnp.logical_and(stored == 1, rows == columns), 1.0, 0.0)

    upto = keep
    reach = 1
    while reach < cd_tiles:
        upto += jnp.where(lane >= reach, pltpu.roll(upto, reach, 1), 0.0)
        reach *= 2
    whole = jnp.broadcast_to(jnp.sum(keep, axis=1, keepdims=True), shape)
    before = whole
    reach = 1
    while reach < ab_tiles:
        before += jnp.where(line >= reach, pltpu.roll(before, reach, 0), 0.0)
        reach *= 2
    found = before[ab_tiles - 1 :, :]
    upto += before - whole

    turned = upto.T
    order = lax.broadcasted_iota(jnp.int32, (cd_tiles, LANES), 1).astype(jnp.float32)
    passed = jnp.zeros((cd_tiles, LANES), jnp.float32)
    for p in range(ab_tiles):
        passed += jnp.where(turned[:cd_tiles, p : p + 1] <= order, 1.0, 0.0)
    places = jnp.sum(passed, axis=0, keepdims=True)
    listed[0:1, :] = jnp.where(order[0:1, :] < found, places, 0.0).astype(jnp.int32)
    listed[1:2, :] = ((found + (UNROLL - 1)) * (1.0 / UNROLL)).astype(jnp.int32)
    for copy in copies[3:]:
        copy.wait()


def part_kernel(cd_tiles, listed, integrals, split, landed, sems):
    def fetch(k):
        start, column = place_in(listed[0, k], cd_tiles)
        slot = lax.bitwise_and(k, FLIGHT - 1)
        return pltpu.make_async_copy(
            integrals.at[pl.ds(start, TILE), pl.ds(column, TILE)], landed.at[slot], sems.at[slot]
        )

    def begin(round_at, carry):
        for unrolled in range(UNROLL):
            fetch(round_at * UNROLL + unrolled).start()
        return carry

    rounds = listed[1, 0]
    lax.fori_loop(0, jnp.minimum(rounds, AHEAD), begin, 0)

    def part(round_at, carry):
        first = round_at * UNROLL
        for unrolled in range(UNROLL):
            fetch(first + unrolled).wait()
        for unrolled in range(UNROLL):
            k = first + unrolled
            real = jnp.logical_or(k == 0, listed[0, k] > 0)
            tile = jnp.where(real, landed[lax.bitwise_and(k, FLIGHT - 1)], 0.0).T
            upper = tile.astype(jnp.bfloat16)
            split[k, :, :TILE] = upper
            split[k, :, TILE:] = (tile - upper.astype(jnp.float32)).astype(jnp.bfloat16)

        @pl.when(round_at + AHEAD < rounds)
        def _():
            begin(round_at + AHEAD, 0)

        return carry

    lax.fori_loop(0, rounds, part, 0)


def place_in(place, cd_tiles):
    bits = cd_tiles.bit_length() - 1
    if cd_tiles == 1 << bits:
        row, column = lax.shift_right_logical(place, bits), lax.bitwise_and(place, cd_tiles - 1)
    else:
        row, column = lax.div(place, cd_tiles), lax.rem(place, cd_tiles)
    return pl.multiple_of(row * TILE, TILE), pl.multiple_of(column * TILE, TILE)


def products(cd_tiles, listed, split, pieces, total):
    total[...] = jnp.zeros_like(total)

    def some(first, many):
        sums = []
        for unrolled in range(many):
            start, column = place_in(listed[0, first + unrolled], cd_tiles)
            left = jnp.concatenate([piece[0, :, pl.ds(column, TILE)] for piece in pieces], axis=0)
            upper = left.astype(jnp.bfloat16)
            lower = (left - upper.astype(jnp.float32)).astype(jnp.bfloat16)
            tile = split[first + unrolled]
            both = jnp.dot(jnp.concatenate([upper, lower], axis=0), tile, preferred_element_type=jnp.float32)
            high, low = both[: left.shape[0]], both[left.shape[0] :]
            sums.append((start, high[:, :TILE] + (high[:, TILE:] + (low[:, :TILE] + low[:, TILE:]))))
        for start, term in sums:
            total[:, pl.ds(start, TILE)] += term

    def step(at, carry):
        some(at * 2 * UNROLL, 2 * UNROLL)
        return carry

    rounds = listed[1, 0]
    lax.fori_loop(0, lax.shift_right_logical(rounds, 1), step, 0)

    @pl.when(lax.bitwise_and(rounds, 1) == 1)
    def _():
        some((rounds - 1) * UNROLL, UNROLL)


def step_kernel(count, rows, cd_tiles, group, listed, split, *refs):
    pieces = refs[: len(group)]
    mine, send, total = refs[-3:]
    products(cd_tiles, listed, split, pieces, total)
    half = rows * count // 2
    for at, (span, offset) in enumerate(group):
        place = place_of(count, rows, offset)
        block = total[at * rows : (at + 1) * rows, :]

        @pl.when(place < half)
        def _():
            mine[span, pl.ds(pl.multiple_of(place, rows), rows), :] = block

        @pl.when(place >= half)
        def _():
            send[span, pl.ds(pl.multiple_of(place - half, rows), rows), :] = block


def last_kernel(cd_tiles, listed, split, *refs):
    products(cd_tiles, listed, split, refs[:-1], refs[-1])


def merge_kernel(mine, received, out):
    out[...] = mine[...] + received[...]


def final_kernel(count, spans, rows, last, received, before, out, total, sems):
    del before
    place = place_of(count, rows, -(count // 2))

    @pl.when(place < rows * count // 2)
    def _():
        total[...] = last[...] + received[...]
        copies = []
        for span in range(spans):
            copies.append(
                pltpu.make_async_copy(
                    total.at[pl.ds(span * rows, rows), :],
                    out.at[span, pl.ds(pl.multiple_of(place, rows), rows), :],
                    sems.at[span],
                )
            )
            copies[-1].start()
        for copy in copies:
            copy.wait()


def solution(mesh):
    count = mesh.shape["ab"]
    grid = grid_of(count)
    far = count // 2
    ahead = [(at_ring(at, *grid), at_ring((at + 1) % count, *grid)) for at in range(count)]
    back = [(to, start) for start, to in ahead]
    swap = [(0, 1), (1, 0)]

    def shards(amplitudes, integrals, ab_irrep, cd_irrep, block_pattern):
        spans, rows, depth = amplitudes.shape
        slab = integrals.shape[0]
        ab_tiles, cd_tiles = block_pattern.shape
        tiles = ab_tiles * cd_tiles
        half = rows * far

        in_hbm = functools.partial(pltpu.with_memory_space_constraint, memory_space=pltpu.HBM)
        smem = pl.BlockSpec(memory_space=pltpu.SMEM)
        vmem = pl.BlockSpec(memory_space=pltpu.VMEM)
        hbm = pl.BlockSpec(memory_space=pltpu.HBM)
        params = pltpu.CompilerParams(vmem_limit_bytes=VMEM_LIMIT)
        piece = pltpu.VMEM((1, rows, depth), jnp.float32)

        *own, listed = pl.pallas_call(
            functools.partial(cut_kernel, ab_tiles, cd_tiles, spans),
            out_shape=(piece,) * spans + (pltpu.VMEM((2, LANES), jnp.int32),),
            in_specs=[hbm] * 4,
            out_specs=(vmem,) * (spans + 1),
            scratch_shapes=[
                pltpu.SMEM(ab_irrep.shape, jnp.int32),
                pltpu.SMEM(cd_irrep.shape, jnp.int32),
                pltpu.VMEM(block_pattern.shape, jnp.int32),
                pltpu.SemaphoreType.DMA((spans + 3,)),
            ],
            compiler_params=params,
            name="cut",
        )(*map(in_hbm, (amplitudes, ab_irrep, cd_irrep, block_pattern)))
        split = pl.pallas_call(
            functools.partial(part_kernel, cd_tiles),
            out_shape=pltpu.VMEM((tiles, TILE, 2 * TILE), jnp.bfloat16),
            in_specs=[smem, hbm],
            out_specs=vmem,
            scratch_shapes=[pltpu.VMEM((FLIGHT, TILE, TILE), jnp.float32), pltpu.SemaphoreType.DMA((FLIGHT,))],
            compiler_params=params,
            cost_estimate=pl.CostEstimate(flops=0, bytes_accessed=8 << 20, transcendentals=0),
            name="part",
        )(listed, in_hbm(integrals))

        block = pltpu.VMEM((spans, half, slab), jnp.float32)

        def step(group, parts):
            pieces = [held[key] for key in group]
            return pl.pallas_call(
                functools.partial(step_kernel, count, rows, cd_tiles, group),
                out_shape=(block, block),
                in_specs=[smem] + [vmem] * (1 + len(pieces) + len(parts)),
                out_specs=(vmem, vmem),
                scratch_shapes=[pltpu.VMEM((len(pieces) * rows, slab), jnp.float32)],
                compiler_params=params,
                input_output_aliases={2 + len(pieces): 0, 3 + len(pieces): 1} if parts else {},
                cost_estimate=pl.CostEstimate(flops=STEP_FLOPS, bytes_accessed=4 << 20, transcendentals=0),
                name="step",
            )(listed, split, *pieces, *parts)

        held = {(span, 0): own[span] for span in range(spans)}
        flows = [(span, sign) for long in (True, False) for span in range(spans) for sign in (-1, 1) if ((sign < 0) == (span % 2 == 0)) == long]
        moving = {(span, sign): own[span] for span, sign in flows}
        arrivals, parts = [(span, 0) for span in range(spans)], ()
        for hop in range(1, far + 1):
            for span, sign in flows:
                long = (sign < 0) == (span % 2 == 0)
                if hop < far or long:
                    moved = moving[span, sign]
                    if hop == 2:
                        moved, _ = lax.optimization_barrier((moved, split))
                    if hop == 3 and long:
                        moved, _ = lax.optimization_barrier((moved, parts[0]))
                    moved = moving[span, sign] = lax.ppermute(moved, "ab", ahead if sign < 0 else back)
                    offset = -far if hop == far else sign * hop
                    held[span, offset] = moved
                    if hop < far:
                        arrivals.append((span, offset))
            if hop == 1:
                parts = step(arrivals, parts)
                arrivals = []
        late = len(arrivals) - spans
        for start in range(0, late, GROUP):
            parts = step(arrivals[start : min(start + GROUP, late)], parts)
        parts = step(arrivals[late:], parts)
        mine, send = parts
        base = pl.pallas_call(
            merge_kernel,
            out_shape=pltpu.HBM((spans, half, slab), jnp.float32),
            in_specs=[vmem, vmem],
            out_specs=vmem,
            compiler_params=params,
            name="merge",
        )(mine, lax.ppermute(send, "cd", swap))

        last = pl.pallas_call(
            functools.partial(last_kernel, cd_tiles),
            out_shape=pltpu.VMEM((spans * rows, slab), jnp.float32),
            in_specs=[smem, vmem] + [vmem] * spans,
            out_specs=vmem,
            compiler_params=params,
            cost_estimate=pl.CostEstimate(flops=1 << 34, bytes_accessed=4 << 20, transcendentals=0),
            name="last",
        )(listed, split, *[held[span, -far] for span in range(spans)])
        return pl.pallas_call(
            functools.partial(final_kernel, count, spans, rows),
            out_shape=pltpu.HBM((spans, half, slab), jnp.float32),
            in_specs=[vmem, vmem, hbm],
            out_specs=hbm,
            scratch_shapes=[pltpu.VMEM((spans * rows, slab), jnp.float32), pltpu.SemaphoreType.DMA((spans,))],
            compiler_params=params,
            input_output_aliases={2: 0},
            name="final",
        )(last, lax.ppermute(last, "cd", swap), base)

    in_specs = (
        P("groups", "ab", "cd"),
        P(("groups", "ab"), "cd"),
        P(("groups", "ab")),
        P(("groups", "cd")),
        P(("groups", "ab"), "cd"),
    )
    out_specs = P("groups", "cd", "ab")
    return jax.shard_map(shards, mesh=mesh, in_specs=in_specs, out_specs=out_specs, check_vma=False)
```

```python
import functools

import jax
import jax.numpy as jnp
from jax import lax
from jax.experimental import pallas as pl
from jax.experimental.pallas import tpu as pltpu
from jax.sharding import PartitionSpec as P

TILE = 128
UNROLL = 4
LANES = 128
BAND = 8
AHEAD = 8
FLIGHT = AHEAD * UNROLL
GROUP = 12
STEP_FLOPS = 1 << 30
VMEM_LIMIT = 12 * 2**20


def grid_of(count):
    bits = count.bit_length() - 1
    if count != 1 << bits or bits < 2:
        return count, 1
    rows = 1 << ((bits + 1) // 2)
    return rows, count // rows


def at_ring(place, rows, columns):
    if columns == 1:
        return place
    wide = columns - 1
    beyond = place - rows
    line = beyond // wide
    step = beyond - line * wide
    even = (line % 2) == 0
    if isinstance(place, int):
        back = (rows - 1 - line) * columns + (1 + step if even else columns - 1 - step)
        return place * columns if place < rows else back
    back = (rows - 1 - line) * columns + jnp.where(even, 1 + step, columns - 1 - step)
    return jnp.where(place < rows, place * columns, back)


def ring_of(index, rows, columns):
    if columns == 1:
        return index
    wide = columns - 1
    row = index // columns
    column = index - row * columns
    line = rows - 1 - row
    step = jnp.where((line % 2) == 0, column - 1, columns - 1 - column)
    return jnp.where(column == 0, row, rows + line * wide + step)


def place_of(count, rows, offset):
    grid = grid_of(count)
    here = ring_of(lax.axis_index("ab"), *grid)
    whole = rows * count
    start = at_ring((here + offset + count) % count, *grid) * rows + lax.axis_index("cd") * (whole // 2)
    return jnp.where(start >= whole, start - whole, start)


def cut_kernel(ab_tiles, cd_tiles, spans, amplitudes, labels_ab, labels_cd, labels_pattern, *refs):
    outs, (listed, ab_irrep, cd_irrep, pattern, sems) = refs[:spans], refs[spans:]
    pairs = [(labels_ab, ab_irrep), (labels_cd, cd_irrep), (labels_pattern, pattern)]
    rows, depth = amplitudes.shape[1:]
    for at, out in enumerate(outs):
        for row in range(0, rows, BAND):
            for column in range(0, depth, depth // 2):
                part = (pl.ds(row, BAND), pl.ds(column, depth // 2))
                pairs.append((amplitudes.at[(pl.ds(at, 1), *part)], out.at[(pl.ds(0, 1), *part)]))
    copies = [pltpu.make_async_copy(start, end, sems.at[at]) for at, (start, end) in enumerate(pairs)]
    for copy in copies:
        copy.start()
    for copy in copies[:3]:
        copy.wait()

    shape = (ab_tiles, LANES)
    lane = lax.broadcasted_iota(jnp.int32, shape, 1)
    line = lax.broadcasted_iota(jnp.int32, shape, 0)
    rows = jnp.full(shape, -1, jnp.int32)
    columns = jnp.full(shape, -2, jnp.int32)
    for p in range(ab_tiles):
        rows = jnp.where(line == p, ab_irrep[p], rows)
    for q in range(cd_tiles):
        columns = jnp.where(lane == q, cd_irrep[q], columns)
    stored = jnp.concatenate([pattern[...], jnp.zeros((ab_tiles, LANES - cd_tiles), jnp.int32)], axis=1)
    keep = jnp.where(jnp.logical_and(stored == 1, rows == columns), 1.0, 0.0)

    upto = keep
    reach = 1
    while reach < cd_tiles:
        upto += jnp.where(lane >= reach, pltpu.roll(upto, reach, 1), 0.0)
        reach *= 2
    whole = jnp.broadcast_to(jnp.sum(keep, axis=1, keepdims=True), shape)
    before = whole
    reach = 1
    while reach < ab_tiles:
        before += jnp.where(line >= reach, pltpu.roll(before, reach, 0), 0.0)
        reach *= 2
    found = before[ab_tiles - 1 :, :]
    upto += before - whole

    turned = upto.T
    order = lax.broadcasted_iota(jnp.int32, (cd_tiles, LANES), 1).astype(jnp.float32)
    passed = jnp.zeros((cd_tiles, LANES), jnp.float32)
    for p in range(ab_tiles):
        passed += jnp.where(turned[:cd_tiles, p : p + 1] <= order, 1.0, 0.0)
    places = jnp.sum(passed, axis=0, keepdims=True)
    listed[0:1, :] = jnp.where(order[0:1, :] < found, places, 0.0).astype(jnp.int32)
    listed[1:2, :] = ((found + (UNROLL - 1)) * (1.0 / UNROLL)).astype(jnp.int32)
    for copy in copies[3:]:
        copy.wait()


def part_kernel(cd_tiles, listed, integrals, split, landed, sems):
    def fetch(k):
        start, column = place_in(listed[0, k], cd_tiles)
        slot = lax.bitwise_and(k, FLIGHT - 1)
        return pltpu.make_async_copy(
            integrals.at[pl.ds(start, TILE), pl.ds(column, TILE)], landed.at[slot], sems.at[slot]
        )

    def begin(round_at, carry):
        for unrolled in range(UNROLL):
            fetch(round_at * UNROLL + unrolled).start()
        return carry

    rounds = listed[1, 0]
    lax.fori_loop(0, jnp.minimum(rounds, AHEAD), begin, 0)

    def part(round_at, carry):
        first = round_at * UNROLL
        for unrolled in range(UNROLL):
            fetch(first + unrolled).wait()
        for unrolled in range(UNROLL):
            k = first + unrolled
            real = jnp.logical_or(k == 0, listed[0, k] > 0)
            tile = jnp.where(real, landed[lax.bitwise_and(k, FLIGHT - 1)], 0.0).T
            upper = tile.astype(jnp.bfloat16)
            split[k, :, :TILE] = upper
            split[k, :, TILE:] = (tile - upper.astype(jnp.float32)).astype(jnp.bfloat16)

        @pl.when(round_at + AHEAD < rounds)
        def _():
            begin(round_at + AHEAD, 0)

        return carry

    lax.fori_loop(0, rounds, part, 0)


def place_in(place, cd_tiles):
    bits = cd_tiles.bit_length() - 1
    if cd_tiles == 1 << bits:
        row, column = lax.shift_right_logical(place, bits), lax.bitwise_and(place, cd_tiles - 1)
    else:
        row, column = lax.div(place, cd_tiles), lax.rem(place, cd_tiles)
    return pl.multiple_of(row * TILE, TILE), pl.multiple_of(column * TILE, TILE)


def products(cd_tiles, listed, split, pieces, total):
    total[...] = jnp.zeros_like(total)

    def some(first, many):
        sums = []
        for unrolled in range(many):
            start, column = place_in(listed[0, first + unrolled], cd_tiles)
            left = jnp.concatenate([piece[0, :, pl.ds(column, TILE)] for piece in pieces], axis=0)
            upper = left.astype(jnp.bfloat16)
            lower = (left - upper.astype(jnp.float32)).astype(jnp.bfloat16)
            tile = split[first + unrolled]
            both = jnp.dot(jnp.concatenate([upper, lower], axis=0), tile, preferred_element_type=jnp.float32)
            high, low = both[: left.shape[0]], both[left.shape[0] :]
            sums.append((start, high[:, :TILE] + (high[:, TILE:] + (low[:, :TILE] + low[:, TILE:]))))
        for start, term in sums:
            total[:, pl.ds(start, TILE)] += term

    def step(at, carry):
        some(at * 2 * UNROLL, 2 * UNROLL)
        return carry

    rounds = listed[1, 0]
    lax.fori_loop(0, lax.shift_right_logical(rounds, 1), step, 0)

    @pl.when(lax.bitwise_and(rounds, 1) == 1)
    def _():
        some((rounds - 1) * UNROLL, UNROLL)


def step_kernel(count, rows, cd_tiles, group, listed, split, *refs):
    pieces = refs[: len(group)]
    mine, send, total = refs[-3:]
    products(cd_tiles, listed, split, pieces, total)
    half = rows * count // 2
    for at, (span, offset) in enumerate(group):
        place = place_of(count, rows, offset)
        block = total[at * rows : (at + 1) * rows, :]

        @pl.when(place < half)
        def _():
            mine[span, pl.ds(pl.multiple_of(place, rows), rows), :] = block

        @pl.when(place >= half)
        def _():
            send[span, pl.ds(pl.multiple_of(place - half, rows), rows), :] = block


def last_kernel(cd_tiles, listed, split, *refs):
    products(cd_tiles, listed, split, refs[:-1], refs[-1])


def merge_kernel(mine, received, out):
    out[...] = mine[...] + received[...]


def final_kernel(count, spans, rows, last, received, before, out, total, sems):
    del before
    place = place_of(count, rows, -(count // 2))

    @pl.when(place < rows * count // 2)
    def _():
        total[...] = last[...] + received[...]
        copies = []
        for span in range(spans):
            for row in range(0, rows, BAND):
                copies.append(
                    pltpu.make_async_copy(
                        total.at[pl.ds(span * rows + row, BAND), :],
                        out.at[span, pl.ds(pl.multiple_of(place + row, BAND), BAND), :],
                        sems.at[len(copies)],
                    )
                )
                copies[-1].start()
        for copy in copies:
            copy.wait()


def solution(mesh):
    count = mesh.shape["ab"]
    grid = grid_of(count)
    far = count // 2
    ahead = [(at_ring(at, *grid), at_ring((at + 1) % count, *grid)) for at in range(count)]
    back = [(to, start) for start, to in ahead]
    swap = [(0, 1), (1, 0)]

    def shards(amplitudes, integrals, ab_irrep, cd_irrep, block_pattern):
        spans, rows, depth = amplitudes.shape
        slab = integrals.shape[0]
        ab_tiles, cd_tiles = block_pattern.shape
        tiles = ab_tiles * cd_tiles
        half = rows * far

        in_hbm = functools.partial(pltpu.with_memory_space_constraint, memory_space=pltpu.HBM)
        smem = pl.BlockSpec(memory_space=pltpu.SMEM)
        vmem = pl.BlockSpec(memory_space=pltpu.VMEM)
        hbm = pl.BlockSpec(memory_space=pltpu.HBM)
        params = pltpu.CompilerParams(vmem_limit_bytes=VMEM_LIMIT)
        piece = pltpu.VMEM((1, rows, depth), jnp.float32)

        *own, listed = pl.pallas_call(
            functools.partial(cut_kernel, ab_tiles, cd_tiles, spans),
            out_shape=(piece,) * spans + (pltpu.VMEM((2, LANES), jnp.int32),),
            in_specs=[hbm] * 4,
            out_specs=(vmem,) * (spans + 1),
            scratch_shapes=[
                pltpu.SMEM(ab_irrep.shape, jnp.int32),
                pltpu.SMEM(cd_irrep.shape, jnp.int32),
                pltpu.VMEM(block_pattern.shape, jnp.int32),
                pltpu.SemaphoreType.DMA((3 + spans * 2 * rows // BAND,)),
            ],
            compiler_params=params,
            name="cut",
        )(*map(in_hbm, (amplitudes, ab_irrep, cd_irrep, block_pattern)))
        split = pl.pallas_call(
            functools.partial(part_kernel, cd_tiles),
            out_shape=pltpu.VMEM((tiles, TILE, 2 * TILE), jnp.bfloat16),
            in_specs=[smem, hbm],
            out_specs=vmem,
            scratch_shapes=[pltpu.VMEM((FLIGHT, TILE, TILE), jnp.float32), pltpu.SemaphoreType.DMA((FLIGHT,))],
            compiler_params=params,
            cost_estimate=pl.CostEstimate(flops=0, bytes_accessed=8 << 20, transcendentals=0),
            name="part",
        )(listed, in_hbm(integrals))

        block = pltpu.VMEM((spans, half, slab), jnp.float32)

        def step(group, parts):
            pieces = [held[key] for key in group]
            return pl.pallas_call(
                functools.partial(step_kernel, count, rows, cd_tiles, group),
                out_shape=(block, block),
                in_specs=[smem] + [vmem] * (1 + len(pieces) + len(parts)),
                out_specs=(vmem, vmem),
                scratch_shapes=[pltpu.VMEM((len(pieces) * rows, slab), jnp.float32)],
                compiler_params=params,
                input_output_aliases={2 + len(pieces): 0, 3 + len(pieces): 1} if parts else {},
                cost_estimate=pl.CostEstimate(flops=STEP_FLOPS, bytes_accessed=4 << 20, transcendentals=0),
                name="step",
            )(listed, split, *pieces, *parts)

        held = {(span, 0): own[span] for span in range(spans)}
        flows = [(span, sign) for long in (True, False) for span in range(spans) for sign in (-1, 1) if ((sign < 0) == (span % 2 == 0)) == long]
        moving = {(span, sign): own[span] for span, sign in flows}
        arrivals, parts = [(span, 0) for span in range(spans)], ()
        for hop in range(1, far + 1):
            for span, sign in flows:
                long = (sign < 0) == (span % 2 == 0)
                if hop < far or long:
                    moved = moving[span, sign]
                    if hop == 2:
                        moved, _ = lax.optimization_barrier((moved, split))
                    if hop == 3 and long:
                        moved, _ = lax.optimization_barrier((moved, parts[0]))
                    moved = moving[span, sign] = lax.ppermute(moved, "ab", ahead if sign < 0 else back)
                    offset = -far if hop == far else sign * hop
                    held[span, offset] = moved
                    if hop < far:
                        arrivals.append((span, offset))
            if hop == 1:
                parts = step(arrivals, parts)
                arrivals = []
        late = len(arrivals) - spans
        for start in range(0, late, GROUP):
            parts = step(arrivals[start : min(start + GROUP, late)], parts)
        parts = step(arrivals[late:], parts)
        mine, send = parts
        base = pl.pallas_call(
            merge_kernel,
            out_shape=pltpu.HBM((spans, half, slab), jnp.float32),
            in_specs=[vmem, vmem],
            out_specs=vmem,
            compiler_params=params,
            name="merge",
        )(mine, lax.ppermute(send, "cd", swap))

        last = pl.pallas_call(
            functools.partial(last_kernel, cd_tiles),
            out_shape=pltpu.VMEM((spans * rows, slab), jnp.float32),
            in_specs=[smem, vmem] + [vmem] * spans,
            out_specs=vmem,
            compiler_params=params,
            cost_estimate=pl.CostEstimate(flops=1 << 34, bytes_accessed=4 << 20, transcendentals=0),
            name="last",
        )(listed, split, *[held[span, -far] for span in range(spans)])
        return pl.pallas_call(
            functools.partial(final_kernel, count, spans, rows),
            out_shape=pltpu.HBM((spans, half, slab), jnp.float32),
            in_specs=[vmem, vmem, hbm],
            out_specs=hbm,
            scratch_shapes=[pltpu.VMEM((spans * rows, slab), jnp.float32), pltpu.SemaphoreType.DMA((spans * rows // BAND,))],
            compiler_params=params,
            input_output_aliases={2: 0},
            name="final",
        )(last, lax.ppermute(last, "cd", swap), base)

    in_specs = (
        P("groups", "ab", "cd"),
        P(("groups", "ab"), "cd"),
        P(("groups", "ab")),
        P(("groups", "cd")),
        P(("groups", "ab"), "cd"),
    )
    out_specs = P("groups", "cd", "ab")
    return jax.shard_map(shards, mesh=mesh, in_specs=in_specs, out_specs=out_specs, check_vma=False)
```

```python
import functools

import jax
import jax.numpy as jnp
from jax import lax
from jax.experimental import pallas as pl
from jax.experimental.pallas import tpu as pltpu
from jax.sharding import PartitionSpec as P

TILE = 128
UNROLL = 4
LANES = 128
AHEAD = 8
FLIGHT = AHEAD * UNROLL
GROUP = 12
STEP_FLOPS = 1 << 30
VMEM_LIMIT = 12 * 2**20


def grid_of(count):
    bits = count.bit_length() - 1
    if count != 1 << bits or bits < 2:
        return count, 1
    rows = 1 << ((bits + 1) // 2)
    return rows, count // rows


def at_ring(place, rows, columns):
    if columns == 1:
        return place
    wide = columns - 1
    beyond = place - rows
    line = beyond // wide
    step = beyond - line * wide
    even = (line % 2) == 0
    if isinstance(place, int):
        back = (rows - 1 - line) * columns + (1 + step if even else columns - 1 - step)
        return place * columns if place < rows else back
    back = (rows - 1 - line) * columns + jnp.where(even, 1 + step, columns - 1 - step)
    return jnp.where(place < rows, place * columns, back)


def ring_of(index, rows, columns):
    if columns == 1:
        return index
    wide = columns - 1
    row = index // columns
    column = index - row * columns
    line = rows - 1 - row
    step = jnp.where((line % 2) == 0, column - 1, columns - 1 - column)
    return jnp.where(column == 0, row, rows + line * wide + step)


def place_of(count, rows, offset):
    grid = grid_of(count)
    here = ring_of(lax.axis_index("ab"), *grid)
    whole = rows * count
    start = at_ring((here + offset + count) % count, *grid) * rows + lax.axis_index("cd") * (whole // 2)
    return jnp.where(start >= whole, start - whole, start)


def cut_kernel(amplitudes, *refs):
    *refs, sems = refs
    labels, outs = refs[:3], refs[3:]
    spans = len(outs) - 3
    pairs = [(amplitudes.at[pl.ds(at, 1)], outs[at]) for at in range(spans)]
    pairs += list(zip(labels, outs[spans:]))
    copies = [pltpu.make_async_copy(start, end, sems.at[at]) for at, (start, end) in enumerate(pairs)]
    for copy in copies:
        copy.start()
    for copy in copies:
        copy.wait()


def part_kernel(ab_tiles, cd_tiles, ab_irrep, cd_irrep, pattern, integrals, listed, split, near, landed, near_sem, sems):
    shape = (ab_tiles, LANES)
    lane = lax.broadcasted_iota(jnp.int32, shape, 1)
    line = lax.broadcasted_iota(jnp.int32, shape, 0)
    rows = jnp.full(shape, -1, jnp.int32)
    columns = jnp.full(shape, -2, jnp.int32)
    for p in range(ab_tiles):
        rows = jnp.where(line == p, ab_irrep[p], rows)
    for q in range(cd_tiles):
        columns = jnp.where(lane == q, cd_irrep[q], columns)
    stored = jnp.concatenate([pattern[...], jnp.zeros((ab_tiles, LANES - cd_tiles), jnp.int32)], axis=1)
    keep = jnp.where(jnp.logical_and(stored == 1, rows == columns), 1.0, 0.0)

    upto = keep
    reach = 1
    while reach < cd_tiles:
        upto += jnp.where(lane >= reach, pltpu.roll(upto, reach, 1), 0.0)
        reach *= 2
    whole = jnp.broadcast_to(jnp.sum(keep, axis=1, keepdims=True), shape)
    before = whole
    reach = 1
    while reach < ab_tiles:
        before += jnp.where(line >= reach, pltpu.roll(before, reach, 0), 0.0)
        reach *= 2
    found = before[ab_tiles - 1 :, :]
    upto += before - whole

    turned = upto.T
    order = lax.broadcasted_iota(jnp.int32, (cd_tiles, LANES), 1).astype(jnp.float32)
    passed = jnp.zeros((cd_tiles, LANES), jnp.float32)
    for p in range(ab_tiles):
        passed += jnp.where(turned[:cd_tiles, p : p + 1] <= order, 1.0, 0.0)
    places = jnp.sum(passed, axis=0, keepdims=True)
    listed[0:1, :] = jnp.where(order[0:1, :] < found, places, 0.0).astype(jnp.int32)
    listed[1:2, :] = ((found + (UNROLL - 1)) * (1.0 / UNROLL)).astype(jnp.int32)
    copy = pltpu.make_async_copy(listed, near, near_sem)
    copy.start()
    copy.wait()

    def fetch(k):
        start, column = place_in(near[0, k], cd_tiles)
        slot = lax.bitwise_and(k, FLIGHT - 1)
        return pltpu.make_async_copy(
            integrals.at[pl.ds(start, TILE), pl.ds(column, TILE)], landed.at[slot], sems.at[slot]
        )

    def begin(round_at, carry):
        for unrolled in range(UNROLL):
            fetch(round_at * UNROLL + unrolled).start()
        return carry

    rounds = near[1, 0]
    lax.fori_loop(0, jnp.minimum(rounds, AHEAD), begin, 0)

    def part(round_at, carry):
        first = round_at * UNROLL
        for unrolled in range(UNROLL):
            fetch(first + unrolled).wait()
        for unrolled in range(UNROLL):
            k = first + unrolled
            real = jnp.logical_or(k == 0, near[0, k] > 0)
            tile = jnp.where(real, landed[lax.bitwise_and(k, FLIGHT - 1)], 0.0).T
            upper = tile.astype(jnp.bfloat16)
            split[k, :, :TILE] = upper
            split[k, :, TILE:] = (tile - upper.astype(jnp.float32)).astype(jnp.bfloat16)

        @pl.when(round_at + AHEAD < rounds)
        def _():
            begin(round_at + AHEAD, 0)

        return carry

    lax.fori_loop(0, rounds, part, 0)


def place_in(place, cd_tiles):
    bits = cd_tiles.bit_length() - 1
    if cd_tiles == 1 << bits:
        row, column = lax.shift_right_logical(place, bits), lax.bitwise_and(place, cd_tiles - 1)
    else:
        row, column = lax.div(place, cd_tiles), lax.rem(place, cd_tiles)
    return pl.multiple_of(row * TILE, TILE), pl.multiple_of(column * TILE, TILE)


def products(cd_tiles, listed, split, pieces, total):
    total[...] = jnp.zeros_like(total)

    def some(first, many):
        sums = []
        for unrolled in range(many):
            start, column = place_in(listed[0, first + unrolled], cd_tiles)
            left = jnp.concatenate([piece[0, :, pl.ds(column, TILE)] for piece in pieces], axis=0)
            upper = left.astype(jnp.bfloat16)
            lower = (left - upper.astype(jnp.float32)).astype(jnp.bfloat16)
            tile = split[first + unrolled]
            both = jnp.dot(jnp.concatenate([upper, lower], axis=0), tile, preferred_element_type=jnp.float32)
            high, low = both[: left.shape[0]], both[left.shape[0] :]
            sums.append((start, high[:, :TILE] + (high[:, TILE:] + (low[:, :TILE] + low[:, TILE:]))))
        for start, term in sums:
            total[:, pl.ds(start, TILE)] += term

    def step(at, carry):
        some(at * 2 * UNROLL, 2 * UNROLL)
        return carry

    rounds = listed[1, 0]
    lax.fori_loop(0, lax.shift_right_logical(rounds, 1), step, 0)

    @pl.when(lax.bitwise_and(rounds, 1) == 1)
    def _():
        some((rounds - 1) * UNROLL, UNROLL)


def step_kernel(count, rows, cd_tiles, group, listed, split, *refs):
    pieces = refs[: len(group)]
    mine, send, total = refs[-3:]
    products(cd_tiles, listed, split, pieces, total)
    half = rows * count // 2
    for at, (span, offset) in enumerate(group):
        place = place_of(count, rows, offset)
        block = total[at * rows : (at + 1) * rows, :]

        @pl.when(place < half)
        def _():
            mine[span, pl.ds(pl.multiple_of(place, rows), rows), :] = block

        @pl.when(place >= half)
        def _():
            send[span, pl.ds(pl.multiple_of(place - half, rows), rows), :] = block


def last_kernel(cd_tiles, listed, split, *refs):
    products(cd_tiles, listed, split, refs[:-1], refs[-1])


def merge_kernel(mine, received, out):
    out[...] = mine[...] + received[...]


def final_kernel(count, spans, rows, last, received, before, out, total, sems):
    del before
    place = place_of(count, rows, -(count // 2))

    @pl.when(place < rows * count // 2)
    def _():
        total[...] = last[...] + received[...]
        copies = []
        for span in range(spans):
            copies.append(
                pltpu.make_async_copy(
                    total.at[pl.ds(span * rows, rows), :],
                    out.at[span, pl.ds(pl.multiple_of(place, rows), rows), :],
                    sems.at[span],
                )
            )
            copies[-1].start()
        for copy in copies:
            copy.wait()


def solution(mesh):
    count = mesh.shape["ab"]
    grid = grid_of(count)
    far = count // 2
    ahead = [(at_ring(at, *grid), at_ring((at + 1) % count, *grid)) for at in range(count)]
    back = [(to, start) for start, to in ahead]
    swap = [(0, 1), (1, 0)]

    def shards(amplitudes, integrals, ab_irrep, cd_irrep, block_pattern):
        spans, rows, depth = amplitudes.shape
        slab = integrals.shape[0]
        ab_tiles, cd_tiles = block_pattern.shape
        tiles = ab_tiles * cd_tiles
        half = rows * far

        in_hbm = functools.partial(pltpu.with_memory_space_constraint, memory_space=pltpu.HBM)
        smem = pl.BlockSpec(memory_space=pltpu.SMEM)
        vmem = pl.BlockSpec(memory_space=pltpu.VMEM)
        hbm = pl.BlockSpec(memory_space=pltpu.HBM)
        params = pltpu.CompilerParams(vmem_limit_bytes=VMEM_LIMIT)
        piece = pltpu.VMEM((1, rows, depth), jnp.float32)

        labels = (ab_irrep, cd_irrep, block_pattern)
        *own, near_ab, near_cd, near_pattern = pl.pallas_call(
            cut_kernel,
            out_shape=(piece,) * spans + tuple(pltpu.VMEM(label.shape, label.dtype) for label in labels),
            in_specs=[hbm] * 4,
            out_specs=(vmem,) * (spans + 3),
            scratch_shapes=[pltpu.SemaphoreType.DMA((spans + 3,))],
            compiler_params=params,
            name="cut",
        )(in_hbm(amplitudes), *map(in_hbm, labels))
        listed, split = pl.pallas_call(
            functools.partial(part_kernel, ab_tiles, cd_tiles),
            out_shape=(
                pltpu.VMEM((2, LANES), jnp.int32),
                pltpu.VMEM((tiles, TILE, 2 * TILE), jnp.bfloat16),
            ),
            in_specs=[smem, smem, vmem, hbm],
            out_specs=(vmem, vmem),
            scratch_shapes=[
                pltpu.SMEM((2, LANES), jnp.int32),
                pltpu.VMEM((FLIGHT, TILE, TILE), jnp.float32),
                pltpu.SemaphoreType.DMA,
                pltpu.SemaphoreType.DMA((FLIGHT,)),
            ],
            compiler_params=params,
            cost_estimate=pl.CostEstimate(flops=0, bytes_accessed=8 << 20, transcendentals=0),
            name="part",
        )(near_ab, near_cd, near_pattern, in_hbm(integrals))

        block = pltpu.VMEM((spans, half, slab), jnp.float32)

        def step(group, parts):
            pieces = [held[key] for key in group]
            return pl.pallas_call(
                functools.partial(step_kernel, count, rows, cd_tiles, group),
                out_shape=(block, block),
                in_specs=[smem] + [vmem] * (1 + len(pieces) + len(parts)),
                out_specs=(vmem, vmem),
                scratch_shapes=[pltpu.VMEM((len(pieces) * rows, slab), jnp.float32)],
                compiler_params=params,
                input_output_aliases={2 + len(pieces): 0, 3 + len(pieces): 1} if parts else {},
                cost_estimate=pl.CostEstimate(flops=STEP_FLOPS, bytes_accessed=4 << 20, transcendentals=0),
                name="step",
            )(listed, split, *pieces, *parts)

        held = {(span, 0): own[span] for span in range(spans)}
        flows = [(span, sign) for long in (True, False) for span in range(spans) for sign in (-1, 1) if ((sign < 0) == (span % 2 == 0)) == long]
        moving = {(span, sign): own[span] for span, sign in flows}
        arrivals, parts = [(span, 0) for span in range(spans)], ()
        for hop in range(1, far + 1):
            for span, sign in flows:
                long = (sign < 0) == (span % 2 == 0)
                if hop < far or long:
                    moved = moving[span, sign]
                    if hop == 2:
                        moved, _ = lax.optimization_barrier((moved, split))
                    if hop == 3 and long:
                        moved, _ = lax.optimization_barrier((moved, parts[0]))
                    moved = moving[span, sign] = lax.ppermute(moved, "ab", ahead if sign < 0 else back)
                    offset = -far if hop == far else sign * hop
                    held[span, offset] = moved
                    if hop < far:
                        arrivals.append((span, offset))
            if hop == 1:
                parts = step(arrivals, parts)
                arrivals = []
        late = len(arrivals) - spans
        for start in range(0, late, GROUP):
            parts = step(arrivals[start : min(start + GROUP, late)], parts)
        parts = step(arrivals[late:], parts)
        mine, send = parts
        base = pl.pallas_call(
            merge_kernel,
            out_shape=pltpu.HBM((spans, half, slab), jnp.float32),
            in_specs=[vmem, vmem],
            out_specs=vmem,
            compiler_params=params,
            name="merge",
        )(mine, lax.ppermute(send, "cd", swap))

        last = pl.pallas_call(
            functools.partial(last_kernel, cd_tiles),
            out_shape=pltpu.VMEM((spans * rows, slab), jnp.float32),
            in_specs=[smem, vmem] + [vmem] * spans,
            out_specs=vmem,
            compiler_params=params,
            cost_estimate=pl.CostEstimate(flops=1 << 34, bytes_accessed=4 << 20, transcendentals=0),
            name="last",
        )(listed, split, *[held[span, -far] for span in range(spans)])
        return pl.pallas_call(
            functools.partial(final_kernel, count, spans, rows),
            out_shape=pltpu.HBM((spans, half, slab), jnp.float32),
            in_specs=[vmem, vmem, hbm],
            out_specs=hbm,
            scratch_shapes=[pltpu.VMEM((spans * rows, slab), jnp.float32), pltpu.SemaphoreType.DMA((spans,))],
            compiler_params=params,
            input_output_aliases={2: 0},
            name="final",
        )(last, lax.ppermute(last, "cd", swap), base)

    in_specs = (
        P("groups", "ab", "cd"),
        P(("groups", "ab"), "cd"),
        P(("groups", "ab")),
        P(("groups", "cd")),
        P(("groups", "ab"), "cd"),
    )
    out_specs = P("groups", "cd", "ab")
    return jax.shard_map(shards, mesh=mesh, in_specs=in_specs, out_specs=out_specs, check_vma=False)
```

```python
import functools

import jax
import jax.numpy as jnp
from jax import lax
from jax.experimental import pallas as pl
from jax.experimental.pallas import tpu as pltpu
from jax.sharding import PartitionSpec as P

TILE = 128
UNROLL = 4
LANES = 128
AHEAD = 8
FLIGHT = AHEAD * UNROLL
GROUP = 12
STEP_FLOPS = 1 << 30
VMEM_LIMIT = 12 * 2**20


def grid_of(count):
    bits = count.bit_length() - 1
    if count != 1 << bits or bits < 2:
        return count, 1
    rows = 1 << ((bits + 1) // 2)
    return rows, count // rows


def at_ring(place, rows, columns):
    if columns == 1:
        return place
    wide = columns - 1
    beyond = place - rows
    line = beyond // wide
    step = beyond - line * wide
    even = (line % 2) == 0
    if isinstance(place, int):
        back = (rows - 1 - line) * columns + (1 + step if even else columns - 1 - step)
        return place * columns if place < rows else back
    back = (rows - 1 - line) * columns + jnp.where(even, 1 + step, columns - 1 - step)
    return jnp.where(place < rows, place * columns, back)


def ring_of(index, rows, columns):
    if columns == 1:
        return index
    wide = columns - 1
    row = index // columns
    column = index - row * columns
    line = rows - 1 - row
    step = jnp.where((line % 2) == 0, column - 1, columns - 1 - column)
    return jnp.where(column == 0, row, rows + line * wide + step)


def place_of(count, rows, offset):
    grid = grid_of(count)
    here = ring_of(lax.axis_index("ab"), *grid)
    whole = rows * count
    start = at_ring((here + offset + count) % count, *grid) * rows + lax.axis_index("cd") * (whole // 2)
    return jnp.where(start >= whole, start - whole, start)


def cut_kernel(ab_tiles, cd_tiles, spans, amplitudes, labels_ab, labels_cd, labels_pattern, *refs):
    outs, (listed, ab_irrep, cd_irrep, pattern, sems) = refs[:spans], refs[spans:]
    pairs = [(labels_ab, ab_irrep), (labels_cd, cd_irrep), (labels_pattern, pattern)]
    pairs += [(amplitudes.at[pl.ds(at, 1)], out) for at, out in enumerate(outs)]
    copies = [pltpu.make_async_copy(start, end, sems.at[at]) for at, (start, end) in enumerate(pairs)]
    for at, copy in enumerate(copies):
        copy.start(priority=at % 2)
    for copy in copies[:3]:
        copy.wait()

    shape = (ab_tiles, LANES)
    lane = lax.broadcasted_iota(jnp.int32, shape, 1)
    line = lax.broadcasted_iota(jnp.int32, shape, 0)
    rows = jnp.full(shape, -1, jnp.int32)
    columns = jnp.full(shape, -2, jnp.int32)
    for p in range(ab_tiles):
        rows = jnp.where(line == p, ab_irrep[p], rows)
    for q in range(cd_tiles):
        columns = jnp.where(lane == q, cd_irrep[q], columns)
    stored = jnp.concatenate([pattern[...], jnp.zeros((ab_tiles, LANES - cd_tiles), jnp.int32)], axis=1)
    keep = jnp.where(jnp.logical_and(stored == 1, rows == columns), 1.0, 0.0)

    upto = keep
    reach = 1
    while reach < cd_tiles:
        upto += jnp.where(lane >= reach, pltpu.roll(upto, reach, 1), 0.0)
        reach *= 2
    whole = jnp.broadcast_to(jnp.sum(keep, axis=1, keepdims=True), shape)
    before = whole
    reach = 1
    while reach < ab_tiles:
        before += jnp.where(line >= reach, pltpu.roll(before, reach, 0), 0.0)
        reach *= 2
    found = before[ab_tiles - 1 :, :]
    upto += before - whole

    turned = upto.T
    order = lax.broadcasted_iota(jnp.int32, (cd_tiles, LANES), 1).astype(jnp.float32)
    passed = jnp.zeros((cd_tiles, LANES), jnp.float32)
    for p in range(ab_tiles):
        passed += jnp.where(turned[:cd_tiles, p : p + 1] <= order, 1.0, 0.0)
    places = jnp.sum(passed, axis=0, keepdims=True)
    listed[0:1, :] = jnp.where(order[0:1, :] < found, places, 0.0).astype(jnp.int32)
    listed[1:2, :] = ((found + (UNROLL - 1)) * (1.0 / UNROLL)).astype(jnp.int32)
    for copy in copies[3:]:
        copy.wait()


def part_kernel(cd_tiles, listed, integrals, split, landed, sems):
    def fetch(k):
        start, column = place_in(listed[0, k], cd_tiles)
        slot = lax.bitwise_and(k, FLIGHT - 1)
        return pltpu.make_async_copy(
            integrals.at[pl.ds(start, TILE), pl.ds(column, TILE)], landed.at[slot], sems.at[slot]
        )

    def begin(round_at, carry):
        for unrolled in range(UNROLL):
            fetch(round_at * UNROLL + unrolled).start(priority=unrolled % 2)
        return carry

    rounds = listed[1, 0]
    lax.fori_loop(0, jnp.minimum(rounds, AHEAD), begin, 0)

    def part(round_at, carry):
        first = round_at * UNROLL
        for unrolled in range(UNROLL):
            fetch(first + unrolled).wait()
        for unrolled in range(UNROLL):
            k = first + unrolled
            real = jnp.logical_or(k == 0, listed[0, k] > 0)
            tile = jnp.where(real, landed[lax.bitwise_and(k, FLIGHT - 1)], 0.0).T
            upper = tile.astype(jnp.bfloat16)
            split[k, :, :TILE] = upper
            split[k, :, TILE:] = (tile - upper.astype(jnp.float32)).astype(jnp.bfloat16)

        @pl.when(round_at + AHEAD < rounds)
        def _():
            begin(round_at + AHEAD, 0)

        return carry

    lax.fori_loop(0, rounds, part, 0)


def place_in(place, cd_tiles):
    bits = cd_tiles.bit_length() - 1
    if cd_tiles == 1 << bits:
        row, column = lax.shift_right_logical(place, bits), lax.bitwise_and(place, cd_tiles - 1)
    else:
        row, column = lax.div(place, cd_tiles), lax.rem(place, cd_tiles)
    return pl.multiple_of(row * TILE, TILE), pl.multiple_of(column * TILE, TILE)


def products(cd_tiles, listed, split, pieces, total):
    total[...] = jnp.zeros_like(total)

    def some(first, many):
        sums = []
        for unrolled in range(many):
            start, column = place_in(listed[0, first + unrolled], cd_tiles)
            left = jnp.concatenate([piece[0, :, pl.ds(column, TILE)] for piece in pieces], axis=0)
            upper = left.astype(jnp.bfloat16)
            lower = (left - upper.astype(jnp.float32)).astype(jnp.bfloat16)
            tile = split[first + unrolled]
            both = jnp.dot(jnp.concatenate([upper, lower], axis=0), tile, preferred_element_type=jnp.float32)
            high, low = both[: left.shape[0]], both[left.shape[0] :]
            sums.append((start, high[:, :TILE] + (high[:, TILE:] + (low[:, :TILE] + low[:, TILE:]))))
        for start, term in sums:
            total[:, pl.ds(start, TILE)] += term

    def step(at, carry):
        some(at * 2 * UNROLL, 2 * UNROLL)
        return carry

    rounds = listed[1, 0]
    lax.fori_loop(0, lax.shift_right_logical(rounds, 1), step, 0)

    @pl.when(lax.bitwise_and(rounds, 1) == 1)
    def _():
        some((rounds - 1) * UNROLL, UNROLL)


def step_kernel(count, rows, cd_tiles, group, listed, split, *refs):
    pieces = refs[: len(group)]
    mine, send, total = refs[-3:]
    products(cd_tiles, listed, split, pieces, total)
    half = rows * count // 2
    for at, (span, offset) in enumerate(group):
        place = place_of(count, rows, offset)
        block = total[at * rows : (at + 1) * rows, :]

        @pl.when(place < half)
        def _():
            mine[span, pl.ds(pl.multiple_of(place, rows), rows), :] = block

        @pl.when(place >= half)
        def _():
            send[span, pl.ds(pl.multiple_of(place - half, rows), rows), :] = block


def last_kernel(cd_tiles, listed, split, *refs):
    products(cd_tiles, listed, split, refs[:-1], refs[-1])


def merge_kernel(mine, received, out):
    out[...] = mine[...] + received[...]


def final_kernel(count, spans, rows, last, received, before, out, total, sems):
    del before
    place = place_of(count, rows, -(count // 2))

    @pl.when(place < rows * count // 2)
    def _():
        total[...] = last[...] + received[...]
        copies = []
        for span in range(spans):
            copies.append(
                pltpu.make_async_copy(
                    total.at[pl.ds(span * rows, rows), :],
                    out.at[span, pl.ds(pl.multiple_of(place, rows), rows), :],
                    sems.at[span],
                )
            )
            copies[-1].start()
        for copy in copies:
            copy.wait()


def solution(mesh):
    count = mesh.shape["ab"]
    grid = grid_of(count)
    far = count // 2
    ahead = [(at_ring(at, *grid), at_ring((at + 1) % count, *grid)) for at in range(count)]
    back = [(to, start) for start, to in ahead]
    swap = [(0, 1), (1, 0)]

    def shards(amplitudes, integrals, ab_irrep, cd_irrep, block_pattern):
        spans, rows, depth = amplitudes.shape
        slab = integrals.shape[0]
        ab_tiles, cd_tiles = block_pattern.shape
        tiles = ab_tiles * cd_tiles
        half = rows * far

        in_hbm = functools.partial(pltpu.with_memory_space_constraint, memory_space=pltpu.HBM)
        smem = pl.BlockSpec(memory_space=pltpu.SMEM)
        vmem = pl.BlockSpec(memory_space=pltpu.VMEM)
        hbm = pl.BlockSpec(memory_space=pltpu.HBM)
        params = pltpu.CompilerParams(vmem_limit_bytes=VMEM_LIMIT)
        piece = pltpu.VMEM((1, rows, depth), jnp.float32)

        *own, listed = pl.pallas_call(
            functools.partial(cut_kernel, ab_tiles, cd_tiles, spans),
            out_shape=(piece,) * spans + (pltpu.VMEM((2, LANES), jnp.int32),),
            in_specs=[hbm] * 4,
            out_specs=(vmem,) * (spans + 1),
            scratch_shapes=[
                pltpu.SMEM(ab_irrep.shape, jnp.int32),
                pltpu.SMEM(cd_irrep.shape, jnp.int32),
                pltpu.VMEM(block_pattern.shape, jnp.int32),
                pltpu.SemaphoreType.DMA((spans + 3,)),
            ],
            compiler_params=params,
            name="cut",
        )(*map(in_hbm, (amplitudes, ab_irrep, cd_irrep, block_pattern)))
        split = pl.pallas_call(
            functools.partial(part_kernel, cd_tiles),
            out_shape=pltpu.VMEM((tiles, TILE, 2 * TILE), jnp.bfloat16),
            in_specs=[smem, hbm],
            out_specs=vmem,
            scratch_shapes=[pltpu.VMEM((FLIGHT, TILE, TILE), jnp.float32), pltpu.SemaphoreType.DMA((FLIGHT,))],
            compiler_params=params,
            cost_estimate=pl.CostEstimate(flops=0, bytes_accessed=8 << 20, transcendentals=0),
            name="part",
        )(listed, in_hbm(integrals))

        block = pltpu.VMEM((spans, half, slab), jnp.float32)

        def step(group, parts):
            pieces = [held[key] for key in group]
            return pl.pallas_call(
                functools.partial(step_kernel, count, rows, cd_tiles, group),
                out_shape=(block, block),
                in_specs=[smem] + [vmem] * (1 + len(pieces) + len(parts)),
                out_specs=(vmem, vmem),
                scratch_shapes=[pltpu.VMEM((len(pieces) * rows, slab), jnp.float32)],
                compiler_params=params,
                input_output_aliases={2 + len(pieces): 0, 3 + len(pieces): 1} if parts else {},
                cost_estimate=pl.CostEstimate(flops=STEP_FLOPS, bytes_accessed=4 << 20, transcendentals=0),
                name="step",
            )(listed, split, *pieces, *parts)

        held = {(span, 0): own[span] for span in range(spans)}
        flows = [(span, sign) for long in (True, False) for span in range(spans) for sign in (-1, 1) if ((sign < 0) == (span % 2 == 0)) == long]
        moving = {(span, sign): own[span] for span, sign in flows}
        arrivals, parts = [(span, 0) for span in range(spans)], ()
        for hop in range(1, far + 1):
            for span, sign in flows:
                long = (sign < 0) == (span % 2 == 0)
                if hop < far or long:
                    moved = moving[span, sign]
                    if hop == 2:
                        moved, _ = lax.optimization_barrier((moved, split))
                    if hop == 3 and long:
                        moved, _ = lax.optimization_barrier((moved, parts[0]))
                    moved = moving[span, sign] = lax.ppermute(moved, "ab", ahead if sign < 0 else back)
                    offset = -far if hop == far else sign * hop
                    held[span, offset] = moved
                    if hop < far:
                        arrivals.append((span, offset))
            if hop == 1:
                parts = step(arrivals, parts)
                arrivals = []
        late = len(arrivals) - spans
        for start in range(0, late, GROUP):
            parts = step(arrivals[start : min(start + GROUP, late)], parts)
        parts = step(arrivals[late:], parts)
        mine, send = parts
        base = pl.pallas_call(
            merge_kernel,
            out_shape=pltpu.HBM((spans, half, slab), jnp.float32),
            in_specs=[vmem, vmem],
            out_specs=vmem,
            compiler_params=params,
            name="merge",
        )(mine, lax.ppermute(send, "cd", swap))

        last = pl.pallas_call(
            functools.partial(last_kernel, cd_tiles),
            out_shape=pltpu.VMEM((spans * rows, slab), jnp.float32),
            in_specs=[smem, vmem] + [vmem] * spans,
            out_specs=vmem,
            compiler_params=params,
            cost_estimate=pl.CostEstimate(flops=1 << 34, bytes_accessed=4 << 20, transcendentals=0),
            name="last",
        )(listed, split, *[held[span, -far] for span in range(spans)])
        return pl.pallas_call(
            functools.partial(final_kernel, count, spans, rows),
            out_shape=pltpu.HBM((spans, half, slab), jnp.float32),
            in_specs=[vmem, vmem, hbm],
            out_specs=hbm,
            scratch_shapes=[pltpu.VMEM((spans * rows, slab), jnp.float32), pltpu.SemaphoreType.DMA((spans,))],
            compiler_params=params,
            input_output_aliases={2: 0},
            name="final",
        )(last, lax.ppermute(last, "cd", swap), base)

    in_specs = (
        P("groups", "ab", "cd"),
        P(("groups", "ab"), "cd"),
        P(("groups", "ab")),
        P(("groups", "cd")),
        P(("groups", "ab"), "cd"),
    )
    out_specs = P("groups", "cd", "ab")
    return jax.shard_map(shards, mesh=mesh, in_specs=in_specs, out_specs=out_specs, check_vma=False)
```

```python
import functools

import jax
import jax.numpy as jnp
from jax import lax
from jax.experimental import pallas as pl
from jax.experimental.pallas import tpu as pltpu
from jax.sharding import PartitionSpec as P

TILE = 128
UNROLL = 8
LANES = 128
AHEAD = 4
FLIGHT = AHEAD * UNROLL
GROUP = 12
STEP_FLOPS = 1 << 30
VMEM_LIMIT = 12 * 2**20


def grid_of(count):
    bits = count.bit_length() - 1
    if count != 1 << bits or bits < 2:
        return count, 1
    rows = 1 << ((bits + 1) // 2)
    return rows, count // rows


def at_ring(place, rows, columns):
    if columns == 1:
        return place
    wide = columns - 1
    beyond = place - rows
    line = beyond // wide
    step = beyond - line * wide
    even = (line % 2) == 0
    if isinstance(place, int):
        back = (rows - 1 - line) * columns + (1 + step if even else columns - 1 - step)
        return place * columns if place < rows else back
    back = (rows - 1 - line) * columns + jnp.where(even, 1 + step, columns - 1 - step)
    return jnp.where(place < rows, place * columns, back)


def ring_of(index, rows, columns):
    if columns == 1:
        return index
    wide = columns - 1
    row = index // columns
    column = index - row * columns
    line = rows - 1 - row
    step = jnp.where((line % 2) == 0, column - 1, columns - 1 - column)
    return jnp.where(column == 0, row, rows + line * wide + step)


def place_of(count, rows, offset):
    grid = grid_of(count)
    here = ring_of(lax.axis_index("ab"), *grid)
    whole = rows * count
    start = at_ring((here + offset + count) % count, *grid) * rows + lax.axis_index("cd") * (whole // 2)
    return jnp.where(start >= whole, start - whole, start)


def cut_kernel(ab_tiles, cd_tiles, spans, amplitudes, labels_ab, labels_cd, labels_pattern, *refs):
    outs, (listed, ab_irrep, cd_irrep, pattern, sems) = refs[:spans], refs[spans:]
    pairs = [(labels_ab, ab_irrep), (labels_cd, cd_irrep), (labels_pattern, pattern)]
    pairs += [(amplitudes.at[pl.ds(at, 1)], out) for at, out in enumerate(outs)]
    copies = [pltpu.make_async_copy(start, end, sems.at[at]) for at, (start, end) in enumerate(pairs)]
    for copy in copies:
        copy.start()
    for copy in copies[:3]:
        copy.wait()

    shape = (ab_tiles, LANES)
    lane = lax.broadcasted_iota(jnp.int32, shape, 1)
    line = lax.broadcasted_iota(jnp.int32, shape, 0)
    rows = jnp.full(shape, -1, jnp.int32)
    columns = jnp.full(shape, -2, jnp.int32)
    for p in range(ab_tiles):
        rows = jnp.where(line == p, ab_irrep[p], rows)
    for q in range(cd_tiles):
        columns = jnp.where(lane == q, cd_irrep[q], columns)
    stored = jnp.concatenate([pattern[...], jnp.zeros((ab_tiles, LANES - cd_tiles), jnp.int32)], axis=1)
    keep = jnp.where(jnp.logical_and(stored == 1, rows == columns), 1.0, 0.0)

    upto = keep
    reach = 1
    while reach < cd_tiles:
        upto += jnp.where(lane >= reach, pltpu.roll(upto, reach, 1), 0.0)
        reach *= 2
    whole = jnp.broadcast_to(jnp.sum(keep, axis=1, keepdims=True), shape)
    before = whole
    reach = 1
    while reach < ab_tiles:
        before += jnp.where(line >= reach, pltpu.roll(before, reach, 0), 0.0)
        reach *= 2
    found = before[ab_tiles - 1 :, :]
    upto += before - whole

    turned = upto.T
    order = lax.broadcasted_iota(jnp.int32, (cd_tiles, LANES), 1).astype(jnp.float32)
    passed = jnp.zeros((cd_tiles, LANES), jnp.float32)
    for p in range(ab_tiles):
        passed += jnp.where(turned[:cd_tiles, p : p + 1] <= order, 1.0, 0.0)
    places = jnp.sum(passed, axis=0, keepdims=True)
    listed[0:1, :] = jnp.where(order[0:1, :] < found, places, 0.0).astype(jnp.int32)
    listed[1:2, :] = ((found + (UNROLL - 1)) * (1.0 / UNROLL)).astype(jnp.int32)
    for copy in copies[3:]:
        copy.wait()


def part_kernel(cd_tiles, listed, integrals, split, landed, sems):
    def fetch(k):
        start, column = place_in(listed[0, k], cd_tiles)
        slot = lax.bitwise_and(k, FLIGHT - 1)
        return pltpu.make_async_copy(
            integrals.at[pl.ds(start, TILE), pl.ds(column, TILE)], landed.at[slot], sems.at[slot]
        )

    def begin(round_at, carry):
        for unrolled in range(UNROLL):
            fetch(round_at * UNROLL + unrolled).start()
        return carry

    rounds = listed[1, 0]
    lax.fori_loop(0, jnp.minimum(rounds, AHEAD), begin, 0)

    def part(round_at, carry):
        first = round_at * UNROLL
        for unrolled in range(UNROLL):
            fetch(first + unrolled).wait()
        for unrolled in range(UNROLL):
            k = first + unrolled
            real = jnp.logical_or(k == 0, listed[0, k] > 0)
            tile = jnp.where(real, landed[lax.bitwise_and(k, FLIGHT - 1)], 0.0).T
            upper = tile.astype(jnp.bfloat16)
            split[k, :, :TILE] = upper
            split[k, :, TILE:] = (tile - upper.astype(jnp.float32)).astype(jnp.bfloat16)

        @pl.when(round_at + AHEAD < rounds)
        def _():
            begin(round_at + AHEAD, 0)

        return carry

    lax.fori_loop(0, rounds, part, 0)


def place_in(place, cd_tiles):
    bits = cd_tiles.bit_length() - 1
    if cd_tiles == 1 << bits:
        row, column = lax.shift_right_logical(place, bits), lax.bitwise_and(place, cd_tiles - 1)
    else:
        row, column = lax.div(place, cd_tiles), lax.rem(place, cd_tiles)
    return pl.multiple_of(row * TILE, TILE), pl.multiple_of(column * TILE, TILE)


def products(cd_tiles, listed, split, pieces, total):
    total[...] = jnp.zeros_like(total)

    def some(first, many):
        sums = []
        for unrolled in range(many):
            start, column = place_in(listed[0, first + unrolled], cd_tiles)
            left = jnp.concatenate([piece[0, :, pl.ds(column, TILE)] for piece in pieces], axis=0)
            upper = left.astype(jnp.bfloat16)
            lower = (left - upper.astype(jnp.float32)).astype(jnp.bfloat16)
            tile = split[first + unrolled]
            both = jnp.dot(jnp.concatenate([upper, lower], axis=0), tile, preferred_element_type=jnp.float32)
            high, low = both[: left.shape[0]], both[left.shape[0] :]
            sums.append((start, high[:, :TILE] + (high[:, TILE:] + (low[:, :TILE] + low[:, TILE:]))))
        for start, term in sums:
            total[:, pl.ds(start, TILE)] += term

    def step(at, carry):
        some(at * 2 * UNROLL, 2 * UNROLL)
        return carry

    rounds = listed[1, 0]
    lax.fori_loop(0, lax.shift_right_logical(rounds, 1), step, 0)

    @pl.when(lax.bitwise_and(rounds, 1) == 1)
    def _():
        some((rounds - 1) * UNROLL, UNROLL)


def step_kernel(count, rows, cd_tiles, group, listed, split, *refs):
    pieces = refs[: len(group)]
    mine, send, total = refs[-3:]
    products(cd_tiles, listed, split, pieces, total)
    half = rows * count // 2
    for at, (span, offset) in enumerate(group):
        place = place_of(count, rows, offset)
        block = total[at * rows : (at + 1) * rows, :]

        @pl.when(place < half)
        def _():
            mine[span, pl.ds(pl.multiple_of(place, rows), rows), :] = block

        @pl.when(place >= half)
        def _():
            send[span, pl.ds(pl.multiple_of(place - half, rows), rows), :] = block


def last_kernel(cd_tiles, listed, split, *refs):
    products(cd_tiles, listed, split, refs[:-1], refs[-1])


def merge_kernel(mine, received, out):
    out[...] = mine[...] + received[...]


def final_kernel(count, spans, rows, last, received, before, out, total, sems):
    del before
    place = place_of(count, rows, -(count // 2))

    @pl.when(place < rows * count // 2)
    def _():
        total[...] = last[...] + received[...]
        copies = []
        for span in range(spans):
            copies.append(
                pltpu.make_async_copy(
                    total.at[pl.ds(span * rows, rows), :],
                    out.at[span, pl.ds(pl.multiple_of(place, rows), rows), :],
                    sems.at[span],
                )
            )
            copies[-1].start()
        for copy in copies:
            copy.wait()


def solution(mesh):
    count = mesh.shape["ab"]
    grid = grid_of(count)
    far = count // 2
    ahead = [(at_ring(at, *grid), at_ring((at + 1) % count, *grid)) for at in range(count)]
    back = [(to, start) for start, to in ahead]
    swap = [(0, 1), (1, 0)]

    def shards(amplitudes, integrals, ab_irrep, cd_irrep, block_pattern):
        spans, rows, depth = amplitudes.shape
        slab = integrals.shape[0]
        ab_tiles, cd_tiles = block_pattern.shape
        tiles = ab_tiles * cd_tiles
        half = rows * far

        in_hbm = functools.partial(pltpu.with_memory_space_constraint, memory_space=pltpu.HBM)
        smem = pl.BlockSpec(memory_space=pltpu.SMEM)
        vmem = pl.BlockSpec(memory_space=pltpu.VMEM)
        hbm = pl.BlockSpec(memory_space=pltpu.HBM)
        params = pltpu.CompilerParams(vmem_limit_bytes=VMEM_LIMIT)
        piece = pltpu.VMEM((1, rows, depth), jnp.float32)

        *own, listed = pl.pallas_call(
            functools.partial(cut_kernel, ab_tiles, cd_tiles, spans),
            out_shape=(piece,) * spans + (pltpu.VMEM((2, LANES), jnp.int32),),
            in_specs=[hbm] * 4,
            out_specs=(vmem,) * (spans + 1),
            scratch_shapes=[
                pltpu.SMEM(ab_irrep.shape, jnp.int32),
                pltpu.SMEM(cd_irrep.shape, jnp.int32),
                pltpu.VMEM(block_pattern.shape, jnp.int32),
                pltpu.SemaphoreType.DMA((spans + 3,)),
            ],
            compiler_params=params,
            name="cut",
        )(*map(in_hbm, (amplitudes, ab_irrep, cd_irrep, block_pattern)))
        split = pl.pallas_call(
            functools.partial(part_kernel, cd_tiles),
            out_shape=pltpu.VMEM((tiles, TILE, 2 * TILE), jnp.bfloat16),
            in_specs=[smem, hbm],
            out_specs=vmem,
            scratch_shapes=[pltpu.VMEM((FLIGHT, TILE, TILE), jnp.float32), pltpu.SemaphoreType.DMA((FLIGHT,))],
            compiler_params=params,
            cost_estimate=pl.CostEstimate(flops=0, bytes_accessed=8 << 20, transcendentals=0),
            name="part",
        )(listed, in_hbm(integrals))

        block = pltpu.VMEM((spans, half, slab), jnp.float32)

        def step(group, parts):
            pieces = [held[key] for key in group]
            return pl.pallas_call(
                functools.partial(step_kernel, count, rows, cd_tiles, group),
                out_shape=(block, block),
                in_specs=[smem] + [vmem] * (1 + len(pieces) + len(parts)),
                out_specs=(vmem, vmem),
                scratch_shapes=[pltpu.VMEM((len(pieces) * rows, slab), jnp.float32)],
                compiler_params=params,
                input_output_aliases={2 + len(pieces): 0, 3 + len(pieces): 1} if parts else {},
                cost_estimate=pl.CostEstimate(flops=STEP_FLOPS, bytes_accessed=4 << 20, transcendentals=0),
                name="step",
            )(listed, split, *pieces, *parts)

        held = {(span, 0): own[span] for span in range(spans)}
        flows = [(span, sign) for long in (True, False) for span in range(spans) for sign in (-1, 1) if ((sign < 0) == (span % 2 == 0)) == long]
        moving = {(span, sign): own[span] for span, sign in flows}
        arrivals, parts = [(span, 0) for span in range(spans)], ()
        for hop in range(1, far + 1):
            for span, sign in flows:
                long = (sign < 0) == (span % 2 == 0)
                if hop < far or long:
                    moved = moving[span, sign]
                    if hop == 2:
                        moved, _ = lax.optimization_barrier((moved, split))
                    if hop == 3 and long:
                        moved, _ = lax.optimization_barrier((moved, parts[0]))
                    moved = moving[span, sign] = lax.ppermute(moved, "ab", ahead if sign < 0 else back)
                    offset = -far if hop == far else sign * hop
                    held[span, offset] = moved
                    if hop < far:
                        arrivals.append((span, offset))
            if hop == 1:
                parts = step(arrivals, parts)
                arrivals = []
        late = len(arrivals) - spans
        for start in range(0, late, GROUP):
            parts = step(arrivals[start : min(start + GROUP, late)], parts)
        parts = step(arrivals[late:], parts)
        mine, send = parts
        base = pl.pallas_call(
            merge_kernel,
            out_shape=pltpu.HBM((spans, half, slab), jnp.float32),
            in_specs=[vmem, vmem],
            out_specs=vmem,
            compiler_params=params,
            name="merge",
        )(mine, lax.ppermute(send, "cd", swap))

        last = pl.pallas_call(
            functools.partial(last_kernel, cd_tiles),
            out_shape=pltpu.VMEM((spans * rows, slab), jnp.float32),
            in_specs=[smem, vmem] + [vmem] * spans,
            out_specs=vmem,
            compiler_params=params,
            cost_estimate=pl.CostEstimate(flops=1 << 34, bytes_accessed=4 << 20, transcendentals=0),
            name="last",
        )(listed, split, *[held[span, -far] for span in range(spans)])
        return pl.pallas_call(
            functools.partial(final_kernel, count, spans, rows),
            out_shape=pltpu.HBM((spans, half, slab), jnp.float32),
            in_specs=[vmem, vmem, hbm],
            out_specs=hbm,
            scratch_shapes=[pltpu.VMEM((spans * rows, slab), jnp.float32), pltpu.SemaphoreType.DMA((spans,))],
            compiler_params=params,
            input_output_aliases={2: 0},
            name="final",
        )(last, lax.ppermute(last, "cd", swap), base)

    in_specs = (
        P("groups", "ab", "cd"),
        P(("groups", "ab"), "cd"),
        P(("groups", "ab")),
        P(("groups", "cd")),
        P(("groups", "ab"), "cd"),
    )
    out_specs = P("groups", "cd", "ab")
    return jax.shard_map(shards, mesh=mesh, in_specs=in_specs, out_specs=out_specs, check_vma=False)
```

```python
import functools

import jax
import jax.numpy as jnp
from jax import lax
from jax.experimental import pallas as pl
from jax.experimental.pallas import tpu as pltpu
from jax.sharding import PartitionSpec as P

TILE = 128
UNROLL = 4
LANES = 128
AHEAD = 8
FLIGHT = AHEAD * UNROLL
GROUP = 12
STEP_FLOPS = 1 << 30
VMEM_LIMIT = 12 * 2**20


def grid_of(count):
    bits = count.bit_length() - 1
    if count != 1 << bits or bits < 2:
        return count, 1
    rows = 1 << ((bits + 1) // 2)
    return rows, count // rows


def at_ring(place, rows, columns):
    if columns == 1:
        return place
    wide = columns - 1
    beyond = place - rows
    line = beyond // wide
    step = beyond - line * wide
    even = (line % 2) == 0
    if isinstance(place, int):
        back = (rows - 1 - line) * columns + (1 + step if even else columns - 1 - step)
        return place * columns if place < rows else back
    back = (rows - 1 - line) * columns + jnp.where(even, 1 + step, columns - 1 - step)
    return jnp.where(place < rows, place * columns, back)


def ring_of(index, rows, columns):
    if columns == 1:
        return index
    wide = columns - 1
    row = index // columns
    column = index - row * columns
    line = rows - 1 - row
    step = jnp.where((line % 2) == 0, column - 1, columns - 1 - column)
    return jnp.where(column == 0, row, rows + line * wide + step)


def place_of(count, rows, offset):
    grid = grid_of(count)
    here = ring_of(lax.axis_index("ab"), *grid)
    whole = rows * count
    start = at_ring((here + offset + count) % count, *grid) * rows + lax.axis_index("cd") * (whole // 2)
    return jnp.where(start >= whole, start - whole, start)


def cut_kernel(ab_tiles, cd_tiles, spans, amplitudes, labels_ab, labels_cd, labels_pattern, *refs):
    outs, (listed, ab_irrep, cd_irrep, pattern, sems) = refs[:spans], refs[spans:]
    pairs = [(labels_ab, ab_irrep), (labels_cd, cd_irrep), (labels_pattern, pattern)]
    pairs += [(amplitudes.at[pl.ds(at, 1)], out) for at, out in enumerate(outs)]
    copies = [pltpu.make_async_copy(start, end, sems.at[at]) for at, (start, end) in enumerate(pairs)]
    for copy in reversed(copies):
        copy.start()
    for copy in copies[:3]:
        copy.wait()

    shape = (ab_tiles, LANES)
    lane = lax.broadcasted_iota(jnp.int32, shape, 1)
    line = lax.broadcasted_iota(jnp.int32, shape, 0)
    rows = jnp.full(shape, -1, jnp.int32)
    columns = jnp.full(shape, -2, jnp.int32)
    for p in range(ab_tiles):
        rows = jnp.where(line == p, ab_irrep[p], rows)
    for q in range(cd_tiles):
        columns = jnp.where(lane == q, cd_irrep[q], columns)
    stored = jnp.concatenate([pattern[...], jnp.zeros((ab_tiles, LANES - cd_tiles), jnp.int32)], axis=1)
    keep = jnp.where(jnp.logical_and(stored == 1, rows == columns), 1.0, 0.0)

    upto = keep
    reach = 1
    while reach < cd_tiles:
        upto += jnp.where(lane >= reach, pltpu.roll(upto, reach, 1), 0.0)
        reach *= 2
    whole = jnp.broadcast_to(jnp.sum(keep, axis=1, keepdims=True), shape)
    before = whole
    reach = 1
    while reach < ab_tiles:
        before += jnp.where(line >= reach, pltpu.roll(before, reach, 0), 0.0)
        reach *= 2
    found = before[ab_tiles - 1 :, :]
    upto += before - whole

    turned = upto.T
    order = lax.broadcasted_iota(jnp.int32, (cd_tiles, LANES), 1).astype(jnp.float32)
    passed = jnp.zeros((cd_tiles, LANES), jnp.float32)
    for p in range(ab_tiles):
        passed += jnp.where(turned[:cd_tiles, p : p + 1] <= order, 1.0, 0.0)
    places = jnp.sum(passed, axis=0, keepdims=True)
    listed[0:1, :] = jnp.where(order[0:1, :] < found, places, 0.0).astype(jnp.int32)
    listed[1:2, :] = ((found + (UNROLL - 1)) * (1.0 / UNROLL)).astype(jnp.int32)
    for copy in copies[3:]:
        copy.wait()


def part_kernel(cd_tiles, listed, integrals, split, landed, sems):
    def fetch(k):
        start, column = place_in(listed[0, k], cd_tiles)
        slot = lax.bitwise_and(k, FLIGHT - 1)
        return pltpu.make_async_copy(
            integrals.at[pl.ds(start, TILE), pl.ds(column, TILE)], landed.at[slot], sems.at[slot]
        )

    def begin(round_at, carry):
        for unrolled in range(UNROLL):
            fetch(round_at * UNROLL + unrolled).start()
        return carry

    rounds = listed[1, 0]
    lax.fori_loop(0, jnp.minimum(rounds, AHEAD), begin, 0)

    def part(round_at, carry):
        first = round_at * UNROLL
        for unrolled in range(UNROLL):
            fetch(first + unrolled).wait()
        for unrolled in range(UNROLL):
            k = first + unrolled
            real = jnp.logical_or(k == 0, listed[0, k] > 0)
            tile = jnp.where(real, landed[lax.bitwise_and(k, FLIGHT - 1)], 0.0).T
            upper = tile.astype(jnp.bfloat16)
            split[k, :, :TILE] = upper
            split[k, :, TILE:] = (tile - upper.astype(jnp.float32)).astype(jnp.bfloat16)

        @pl.when(round_at + AHEAD < rounds)
        def _():
            begin(round_at + AHEAD, 0)

        return carry

    lax.fori_loop(0, rounds, part, 0)


def place_in(place, cd_tiles):
    bits = cd_tiles.bit_length() - 1
    if cd_tiles == 1 << bits:
        row, column = lax.shift_right_logical(place, bits), lax.bitwise_and(place, cd_tiles - 1)
    else:
        row, column = lax.div(place, cd_tiles), lax.rem(place, cd_tiles)
    return pl.multiple_of(row * TILE, TILE), pl.multiple_of(column * TILE, TILE)


def products(cd_tiles, listed, split, pieces, total):
    total[...] = jnp.zeros_like(total)

    def some(first, many):
        sums = []
        for unrolled in range(many):
            start, column = place_in(listed[0, first + unrolled], cd_tiles)
            left = jnp.concatenate([piece[0, :, pl.ds(column, TILE)] for piece in pieces], axis=0)
            upper = left.astype(jnp.bfloat16)
            lower = (left - upper.astype(jnp.float32)).astype(jnp.bfloat16)
            tile = split[first + unrolled]
            both = jnp.dot(jnp.concatenate([upper, lower], axis=0), tile, preferred_element_type=jnp.float32)
            high, low = both[: left.shape[0]], both[left.shape[0] :]
            sums.append((start, high[:, :TILE] + (high[:, TILE:] + (low[:, :TILE] + low[:, TILE:]))))
        for start, term in sums:
            total[:, pl.ds(start, TILE)] += term

    def step(at, carry):
        some(at * 2 * UNROLL, 2 * UNROLL)
        return carry

    rounds = listed[1, 0]
    lax.fori_loop(0, lax.shift_right_logical(rounds, 1), step, 0)

    @pl.when(lax.bitwise_and(rounds, 1) == 1)
    def _():
        some((rounds - 1) * UNROLL, UNROLL)


def step_kernel(count, rows, cd_tiles, group, listed, split, *refs):
    pieces = refs[: len(group)]
    mine, send, total = refs[-3:]
    products(cd_tiles, listed, split, pieces, total)
    half = rows * count // 2
    for at, (span, offset) in enumerate(group):
        place = place_of(count, rows, offset)
        block = total[at * rows : (at + 1) * rows, :]

        @pl.when(place < half)
        def _():
            mine[span, pl.ds(pl.multiple_of(place, rows), rows), :] = block

        @pl.when(place >= half)
        def _():
            send[span, pl.ds(pl.multiple_of(place - half, rows), rows), :] = block


def last_kernel(cd_tiles, listed, split, *refs):
    products(cd_tiles, listed, split, refs[:-1], refs[-1])


def merge_kernel(mine, received, out):
    out[...] = mine[...] + received[...]


def final_kernel(count, spans, rows, last, received, before, out, total, sems):
    del before
    place = place_of(count, rows, -(count // 2))

    @pl.when(place < rows * count // 2)
    def _():
        total[...] = last[...] + received[...]
        copies = []
        for span in range(spans):
            copies.append(
                pltpu.make_async_copy(
                    total.at[pl.ds(span * rows, rows), :],
                    out.at[span, pl.ds(pl.multiple_of(place, rows), rows), :],
                    sems.at[span],
                )
            )
            copies[-1].start()
        for copy in copies:
            copy.wait()


def solution(mesh):
    count = mesh.shape["ab"]
    grid = grid_of(count)
    far = count // 2
    ahead = [(at_ring(at, *grid), at_ring((at + 1) % count, *grid)) for at in range(count)]
    back = [(to, start) for start, to in ahead]
    swap = [(0, 1), (1, 0)]

    def shards(amplitudes, integrals, ab_irrep, cd_irrep, block_pattern):
        spans, rows, depth = amplitudes.shape
        slab = integrals.shape[0]
        ab_tiles, cd_tiles = block_pattern.shape
        tiles = ab_tiles * cd_tiles
        half = rows * far

        in_hbm = functools.partial(pltpu.with_memory_space_constraint, memory_space=pltpu.HBM)
        smem = pl.BlockSpec(memory_space=pltpu.SMEM)
        vmem = pl.BlockSpec(memory_space=pltpu.VMEM)
        hbm = pl.BlockSpec(memory_space=pltpu.HBM)
        params = pltpu.CompilerParams(vmem_limit_bytes=VMEM_LIMIT)
        piece = pltpu.VMEM((1, rows, depth), jnp.float32)

        *own, listed = pl.pallas_call(
            functools.partial(cut_kernel, ab_tiles, cd_tiles, spans),
            out_shape=(piece,) * spans + (pltpu.VMEM((2, LANES), jnp.int32),),
            in_specs=[hbm] * 4,
            out_specs=(vmem,) * (spans + 1),
            scratch_shapes=[
                pltpu.SMEM(ab_irrep.shape, jnp.int32),
                pltpu.SMEM(cd_irrep.shape, jnp.int32),
                pltpu.VMEM(block_pattern.shape, jnp.int32),
                pltpu.SemaphoreType.DMA((spans + 3,)),
            ],
            compiler_params=params,
            name="cut",
        )(*map(in_hbm, (amplitudes, ab_irrep, cd_irrep, block_pattern)))
        split = pl.pallas_call(
            functools.partial(part_kernel, cd_tiles),
            out_shape=pltpu.VMEM((tiles, TILE, 2 * TILE), jnp.bfloat16),
            in_specs=[smem, hbm],
            out_specs=vmem,
            scratch_shapes=[pltpu.VMEM((FLIGHT, TILE, TILE), jnp.float32), pltpu.SemaphoreType.DMA((FLIGHT,))],
            compiler_params=params,
            cost_estimate=pl.CostEstimate(flops=0, bytes_accessed=8 << 20, transcendentals=0),
            name="part",
        )(listed, in_hbm(integrals))

        block = pltpu.VMEM((spans, half, slab), jnp.float32)

        def step(group, parts):
            pieces = [held[key] for key in group]
            return pl.pallas_call(
                functools.partial(step_kernel, count, rows, cd_tiles, group),
                out_shape=(block, block),
                in_specs=[smem] + [vmem] * (1 + len(pieces) + len(parts)),
                out_specs=(vmem, vmem),
                scratch_shapes=[pltpu.VMEM((len(pieces) * rows, slab), jnp.float32)],
                compiler_params=params,
                input_output_aliases={2 + len(pieces): 0, 3 + len(pieces): 1} if parts else {},
                cost_estimate=pl.CostEstimate(flops=STEP_FLOPS, bytes_accessed=4 << 20, transcendentals=0),
                name="step",
            )(listed, split, *pieces, *parts)

        held = {(span, 0): own[span] for span in range(spans)}
        flows = [(span, sign) for long in (True, False) for span in range(spans) for sign in (-1, 1) if ((sign < 0) == (span % 2 == 0)) == long]
        moving = {(span, sign): own[span] for span, sign in flows}
        arrivals, parts = [(span, 0) for span in range(spans)], ()
        for hop in range(1, far + 1):
            for span, sign in flows:
                long = (sign < 0) == (span % 2 == 0)
                if hop < far or long:
                    moved = moving[span, sign]
                    if hop == 2:
                        moved, _ = lax.optimization_barrier((moved, split))
                    if hop == 3 and long:
                        moved, _ = lax.optimization_barrier((moved, parts[0]))
                    moved = moving[span, sign] = lax.ppermute(moved, "ab", ahead if sign < 0 else back)
                    offset = -far if hop == far else sign * hop
                    held[span, offset] = moved
                    if hop < far:
                        arrivals.append((span, offset))
            if hop == 1:
                parts = step(arrivals, parts)
                arrivals = []
        late = len(arrivals) - spans
        for start in range(0, late, GROUP):
            parts = step(arrivals[start : min(start + GROUP, late)], parts)
        parts = step(arrivals[late:], parts)
        mine, send = parts
        base = pl.pallas_call(
            merge_kernel,
            out_shape=pltpu.HBM((spans, half, slab), jnp.float32),
            in_specs=[vmem, vmem],
            out_specs=vmem,
            compiler_params=params,
            name="merge",
        )(mine, lax.ppermute(send, "cd", swap))

        last = pl.pallas_call(
            functools.partial(last_kernel, cd_tiles),
            out_shape=pltpu.VMEM((spans * rows, slab), jnp.float32),
            in_specs=[smem, vmem] + [vmem] * spans,
            out_specs=vmem,
            compiler_params=params,
            cost_estimate=pl.CostEstimate(flops=1 << 34, bytes_accessed=4 << 20, transcendentals=0),
            name="last",
        )(listed, split, *[held[span, -far] for span in range(spans)])
        return pl.pallas_call(
            functools.partial(final_kernel, count, spans, rows),
            out_shape=pltpu.HBM((spans, half, slab), jnp.float32),
            in_specs=[vmem, vmem, hbm],
            out_specs=hbm,
            scratch_shapes=[pltpu.VMEM((spans * rows, slab), jnp.float32), pltpu.SemaphoreType.DMA((spans,))],
            compiler_params=params,
            input_output_aliases={2: 0},
            name="final",
        )(last, lax.ppermute(last, "cd", swap), base)

    in_specs = (
        P("groups", "ab", "cd"),
        P(("groups", "ab"), "cd"),
        P(("groups", "ab")),
        P(("groups", "cd")),
        P(("groups", "ab"), "cd"),
    )
    out_specs = P("groups", "cd", "ab")
    return jax.shard_map(shards, mesh=mesh, in_specs=in_specs, out_specs=out_specs, check_vma=False)
```
